256 devices in a mesh: wide: 16 (over y, z_hi, core), narrow: 16 (over z_lo, x).
Axes of the slice: x: 4, y: 4, z: 8 (z_hi: 2, z_lo: 4; z = z_hi * 4 + z_lo), core: 2. Of those that a mesh axis runs over, the one named last changes fastest.
Arguments:
- embeds: bfloat16 [32768, 512], P(('wide', 'narrow')), may hold values from -6 to 6
- weight: bfloat16 [512, 256], replicated, may hold values from -0.016479492 to 0.016479492
- solve: float32 [32768], P(('wide', 'narrow')), may hold values from -6 to 6
- probes: float32 [32768, 15], P(('wide', 'narrow')), may hold values from -6 to 6
- probe_solves: float32 [32768, 15], P(('wide', 'narrow')), may hold values from -6 to 6
Outputs:
- grad_rows: float32 [32768, 256], P(('wide', 'narrow'))
- grad_weight: float32 [512, 256], replicated
The draws below stay inside these ranges and needn't reach their ends.
All inputs are finite; a program needn't handle non-finite values.
Results may differ from the reference program's by a relative error of at most 0.0042.
Values may be sent and summed in bfloat16 or wider, within the bound.
No kernel may reach another device: no remote copies, remote signals or barrier semaphores. Data moves between devices by JAX's collectives and lax.ppermute only.
A program may use at most 64 MiB of HBM per device.

```python
import math
import jax
import jax.numpy as jnp
from jax import lax

E = 512
D = 256
PROBES = 15
TOKENS = 32768


def steps_of(stream_key, dims, cuts, smallest, high):
    level, own = 1.0, jax.random.fold_in(stream_key, 6)
    for position, blocks in cuts:
        draws = jnp.exp(jax.random.uniform(jax.random.fold_in(own, position), (blocks,), jnp.float32, smallest / len(cuts), high / len(cuts)))
        level = level * jnp.repeat(draws, dims[position] // blocks).reshape([-1 if axis == position else 1 for axis in range(len(dims))])
    return level


def bell_draw(stream_key, dims, spread, bound, cuts=(), dtype=jnp.bfloat16):
    drawn = jax.random.normal(stream_key, dims, jnp.float32) * spread
    if len(cuts) > 0:
        drawn = steps_of(stream_key, dims, cuts, -0.22, 0.18) * drawn
    return jnp.clip(drawn, min=-bound, max=bound).astype(dtype)


def setup_inputs(seed: int = 0) -> dict:
    key_list = jax.random.split(jax.random.key(seed), 6)
    embeds = bell_draw(key_list[0], (TOKENS, E), 1.0, 6.0, ((0, 256),))
    weight = bell_draw(key_list[1], (E, D), (1.0 / (E * D) ** 0.5), 0.016479492)
    solve = bell_draw(key_list[2], (TOKENS,), 1.0, 6.0, ((0, 256),), jnp.float32)
    probes = bell_draw(key_list[3], (TOKENS, PROBES), 1.0, 6.0, ((0, 256),), jnp.float32)
    probe_solves = bell_draw(key_list[4], (TOKENS, PROBES), 1.0, 6.0, ((0, 256),), jnp.float32)
    return dict(embeds=embeds, weight=weight, solve=solve, probes=probes, probe_solves=probe_solves)


def side_rows(solve, probes, probe_solves):
    scale = (2.0 * probes.shape[1]) ** (-0.5)
    zero = jnp.zeros((solve.shape[0], 1), jnp.float32)
    left = jnp.concatenate([solve[:, None], probe_solves * scale, probes * scale, zero], axis=1)
    right = jnp.concatenate([solve[:, None], -probes * scale, -probe_solves * scale, zero], axis=1)
    return (left, right)

def tile_terms(u_rows, left_rows, u_cols, right_cols):
    gram = jnp.dot(u_rows, u_cols.T, preferred_element_type=jnp.float32)
    row_sq = lax.optimization_barrier(jnp.sum(jnp.square(u_rows.astype(jnp.float32)), axis=1))
    col_sq = lax.optimization_barrier(jnp.sum(jnp.square(u_cols.astype(jnp.float32)), axis=1))
    dist = jnp.sqrt(jnp.maximum(row_sq[:, None] + col_sq[None, :] - 2.0 * gram, 0.0))
    root_five = math.sqrt(5.0)
    shape_term = 5.0 / 3.0 * (1.0 + root_five * dist) * jnp.exp(-root_five * dist)
    pair_weight = jnp.dot(left_rows, right_cols.T, precision=lax.Precision.HIGHEST, preferred_element_type=jnp.float32)
    coupling = pair_weight * shape_term
    mixed = jnp.dot(coupling.astype(jnp.bfloat16), u_cols, preferred_element_type=jnp.float32)
    return (mixed, lax.optimization_barrier(jnp.sum(coupling, axis=1)))

def reference(embeds, weight, solve, probes, probe_solves):
    feats = jnp.dot(embeds, weight, preferred_element_type=jnp.float32).astype(jnp.bfloat16)
    left, right = side_rows(solve, probes, probe_solves)
    total = feats.shape[0]
    block = math.gcd(total, 512)
    count = total // block

    def one_block(pieces):
        u_rows, left_rows = pieces
        mixed, row_total = tile_terms(u_rows, left_rows, feats, right)
        return mixed - row_total[:, None] * u_rows.astype(jnp.float32)
    grad_rows = lax.map(one_block, (feats.reshape(count, block, -1), left.reshape(count, block, -1)))
    grad_rows = grad_rows.reshape(total, -1)
    grad_weight = jnp.dot(embeds.astype(jnp.float32).T, grad_rows, precision=lax.Precision.HIGHEST, preferred_element_type=jnp.float32)
    return (grad_rows, grad_weight / math.sqrt(total))
```

```python
import functools
import math

import jax
import jax.numpy as jnp
import numpy as np
from jax import lax
from jax.experimental import pallas as pl
from jax.experimental.pallas import tpu as pltpu
from jax.sharding import Mesh, PartitionSpec as P

LOG2E = math.log2(math.e)
ROOT5 = math.sqrt(5.0)
ALL = ("y", "zh", "core", "zl", "x")
PLANE = ("y", "core", "x")
DEPTH = ("zh", "zl")
F32 = jnp.float32
BF16 = jnp.bfloat16
VMEM = pl.BlockSpec(memory_space=pltpu.VMEM)


def params(mib):
    return pltpu.CompilerParams(vmem_limit_bytes=mib << 20)


def dot_nt(a, b):
    return lax.dot_general(a, b, (((1,), (1,)), ((), ())), preferred_element_type=F32)


def dot_tn(a, b):
    return lax.dot_general(a, b, (((0,), (0,)), ((), ())), preferred_element_type=F32)


def pack_kernel(embeds, weight, solve, probes, probe_solves, out):
    rows, width = embeds.shape[0], weight.shape[1]
    count = probes.shape[1]
    feats = jnp.dot(embeds[...], weight[...], preferred_element_type=F32).astype(BF16)
    out[:, :width] = feats
    wide = feats.astype(F32)
    sq = jnp.sum(wide * wide, axis=1, keepdims=True)
    sq_hi = sq.astype(BF16).astype(F32)
    sq_mid = (sq - sq_hi).astype(BF16).astype(F32)
    sq_lo = sq - sq_hi - sq_mid
    fold = math.sqrt(5.0 / 3.0 * ROOT5)
    scale = (2.0 * count) ** (-0.5) * fold
    factors = jnp.concatenate(
        [
            solve[...] * fold,
            probes[...] * -scale,
            probe_solves[...] * -scale,
            jnp.zeros((rows, 1), F32),
        ],
        axis=1,
    )
    hi = factors.astype(BF16).astype(F32)
    lo = factors - hi
    lane = lax.broadcasted_iota(jnp.int32, (rows, 32), 1)
    tail = jnp.where(lane == 0, sq_hi, jnp.where(lane == 1, sq_mid, jnp.where(lane == 2, sq_lo, 0.0)))
    out[:, width:] = jnp.concatenate([hi, lo, hi, tail], axis=1).astype(BF16)


def left_map(count):
    source = np.zeros((32,), np.int32)
    sign = np.zeros((32,), np.float32)
    sign[0] = 1.0
    for k in range(count):
        source[1 + k], sign[1 + k] = 1 + count + k, -1.0
        source[1 + count + k], sign[1 + count + k] = 1 + k, -1.0
    table = np.zeros((128, 128), np.float32)
    for group, offset in ((0, 0), (1, 0), (2, 32)):
        for k in range(32):
            table[offset + source[k], 32 * group + k] = sign[k]
    return jnp.asarray(table, BF16)


def tile_kernel(sub, step, table, rows_ref, *refs):
    *columns, out = refs
    width = out.shape[1]
    rows = rows_ref.shape[0]
    u_rows = rows_ref[:, :width]
    fac = rows_ref[:, width:]
    twice = (u_rows.astype(F32) * -2.0).astype(BF16)
    left = jnp.dot(fac, table[...], preferred_element_type=F32).astype(BF16)
    lane = lax.broadcasted_iota(jnp.int32, (128, 128), 0)
    pick = jnp.where((lane >= 96) & (lane < 99), 1.0, 0.0).astype(BF16)
    sq_rows = jnp.dot(fac, pick, preferred_element_type=F32)[:, :1]
    lane = lax.broadcasted_iota(jnp.int32, (8, 128), 1)
    pick_cols = jnp.where((lane >= 96) & (lane < 99), 1.0, 0.0).astype(BF16)
    blocks = [slice(k, k + sub) for k in range(0, rows, sub)]
    acc = [jnp.zeros((sub, width), F32) for _ in blocks]
    total = [jnp.zeros((sub, 128), F32) for _ in blocks]
    work = [
        (ref, start, k)
        for ref in columns
        for start in range(0, ref.shape[0], step)
        for k in range(len(blocks))
    ]

    def products(ref, start, k):
        u_cols = ref[start : start + step, :width]
        right = ref[start : start + step, width:]
        sq_cols = dot_nt(pick_cols, right)[:1]
        return u_cols, sq_cols, dot_nt(twice[blocks[k]], u_cols), dot_nt(left[blocks[k]], right)

    ahead = products(*work[0])
    for index, (_, _, k) in enumerate(work):
        u_cols, sq_cols, cross, pair = ahead
        if index + 1 < len(work):
            ahead = products(*work[index + 1])
        d2 = jnp.maximum((sq_rows[blocks[k]] + sq_cols) + cross, 1e-30)
        dist = d2 * lax.rsqrt(d2)
        coupling = pair * ((dist + 1.0 / ROOT5) * jnp.exp2(dist * (-ROOT5 * LOG2E)))
        for j in range(0, step, 128):
            total[k] = total[k] + coupling[:, j : j + 128]
        acc[k] = acc[k] + jnp.dot(coupling.astype(BF16), u_cols, preferred_element_type=F32)
    for k, block in enumerate(blocks):
        row_total = jnp.sum(total[k], axis=1, keepdims=True)
        out[block, :] = (acc[k] - row_total * u_rows[block].astype(F32)).astype(out.dtype)


def sum_rows_kernel(place, a, b, c, d, embeds, partial, own, *others):
    rows = own.shape[0]
    count = 1 + len(others)
    total = (a[...] + b[...].astype(F32)) + (c[...].astype(F32) + d[...].astype(F32))
    hi = total.astype(BF16)
    lo = (total - hi.astype(F32)).astype(BF16)
    own[...] = total[:rows]
    for k, ref in enumerate(others):
        ref[...] = hi[(k + 1) * rows : (k + 2) * rows]
    weight = jnp.zeros(partial.shape, F32)
    for k in range(count):
        start = pl.multiple_of(lax.rem(place[0] + k, count) * rows, rows)
        line = embeds[pl.ds(start, rows), :]
        block = slice(k * rows, (k + 1) * rows)
        weight = weight + (dot_tn(line, hi[block]) + dot_tn(line, lo[block]))
    partial[...] = weight.astype(BF16)


def finish_rows_kernel(own, b, c, d, grad_rows):
    grad_rows[...] = (own[...] + b[...].astype(F32)) + (c[...].astype(F32) + d[...].astype(F32))


def sum_spread_kernel(parts, out):
    total = parts[0].astype(F32)
    for k in range(1, parts.shape[0]):
        total = total + parts[k].astype(F32)
    low = total.astype(out.dtype)
    for k in range(out.shape[0]):
        out[k] = low


def sum_spread(parts, copies, dtype):
    return pl.pallas_call(
        sum_spread_kernel,
        out_shape=jax.ShapeDtypeStruct((copies,) + parts.shape[1:], dtype),
        in_specs=[VMEM],
        out_specs=VMEM,
        compiler_params=params(16),
        name="sum_spread",
    )(parts)


def ring(array, axis, size, shift):
    return lax.ppermute(array, axis, [(i, (i + shift) % size) for i in range(size)])


def exchange(array, axes):
    return lax.all_to_all(array, axes, split_axis=0, concat_axis=0, tiled=True)


def shards(sizes, embeds, weight, solve, probes, probe_solves):
    rows, width = embeds.shape[0], weight.shape[1]
    n_x, n_y, n_z = sizes["x"], sizes["y"], sizes["zh"] * sizes["zl"]
    pack = pl.pallas_call(
        pack_kernel,
        out_shape=jax.ShapeDtypeStruct((rows, width + 128), BF16),
        in_specs=[VMEM] * 5,
        out_specs=VMEM,
        compiler_params=params(16),
        name="pack",
    )(embeds, weight, solve[:, None], probes, probe_solves)

    embeds_line = lax.all_gather(embeds, "y", axis=0, tiled=True)

    line = jnp.concatenate([pack] + [ring(pack, "y", n_y, -d) for d in range(1, n_y)], axis=0)
    pair = jnp.concatenate([pack, ring(pack, DEPTH, n_z, n_z // 2)], axis=0)
    pair, _ = lax.optimization_barrier((pair, line))
    columns = [pair] + [ring(pair, DEPTH, n_z, d) for d in (1, -1, 2)]
    columns += [ring(part, "core", 2, 1) for part in columns]
    lines = [line] + [ring(line, "x", n_x, -d) for d in range(1, n_x)]


    table = left_map(probes.shape[1])
    back = {}
    for d in (0, 3, 1, 2):
        if d == 3:
            lines[d], _, embeds_line = lax.optimization_barrier((lines[d], back[0], embeds_line))
        elif d != 0:
            lines[d], _ = lax.optimization_barrier((lines[d], back[0]))
        part = pl.pallas_call(
            functools.partial(tile_kernel, 256, 256),
            out_shape=jax.ShapeDtypeStruct((n_y * rows, width), F32 if d == 0 else BF16),
            in_specs=[VMEM] * (2 + len(columns)),
            out_specs=VMEM,
            compiler_params=params(40),
            name="tile",
        )(table, lines[d], *columns)
        back[d] = part if d == 0 else ring(part, "x", n_x, d)

    sums = pl.pallas_call(
        sum_rows_kernel,
        out_shape=[
            jax.ShapeDtypeStruct((embeds.shape[1], width), BF16),
            jax.ShapeDtypeStruct((rows, width), F32),
        ]
        + [jax.ShapeDtypeStruct((rows, width), BF16)] * (n_y - 1),
        in_specs=[pl.BlockSpec(memory_space=pltpu.SMEM)] + [VMEM] * (n_x + 1),
        out_specs=[VMEM] * (n_y + 1),
        compiler_params=params(16),
        name="sum_rows",
    )(lax.axis_index("y")[None], *(back[d] for d in range(n_x)), embeds_line)
    partial, own_rows, *other_rows = sums
    arrived = [ring(block, "y", n_y, d + 1) for d, block in enumerate(other_rows)]

    n_plane = n_x * n_y * 2
    pieces = exchange(partial.reshape(n_plane, -1, width), PLANE)
    pieces, arrived = lax.optimization_barrier((pieces, arrived))
    pieces = exchange(sum_spread(pieces, n_z, F32), DEPTH)
    pieces = exchange(sum_spread(pieces, n_plane, BF16), PLANE)
    total_points = rows * n_plane * n_z
    grad_weight = pieces.reshape(-1, width).astype(F32) * (1.0 / math.sqrt(total_points))

    grad_rows = pl.pallas_call(
        finish_rows_kernel,
        out_shape=jax.ShapeDtypeStruct((rows, width), F32),
        in_specs=[VMEM] * 4,
        out_specs=VMEM,
        compiler_params=params(16),
        name="finish_rows",
    )(own_rows, *arrived)
    return grad_rows, grad_weight


def solution(mesh):
    sizes = {"y": 4, "zh": 2, "core": 2, "zl": 4, "x": 4}
    fine = Mesh(mesh.devices.reshape(tuple(sizes[a] for a in ALL)), ALL)
    return jax.shard_map(
        functools.partial(shards, sizes),
        mesh=fine,
        in_specs=(P(ALL, None), P(), P(ALL), P(ALL, None), P(ALL, None)),
        out_specs=(P(ALL, None), P()),
        check_vma=False,
    )
```

```python
import functools
import math

import jax
import jax.numpy as jnp
import numpy as np
from jax import lax
from jax.experimental import pallas as pl
from jax.experimental.pallas import tpu as pltpu
from jax.sharding import Mesh, PartitionSpec as P

LOG2E = math.log2(math.e)
ROOT5 = math.sqrt(5.0)
ALL = ("y", "zh", "core", "zl", "x")
PLANE = ("y", "core", "x")
DEPTH = ("zh", "zl")
F32 = jnp.float32
BF16 = jnp.bfloat16
VMEM = pl.BlockSpec(memory_space=pltpu.VMEM)


def params(mib):
    return pltpu.CompilerParams(vmem_limit_bytes=mib << 20)


def dot_nt(a, b):
    return lax.dot_general(a, b, (((1,), (1,)), ((), ())), preferred_element_type=F32)


def dot_tn(a, b):
    return lax.dot_general(a, b, (((0,), (0,)), ((), ())), preferred_element_type=F32)


def pack_kernel(embeds, weight, solve, probes, probe_solves, out, extended):
    rows, width = embeds.shape[0], weight.shape[1]
    count = probes.shape[1]
    feats = jnp.dot(embeds[...], weight[...], preferred_element_type=F32).astype(BF16)
    out[:, :width] = feats
    wide = feats.astype(F32)
    sq = jnp.sum(wide * wide, axis=1, keepdims=True)
    sq_hi = sq.astype(BF16).astype(F32)
    sq_mid = (sq - sq_hi).astype(BF16).astype(F32)
    sq_lo = sq - sq_hi - sq_mid
    fold = math.sqrt(5.0 / 3.0 * ROOT5)
    scale = (2.0 * count) ** (-0.5) * fold
    factors = jnp.concatenate(
        [
            solve[...] * fold,
            probes[...] * -scale,
            probe_solves[...] * -scale,
            jnp.zeros((rows, 1), F32),
        ],
        axis=1,
    )
    hi = factors.astype(BF16).astype(F32)
    lo = factors - hi
    lane = lax.broadcasted_iota(jnp.int32, (rows, 32), 1)
    tail = jnp.where(lane == 0, sq_hi, jnp.where(lane == 1, sq_mid, jnp.where(lane == 2, sq_lo, 0.0)))
    tail = jnp.concatenate([hi, lo, hi, tail], axis=1).astype(BF16)
    out[:, width:] = tail
    extended[:, :width] = feats
    extended[:, width : width + 128] = tail
    extended[:, width + 128 :] = embeds[...]


def left_map(count):
    source = np.zeros((32,), np.int32)
    sign = np.zeros((32,), np.float32)
    sign[0] = 1.0
    for k in range(count):
        source[1 + k], sign[1 + k] = 1 + count + k, -1.0
        source[1 + count + k], sign[1 + count + k] = 1 + k, -1.0
    table = np.zeros((128, 128), np.float32)
    for group, offset in ((0, 0), (1, 0), (2, 32)):
        for k in range(32):
            table[offset + source[k], 32 * group + k] = sign[k]
    return jnp.asarray(table, BF16)


def tile_kernel(sub, step, table, rows_ref, *refs):
    *columns, out = refs
    width = out.shape[1]
    rows = rows_ref.shape[0]
    u_rows = rows_ref[:, :width]
    fac = rows_ref[:, width:]
    twice = (u_rows.astype(F32) * -2.0).astype(BF16)
    left = jnp.dot(fac, table[...], preferred_element_type=F32).astype(BF16)
    lane = lax.broadcasted_iota(jnp.int32, (128, 128), 0)
    pick = jnp.where((lane >= 96) & (lane < 99), 1.0, 0.0).astype(BF16)
    sq_rows = jnp.dot(fac, pick, preferred_element_type=F32)[:, :1]
    lane = lax.broadcasted_iota(jnp.int32, (8, 128), 1)
    pick_cols = jnp.where((lane >= 96) & (lane < 99), 1.0, 0.0).astype(BF16)
    blocks = [slice(k, k + sub) for k in range(0, rows, sub)]
    acc = [jnp.zeros((sub, width), F32) for _ in blocks]
    total = [jnp.zeros((sub, 128), F32) for _ in blocks]
    work = [
        (ref, start, k)
        for ref in columns
        for start in range(0, ref.shape[0], step)
        for k in range(len(blocks))
    ]

    def products(ref, start, k):
        u_cols = ref[start : start + step, :width]
        right = ref[start : start + step, width:]
        sq_cols = dot_nt(pick_cols, right)[:1]
        return u_cols, sq_cols, dot_nt(twice[blocks[k]], u_cols), dot_nt(left[blocks[k]], right)

    ahead = products(*work[0])
    for index, (_, _, k) in enumerate(work):
        u_cols, sq_cols, cross, pair = ahead
        if index + 1 < len(work):
            ahead = products(*work[index + 1])
        d2 = jnp.maximum((sq_rows[blocks[k]] + sq_cols) + cross, 1e-30)
        dist = d2 * lax.rsqrt(d2)
        coupling = pair * ((dist + 1.0 / ROOT5) * jnp.exp2(dist * (-ROOT5 * LOG2E)))
        for j in range(0, step, 128):
            total[k] = total[k] + coupling[:, j : j + 128]
        acc[k] = acc[k] + jnp.dot(coupling.astype(BF16), u_cols, preferred_element_type=F32)
    for k, block in enumerate(blocks):
        row_total = jnp.sum(total[k], axis=1, keepdims=True)
        out[block, :] = (acc[k] - row_total * u_rows[block].astype(F32)).astype(out.dtype)


def sum_rows_kernel(count, *refs):
    parts, lines, (partial, own, *others) = refs[:count], refs[count : 2 * count], refs[2 * count :]
    rows, width = own.shape
    total = parts[0][...]
    for ref in parts[1:]:
        total = total + ref[...].astype(F32)
    hi = total.astype(BF16)
    lo = (total - hi.astype(F32)).astype(BF16)
    own[...] = total[:rows]
    for k, ref in enumerate(others):
        ref[...] = hi[(k + 1) * rows : (k + 2) * rows]
    weight = jnp.zeros(partial.shape, F32)
    for k, ref in enumerate(lines):
        block = slice(k * rows, (k + 1) * rows)
        embeds = ref[:, width + 128 :]
        weight = weight + (dot_tn(embeds, hi[block]) + dot_tn(embeds, lo[block]))
    partial[...] = weight.astype(BF16)


def finish_rows_kernel(own, b, c, d, grad_rows):
    grad_rows[...] = (own[...] + b[...].astype(F32)) + (c[...].astype(F32) + d[...].astype(F32))


def sum_spread_kernel(parts, out):
    total = parts[0].astype(F32)
    for k in range(1, parts.shape[0]):
        total = total + parts[k].astype(F32)
    low = total.astype(out.dtype)
    for k in range(out.shape[0]):
        out[k] = low


def sum_spread(parts, copies, dtype):
    return pl.pallas_call(
        sum_spread_kernel,
        out_shape=jax.ShapeDtypeStruct((copies,) + parts.shape[1:], dtype),
        in_specs=[VMEM],
        out_specs=VMEM,
        compiler_params=params(16),
        name="sum_spread",
    )(parts)


def ring(array, axis, size, shift):
    return lax.ppermute(array, axis, [(i, (i + shift) % size) for i in range(size)])


def turn(array, sizes, stage, shift):
    dims = [sizes[a] for a in ALL]
    perm = []
    for source in range(math.prod(dims)):
        place = list(np.unravel_index(source, dims))
        axis = ALL.index(PLANE[0] if (place[ALL.index("core")] + stage) % 2 == 0 else PLANE[-1])
        place[axis] = (place[axis] + shift) % dims[axis]
        perm.append((source, int(np.ravel_multi_index(place, dims))))
    return lax.ppermute(array, ALL, perm)


def exchange(array, axes):
    return lax.all_to_all(array, axes, split_axis=0, concat_axis=0, tiled=True)


def shards(sizes, embeds, weight, solve, probes, probe_solves):
    rows, width = embeds.shape[0], weight.shape[1]
    n_side, n_z = sizes["x"], sizes["zh"] * sizes["zl"]
    pack, extended = pl.pallas_call(
        pack_kernel,
        out_shape=[
            jax.ShapeDtypeStruct((rows, width + 128), BF16),
            jax.ShapeDtypeStruct((rows, width + 128 + embeds.shape[1]), BF16),
        ],
        in_specs=[VMEM] * 5,
        out_specs=[VMEM] * 2,
        compiler_params=params(16),
        name="pack",
    )(embeds, weight, solve[:, None], probes, probe_solves)

    blocks = [extended] + [turn(extended, sizes, 0, -d) for d in range(1, n_side)]
    line = jnp.concatenate([block[:, : width + 128] for block in blocks], axis=0)
    pair = jnp.concatenate([pack, ring(pack, DEPTH, n_z, n_z // 2)], axis=0)
    pair, _ = lax.optimization_barrier((pair, line))
    columns = [pair] + [ring(pair, DEPTH, n_z, d) for d in (1, -1, 2)]
    lines = [line] + [turn(line, sizes, 1, -d) for d in range(1, n_side)]
    columns, lines = lax.optimization_barrier((columns, lines))
    columns += [ring(part, "core", 2, 1) for part in columns]

    table = left_map(probes.shape[1])
    back = {}
    for d in (0, 3, 1, 2):
        part = pl.pallas_call(
            functools.partial(tile_kernel, 256, 256),
            out_shape=jax.ShapeDtypeStruct((n_side * rows, width), F32 if d == 0 else BF16),
            in_specs=[VMEM] * (2 + len(columns)),
            out_specs=VMEM,
            compiler_params=params(40),
            name="tile",
        )(table, lines[d], *columns)
        back[d] = part if d == 0 else turn(part, sizes, 1, d)

    partial, own_rows, *other_rows = pl.pallas_call(
        functools.partial(sum_rows_kernel, n_side),
        out_shape=[
            jax.ShapeDtypeStruct((embeds.shape[1], width), BF16),
            jax.ShapeDtypeStruct((rows, width), F32),
        ]
        + [jax.ShapeDtypeStruct((rows, width), BF16)] * (n_side - 1),
        in_specs=[VMEM] * (2 * n_side),
        out_specs=[VMEM] * (n_side + 1),
        compiler_params=params(16),
        name="sum_rows",
    )(*(back[d] for d in range(n_side)), *blocks)
    arrived = [turn(block, sizes, 0, d + 1) for d, block in enumerate(other_rows)]
    grad_rows = pl.pallas_call(
        finish_rows_kernel,
        out_shape=jax.ShapeDtypeStruct((rows, width), F32),
        in_specs=[VMEM] * 4,
        out_specs=VMEM,
        compiler_params=params(16),
        name="finish_rows",
    )(own_rows, *arrived)

    n_plane = n_side * n_side * 2
    pieces = exchange(partial.reshape(n_plane, -1, width), PLANE)
    pieces, grad_rows = lax.optimization_barrier((pieces, grad_rows))
    pieces = exchange(sum_spread(pieces, n_z, F32), DEPTH)
    pieces = exchange(sum_spread(pieces, n_plane, BF16), PLANE)
    total_points = rows * n_plane * n_z
    grad_weight = pieces.reshape(-1, width).astype(F32) * (1.0 / math.sqrt(total_points))
    return grad_rows, grad_weight


def solution(mesh):
    sizes = {"y": 4, "zh": 2, "core": 2, "zl": 4, "x": 4}
    fine = Mesh(mesh.devices.reshape(tuple(sizes[a] for a in ALL)), ALL)
    return jax.shard_map(
        functools.partial(shards, sizes),
        mesh=fine,
        in_specs=(P(ALL, None), P(), P(ALL), P(ALL, None), P(ALL, None)),
        out_specs=(P(ALL, None), P()),
        check_vma=False,
    )
```

```python
import functools
import math

import jax
import jax.numpy as jnp
import numpy as np
from jax import lax
from jax.experimental import pallas as pl
from jax.experimental.pallas import tpu as pltpu
from jax.sharding import Mesh, PartitionSpec as P

LOG2E = math.log2(math.e)
ROOT5 = math.sqrt(5.0)
ALL = ("y", "zh", "core", "zl", "x")
PLANE = ("y", "core", "x")
DEPTH = ("zh", "zl")
F32 = jnp.float32
BF16 = jnp.bfloat16
VMEM = pl.BlockSpec(memory_space=pltpu.VMEM)


def params(mib):
    return pltpu.CompilerParams(vmem_limit_bytes=mib << 20)


def dot_nt(a, b):
    return lax.dot_general(a, b, (((1,), (1,)), ((), ())), preferred_element_type=F32)


def dot_tn(a, b):
    return lax.dot_general(a, b, (((0,), (0,)), ((), ())), preferred_element_type=F32)


def pack_kernel(embeds, weight, solve, probes, probe_solves, out, extended):
    rows, width = embeds.shape[0], weight.shape[1]
    count = probes.shape[0]
    feats = jnp.dot(embeds[...], weight[...], preferred_element_type=F32).astype(BF16)
    out[:, :width] = feats
    wide = feats.astype(F32)
    sq = jnp.sum(wide * wide, axis=1, keepdims=True)
    sq_hi = sq.astype(BF16).astype(F32)
    sq_mid = (sq - sq_hi).astype(BF16).astype(F32)
    sq_lo = sq - sq_hi - sq_mid
    fold = math.sqrt(5.0 / 3.0 * ROOT5)
    scale = (2.0 * count) ** (-0.5) * fold
    factors = jnp.concatenate(
        [solve[...] * fold, probes[...] * -scale, probe_solves[...] * -scale, jnp.zeros((1, rows), F32)],
        axis=0,
    ).T
    hi = factors.astype(BF16).astype(F32)
    lo = factors - hi
    lane = lax.broadcasted_iota(jnp.int32, (rows, 32), 1)
    tail = jnp.where(lane == 0, sq_hi, jnp.where(lane == 1, sq_mid, jnp.where(lane == 2, sq_lo, 0.0)))
    tail = jnp.concatenate([hi, lo, hi, tail], axis=1).astype(BF16)
    out[:, width:] = tail
    extended[:, :width] = feats
    extended[:, width : width + 128] = tail
    extended[:, width + 128 :] = embeds[...]


def split_kernel(count, *refs):
    line, embeds = refs[count:]
    rows, width = refs[0].shape[0], line.shape[1]
    for k, ref in enumerate(refs[:count]):
        line[k * rows : (k + 1) * rows, :] = ref[:, :width]
        embeds[k * rows : (k + 1) * rows, :] = ref[:, width:]


def left_map(count):
    source = np.zeros((32,), np.int32)
    sign = np.zeros((32,), np.float32)
    sign[0] = 1.0
    for k in range(count):
        source[1 + k], sign[1 + k] = 1 + count + k, -1.0
        source[1 + count + k], sign[1 + count + k] = 1 + k, -1.0
    table = np.zeros((128, 128), np.float32)
    for group, offset in ((0, 0), (1, 0), (2, 32)):
        for k in range(32):
            table[offset + source[k], 32 * group + k] = sign[k]
    return jnp.asarray(table, BF16)


def tile_kernel(sub, step, table, rows_ref, *refs):
    *columns, out = refs
    width = out.shape[1]
    rows = rows_ref.shape[0]
    u_rows = rows_ref[:, :width]
    fac = rows_ref[:, width:]
    twice = (u_rows.astype(F32) * -2.0).astype(BF16)
    left = jnp.dot(fac, table[...], preferred_element_type=F32).astype(BF16)
    lane = lax.broadcasted_iota(jnp.int32, (128, 128), 0)
    pick = jnp.where((lane >= 96) & (lane < 99), 1.0, 0.0).astype(BF16)
    sq_rows = jnp.dot(fac, pick, preferred_element_type=F32)[:, :1]
    lane = lax.broadcasted_iota(jnp.int32, (8, 128), 1)
    pick_cols = jnp.where((lane >= 96) & (lane < 99), 1.0, 0.0).astype(BF16)
    blocks = [slice(k, k + sub) for k in range(0, rows, sub)]
    acc = [jnp.zeros((sub, width), F32) for _ in blocks]
    total = [jnp.zeros((sub, 128), F32) for _ in blocks]
    work = [
        (ref, start, k)
        for ref in columns
        for start in range(0, ref.shape[0], step)
        for k in range(len(blocks))
    ]

    def products(ref, start, k):
        u_cols = ref[start : start + step, :width]
        right = ref[start : start + step, width:]
        sq_cols = dot_nt(pick_cols, right)[:1]
        return u_cols, sq_cols, dot_nt(twice[blocks[k]], u_cols), dot_nt(left[blocks[k]], right)

    ahead = products(*work[0])
    for index, (_, _, k) in enumerate(work):
        u_cols, sq_cols, cross, pair = ahead
        if index + 1 < len(work):
            ahead = products(*work[index + 1])
        d2 = jnp.maximum((sq_rows[blocks[k]] + sq_cols) + cross, 1e-30)
        dist = d2 * lax.rsqrt(d2)
        coupling = pair * ((dist + 1.0 / ROOT5) * jnp.exp2(dist * (-ROOT5 * LOG2E)))
        for j in range(0, step, 128):
            total[k] = total[k] + coupling[:, j : j + 128]
        acc[k] = acc[k] + jnp.dot(coupling.astype(BF16), u_cols, preferred_element_type=F32)
    for k, block in enumerate(blocks):
        row_total = jnp.sum(total[k], axis=1, keepdims=True)
        out[block, :] = (acc[k] - row_total * u_rows[block].astype(F32)).astype(out.dtype)


def sum_rows_kernel(count, *refs):
    parts, (embeds, partial, own, *others) = refs[:count], refs[count:]
    rows = own.shape[0]
    total = parts[0][...]
    for ref in parts[1:]:
        total = total + ref[...].astype(F32)
    hi = total.astype(BF16)
    lo = (total - hi.astype(F32)).astype(BF16)
    own[...] = total[:rows]
    for k, ref in enumerate(others):
        ref[...] = hi[(k + 1) * rows : (k + 2) * rows]
    partial[...] = (dot_tn(embeds[...], hi) + dot_tn(embeds[...], lo)).astype(BF16)


def finish_rows_kernel(own, b, c, d, grad_rows):
    grad_rows[...] = (own[...] + b[...].astype(F32)) + (c[...].astype(F32) + d[...].astype(F32))


def sum_spread_kernel(parts, out):
    total = parts[0].astype(F32)
    for k in range(1, parts.shape[0]):
        total = total + parts[k].astype(F32)
    low = total.astype(out.dtype)
    for k in range(out.shape[0]):
        out[k] = low


def sum_spread(parts, copies, dtype):
    return pl.pallas_call(
        sum_spread_kernel,
        out_shape=jax.ShapeDtypeStruct((copies,) + parts.shape[1:], dtype),
        in_specs=[VMEM],
        out_specs=VMEM,
        compiler_params=params(16),
        name="sum_spread",
    )(parts)


def ring(array, axis, size, shift):
    return lax.ppermute(array, axis, [(i, (i + shift) % size) for i in range(size)])


def move(array, sizes, where):
    dims = [sizes[a] for a in ALL]
    perm = []
    for source in range(math.prod(dims)):
        place = dict(zip(ALL, (int(i) for i in np.unravel_index(source, dims))))
        for axis, shift in where(place["core"]).items():
            if axis == "z":
                z = (place["zh"] * sizes["zl"] + place["zl"] + shift) % (sizes["zh"] * sizes["zl"])
                place["zh"], place["zl"] = divmod(z, sizes["zl"])
            else:
                place[axis] = (place[axis] + shift) % sizes[axis]
        perm.append((source, int(np.ravel_multi_index([place[a] for a in ALL], dims))))
    return lax.ppermute(array, ALL, perm)


def turn(array, sizes, stage, shift):
    return move(array, sizes, lambda core: {"y" if (core + stage) % 2 == 0 else "x": shift})


def exchange(array, axes):
    return lax.all_to_all(array, axes, split_axis=0, concat_axis=0, tiled=True)


def shards(sizes, embeds, weight, solve, probes, probe_solves):
    rows, width = embeds.shape[0], weight.shape[1]
    n_side, n_z = sizes["x"], sizes["zh"] * sizes["zl"]
    pack, extended = pl.pallas_call(
        pack_kernel,
        out_shape=[
            jax.ShapeDtypeStruct((rows, width + 128), BF16),
            jax.ShapeDtypeStruct((rows, width + 128 + embeds.shape[1]), BF16),
        ],
        in_specs=[VMEM] * 5,
        out_specs=[VMEM] * 2,
        compiler_params=params(16),
        name="pack",
    )(embeds, weight, solve[None, :], probes.T, probe_solves.T)

    blocks = [extended] + [turn(extended, sizes, 0, -d) for d in range(1, n_side)]
    line, embeds_line = pl.pallas_call(
        functools.partial(split_kernel, n_side),
        out_shape=[
            jax.ShapeDtypeStruct((n_side * rows, width + 128), BF16),
            jax.ShapeDtypeStruct((n_side * rows, embeds.shape[1]), BF16),
        ],
        in_specs=[VMEM] * n_side,
        out_specs=[VMEM] * 2,
        compiler_params=params(8),
        name="split",
    )(*blocks)
    pair = jnp.concatenate([pack, ring(pack, DEPTH, n_z, n_z // 2)], axis=0)
    pair, line = lax.optimization_barrier((pair, line))
    four = jnp.concatenate([pair, ring(pair, "core", 2, 1)], axis=0)
    near = move(four, sizes, lambda core: {"z": 1 - 2 * core})
    far = ring(pair, DEPTH, n_z, 2)
    lines = [line] + [turn(line, sizes, 1, -d) for d in range(1, n_side)]
    near, far, lines = lax.optimization_barrier((near, far, lines))
    columns = [four, near, far, ring(near, "core", 2, 1), ring(far, "core", 2, 1)]

    table = left_map(probes.shape[1])
    back = {}
    for d in (0, 3, 1, 2):
        part = pl.pallas_call(
            functools.partial(tile_kernel, 256, 256),
            out_shape=jax.ShapeDtypeStruct((n_side * rows, width), F32 if d == 0 else BF16),
            in_specs=[VMEM] * (2 + len(columns)),
            out_specs=VMEM,
            compiler_params=params(16),
            name="tile",
        )(table, lines[d], *columns)
        back[d] = part if d == 0 else turn(part, sizes, 1, d)

    partial, own_rows, *other_rows = pl.pallas_call(
        functools.partial(sum_rows_kernel, n_side),
        out_shape=[
            jax.ShapeDtypeStruct((embeds.shape[1], width), BF16),
            jax.ShapeDtypeStruct((rows, width), F32),
        ]
        + [jax.ShapeDtypeStruct((rows, width), BF16)] * (n_side - 1),
        in_specs=[VMEM] * (n_side + 1),
        out_specs=[VMEM] * (n_side + 1),
        compiler_params=params(16),
        name="sum_rows",
    )(*(back[d] for d in range(n_side)), embeds_line)
    arrived = [turn(block, sizes, 0, d + 1) for d, block in enumerate(other_rows)]
    n_plane = n_side * n_side * 2
    pieces = exchange(partial.reshape(n_plane, -1, width), PLANE)
    pieces, arrived[0], arrived[1] = lax.optimization_barrier((pieces, arrived[0], arrived[1]))
    pieces = exchange(sum_spread(pieces, n_z, F32), DEPTH)
    pieces, arrived[2] = lax.optimization_barrier((pieces, arrived[2]))
    pieces = exchange(sum_spread(pieces, n_plane, BF16), PLANE)
    total_points = rows * n_plane * n_z
    grad_weight = pieces.reshape(-1, width).astype(F32) * (1.0 / math.sqrt(total_points))
    grad_rows = pl.pallas_call(
        finish_rows_kernel,
        out_shape=jax.ShapeDtypeStruct((rows, width), F32),
        in_specs=[VMEM] * 4,
        out_specs=VMEM,
        compiler_params=params(16),
        name="finish_rows",
    )(own_rows, *arrived)
    return grad_rows, grad_weight


def solution(mesh):
    sizes = {"y": 4, "zh": 2, "core": 2, "zl": 4, "x": 4}
    fine = Mesh(mesh.devices.reshape(tuple(sizes[a] for a in ALL)), ALL)
    return jax.shard_map(
        functools.partial(shards, sizes),
        mesh=fine,
        in_specs=(P(ALL, None), P(), P(ALL), P(ALL, None), P(ALL, None)),
        out_specs=(P(ALL, None), P()),
        check_vma=False,
    )
```

```python
import functools
import math

import jax
import jax.numpy as jnp
import numpy as np
from jax import lax
from jax.experimental import pallas as pl
from jax.experimental.pallas import tpu as pltpu
from jax.sharding import Mesh, PartitionSpec as P

LOG2E = math.log2(math.e)
ROOT5 = math.sqrt(5.0)
ALL = ("y", "zh", "core", "zl", "x")
PLANE = ("y", "core", "x")
DEPTH = ("zh", "zl")
F32 = jnp.float32
BF16 = jnp.bfloat16
VMEM = pl.BlockSpec(memory_space=pltpu.VMEM)


def params(mib):
    return pltpu.CompilerParams(vmem_limit_bytes=mib << 20)


def dot_nt(a, b):
    return lax.dot_general(a, b, (((1,), (1,)), ((), ())), preferred_element_type=F32)


def dot_tn(a, b):
    return lax.dot_general(a, b, (((0,), (0,)), ((), ())), preferred_element_type=F32)


def pack_kernel(embeds, weight, factors, copies, extended):
    rows, width = embeds.shape[0], weight.shape[1]
    feats = jnp.dot(embeds[...], weight[...], preferred_element_type=F32).astype(BF16)
    wide = feats.astype(F32)
    sq = jnp.sum(wide * wide, axis=1, keepdims=True)
    sq_hi = sq.astype(BF16).astype(F32)
    sq_mid = (sq - sq_hi).astype(BF16).astype(F32)
    sq_lo = sq - sq_hi - sq_mid
    both = factors[...].T
    hi = both.astype(BF16).astype(F32)
    lo = both - hi
    lane = lax.broadcasted_iota(jnp.int32, (rows, 32), 1)
    tail = jnp.where(lane == 0, sq_hi, jnp.where(lane == 1, sq_mid, jnp.where(lane == 2, sq_lo, 0.0)))
    tail = jnp.concatenate([hi, lo, hi, tail], axis=1).astype(BF16)
    extended[:, :width] = feats
    extended[:, width : width + 128] = tail
    extended[:, width + 128 :] = embeds[...]
    for k in range(copies.shape[0]):
        copies[k, :, :width] = feats
        copies[k, :, width:] = tail


def split_kernel(count, *refs):
    line, embeds = refs[count:]
    rows, width = refs[0].shape[0], line.shape[1]
    for k, ref in enumerate(refs[:count]):
        line[k * rows : (k + 1) * rows, :] = ref[:, :width]
        embeds[k * rows : (k + 1) * rows, :] = ref[:, width:]


def left_map(count):
    source = np.zeros((32,), np.int32)
    sign = np.zeros((32,), np.float32)
    sign[0] = 1.0
    for k in range(count):
        source[1 + k], sign[1 + k] = 1 + count + k, -1.0
        source[1 + count + k], sign[1 + count + k] = 1 + k, -1.0
    table = np.zeros((128, 128), np.float32)
    for group, offset in ((0, 0), (1, 0), (2, 32)):
        for k in range(32):
            table[offset + source[k], 32 * group + k] = sign[k]
    return jnp.asarray(table, BF16)


def tile_kernel(sub, step, table, rows_ref, *refs):
    *columns, out = refs
    width = out.shape[1]
    rows = rows_ref.shape[0]
    u_rows = rows_ref[:, :width]
    fac = rows_ref[:, width:]
    twice = (u_rows.astype(F32) * -2.0).astype(BF16)
    left = jnp.dot(fac, table[...], preferred_element_type=F32).astype(BF16)
    lane = lax.broadcasted_iota(jnp.int32, (128, 128), 0)
    pick = jnp.where((lane >= 96) & (lane < 99), 1.0, 0.0).astype(BF16)
    sq_rows = jnp.dot(fac, pick, preferred_element_type=F32)[:, :1]
    lane = lax.broadcasted_iota(jnp.int32, (8, 128), 1)
    pick_cols = jnp.where((lane >= 96) & (lane < 99), 1.0, 0.0).astype(BF16)
    blocks = [slice(k, k + sub) for k in range(0, rows, sub)]
    acc = [jnp.zeros((sub, width), F32) for _ in blocks]
    total = [jnp.zeros((sub, 128), F32) for _ in blocks]
    work = [
        (ref, start, k)
        for ref in columns
        for start in range(0, ref.shape[0], step)
        for k in range(len(blocks))
    ]

    def products(ref, start, k):
        u_cols = ref[start : start + step, :width]
        right = ref[start : start + step, width:]
        sq_cols = dot_nt(pick_cols, right)[:1]
        return u_cols, sq_cols, dot_nt(twice[blocks[k]], u_cols), dot_nt(left[blocks[k]], right)

    ahead = products(*work[0])
    for index, (_, _, k) in enumerate(work):
        u_cols, sq_cols, cross, pair = ahead
        if index + 1 < len(work):
            ahead = products(*work[index + 1])
        d2 = jnp.maximum((sq_rows[blocks[k]] + sq_cols) + cross, 1e-30)
        dist = d2 * lax.rsqrt(d2)
        coupling = pair * ((dist + 1.0 / ROOT5) * jnp.exp2(dist * (-ROOT5 * LOG2E)))
        for j in range(0, step, 128):
            total[k] = total[k] + coupling[:, j : j + 128]
        acc[k] = acc[k] + jnp.dot(coupling.astype(BF16), u_cols, preferred_element_type=F32)
    for k, block in enumerate(blocks):
        row_total = jnp.sum(total[k], axis=1, keepdims=True)
        out[block, :] = (acc[k] - row_total * u_rows[block].astype(F32)).astype(out.dtype)


def sum_rows_kernel(count, *refs):
    parts, (embeds, partial, own, *others) = refs[:count], refs[count:]
    rows = own.shape[0]
    total = parts[0][...]
    for ref in parts[1:]:
        total = total + ref[...].astype(F32)
    hi = total.astype(BF16)
    lo = (total - hi.astype(F32)).astype(BF16)
    own[...] = total[:rows]
    for k, ref in enumerate(others):
        ref[...] = hi[(k + 1) * rows : (k + 2) * rows]
    partial[...] = (dot_tn(embeds[...], hi) + dot_tn(embeds[...], lo)).astype(BF16)


def finish_rows_kernel(own, b, c, d, grad_rows):
    grad_rows[...] = (own[...] + b[...].astype(F32)) + (c[...].astype(F32) + d[...].astype(F32))


def sum_spread_kernel(parts, out):
    total = parts[0].astype(F32)
    for k in range(1, parts.shape[0]):
        total = total + parts[k].astype(F32)
    low = total.astype(out.dtype)
    for k in range(out.shape[0]):
        out[k] = low


def sum_spread(parts, copies, dtype):
    return pl.pallas_call(
        sum_spread_kernel,
        out_shape=jax.ShapeDtypeStruct((copies,) + parts.shape[1:], dtype),
        in_specs=[VMEM],
        out_specs=VMEM,
        compiler_params=params(16),
        name="sum_spread",
    )(parts)


def ring(array, axis, size, shift):
    return lax.ppermute(array, axis, [(i, (i + shift) % size) for i in range(size)])


def move(array, sizes, where):
    dims = [sizes[a] for a in ALL]
    perm = []
    for source in range(math.prod(dims)):
        place = dict(zip(ALL, (int(i) for i in np.unravel_index(source, dims))))
        for axis, shift in where(place["core"]).items():
            if axis == "z":
                z = (place["zh"] * sizes["zl"] + place["zl"] + shift) % (sizes["zh"] * sizes["zl"])
                place["zh"], place["zl"] = divmod(z, sizes["zl"])
            else:
                place[axis] = (place[axis] + shift) % sizes[axis]
        perm.append((source, int(np.ravel_multi_index([place[a] for a in ALL], dims))))
    return lax.ppermute(array, ALL, perm)


def turn(array, sizes, stage, shift):
    return move(array, sizes, lambda core: {"y" if (core + stage) % 2 == 0 else "x": shift})


def exchange(array, axes):
    return lax.all_to_all(array, axes, split_axis=0, concat_axis=0, tiled=True)


def shards(sizes, embeds, weight, solve, probes, probe_solves):
    rows, width = embeds.shape[0], weight.shape[1]
    n_side, n_z = sizes["x"], sizes["zh"] * sizes["zl"]
    fold = math.sqrt(5.0 / 3.0 * ROOT5)
    scale = (2.0 * probes.shape[1]) ** (-0.5) * fold
    factors = jnp.concatenate(
        [solve[None, :] * fold, probes.T * -scale, probe_solves.T * -scale, jnp.zeros((1, rows), F32)],
        axis=0,
    )
    copies, extended = pl.pallas_call(
        pack_kernel,
        out_shape=[
            jax.ShapeDtypeStruct((n_z, rows, width + 128), BF16),
            jax.ShapeDtypeStruct((rows, width + 128 + embeds.shape[1]), BF16),
        ],
        in_specs=[VMEM] * 3,
        out_specs=[VMEM] * 2,
        compiler_params=params(16),
        name="pack",
    )(embeds, weight, factors)

    blocks = [extended] + [turn(extended, sizes, 0, -d) for d in range(1, n_side)]
    line, embeds_line = pl.pallas_call(
        functools.partial(split_kernel, n_side),
        out_shape=[
            jax.ShapeDtypeStruct((n_side * rows, width + 128), BF16),
            jax.ShapeDtypeStruct((n_side * rows, embeds.shape[1]), BF16),
        ],
        in_specs=[VMEM] * n_side,
        out_specs=[VMEM] * 2,
        compiler_params=params(8),
        name="split",
    )(*blocks)
    stack = exchange(copies, DEPTH).reshape(n_z * rows, width + 128)
    stack, line = lax.optimization_barrier((stack, line))
    lines = [line] + [turn(line, sizes, 1, -d) for d in range(1, n_side)]
    columns = [stack, ring(stack, "core", 2, 1)]

    table = left_map(probes.shape[1])
    back = {}
    for d in (0, 3, 1, 2):
        if d != 0:
            lines[d], _ = lax.optimization_barrier((lines[d], back[0]))
        part = pl.pallas_call(
            functools.partial(tile_kernel, 256, 256),
            out_shape=jax.ShapeDtypeStruct((n_side * rows, width), F32 if d == 0 else BF16),
            in_specs=[VMEM] * (2 + len(columns)),
            out_specs=VMEM,
            compiler_params=params(16),
            name="tile",
        )(table, lines[d], *columns)
        back[d] = part if d == 0 else turn(part, sizes, 1, d)

    partial, own_rows, *other_rows = pl.pallas_call(
        functools.partial(sum_rows_kernel, n_side),
        out_shape=[
            jax.ShapeDtypeStruct((embeds.shape[1], width), BF16),
            jax.ShapeDtypeStruct((rows, width), F32),
        ]
        + [jax.ShapeDtypeStruct((rows, width), BF16)] * (n_side - 1),
        in_specs=[VMEM] * (n_side + 1),
        out_specs=[VMEM] * (n_side + 1),
        compiler_params=params(16),
        name="sum_rows",
    )(*(back[d] for d in range(n_side)), embeds_line)
    arrived = [turn(block, sizes, 0, d + 1) for d, block in enumerate(other_rows)]
    n_plane = n_side * n_side * 2
    pieces = exchange(partial.reshape(n_plane, -1, width), PLANE)
    pieces, arrived[0] = lax.optimization_barrier((pieces, arrived[0]))
    pieces = exchange(sum_spread(pieces, n_z, F32), DEPTH)
    pieces, arrived[1] = lax.optimization_barrier((pieces, arrived[1]))
    pieces = exchange(sum_spread(pieces, n_plane, BF16), PLANE)
    grad_rows = pl.pallas_call(
        finish_rows_kernel,
        out_shape=jax.ShapeDtypeStruct((rows, width), F32),
        in_specs=[VMEM] * 4,
        out_specs=VMEM,
        compiler_params=params(16),
        name="finish_rows",
    )(own_rows, *arrived)
    pieces, grad_rows = lax.optimization_barrier((pieces, grad_rows))
    total_points = rows * n_plane * n_z
    grad_weight = pieces.reshape(-1, width).astype(F32) * (1.0 / math.sqrt(total_points))
    return grad_rows, grad_weight


def solution(mesh):
    sizes = {"y": 4, "zh": 2, "core": 2, "zl": 4, "x": 4}
    fine = Mesh(mesh.devices.reshape(tuple(sizes[a] for a in ALL)), ALL)
    return jax.shard_map(
        functools.partial(shards, sizes),
        mesh=fine,
        in_specs=(P(ALL, None), P(), P(ALL), P(ALL, None), P(ALL, None)),
        out_specs=(P(ALL, None), P()),
        check_vma=False,
    )
```

```python
import functools
import math

import jax
import jax.numpy as jnp
import numpy as np
from jax import lax
from jax.experimental import pallas as pl
from jax.experimental.pallas import tpu as pltpu
from jax.sharding import Mesh, PartitionSpec as P

LOG2E = math.log2(math.e)
ROOT5 = math.sqrt(5.0)
ALL = ("y", "zh", "core", "zl", "x")
PLANE = ("y", "core", "x")
DEPTH = ("zh", "zl")
F32 = jnp.float32
BF16 = jnp.bfloat16
VMEM = pl.BlockSpec(memory_space=pltpu.VMEM)


def params(mib):
    return pltpu.CompilerParams(vmem_limit_bytes=mib << 20)


def dot_nt(a, b):
    return lax.dot_general(a, b, (((1,), (1,)), ((), ())), preferred_element_type=F32)


def dot_tn(a, b):
    return lax.dot_general(a, b, (((0,), (0,)), ((), ())), preferred_element_type=F32)


def pack_kernel(embeds, weight, solve, probes, probe_solves, packed, extended, weight_in, solve_in, probes_in, probe_solves_in, sems):
    rows, width = embeds.shape[0], weight.shape[1]
    embeds_in = extended.at[:, width + 128 :]
    loads = [
        pltpu.make_async_copy(source, target, sems.at[k])
        for k, (source, target) in enumerate(
            (
                (weight, weight_in),
                (embeds, embeds_in),
                (probes, probes_in),
                (probe_solves, probe_solves_in),
                (solve, solve_in),
            )
        )
    ]
    for load in loads:
        load.start()
    for load in loads:
        load.wait()
    feats = jnp.dot(embeds_in[...], weight_in[...], preferred_element_type=F32).astype(BF16)
    wide = feats.astype(F32)
    sq = jnp.sum(wide * wide, axis=1, keepdims=True)
    sq_hi = sq.astype(BF16).astype(F32)
    sq_mid = (sq - sq_hi).astype(BF16).astype(F32)
    sq_lo = sq - sq_hi - sq_mid
    fold = math.sqrt(5.0 / 3.0 * ROOT5)
    scale = (2.0 * probes.shape[0]) ** (-0.5) * fold
    both = jnp.concatenate(
        [solve_in[...] * fold, probes_in[...] * -scale, probe_solves_in[...] * -scale, jnp.zeros((1, rows), F32)],
        axis=0,
    ).T
    hi = both.astype(BF16).astype(F32)
    lo = both - hi
    lane = lax.broadcasted_iota(jnp.int32, (rows, 32), 1)
    tail = jnp.where(lane == 0, sq_hi, jnp.where(lane == 1, sq_mid, jnp.where(lane == 2, sq_lo, 0.0)))
    tail = jnp.concatenate([hi, lo, hi, tail], axis=1).astype(BF16)
    extended[:, :width] = feats
    extended[:, width : width + 128] = tail
    packed[:, :width] = feats
    packed[:, width:] = tail


def split_kernel(count, *refs):
    line, embeds = refs[count:]
    rows, width = refs[0].shape[0], line.shape[1]
    for k, ref in enumerate(refs[:count]):
        line[k * rows : (k + 1) * rows, :] = ref[:, :width]
        embeds[k * rows : (k + 1) * rows, :] = ref[:, width:]


def left_map(count):
    source = np.zeros((32,), np.int32)
    sign = np.zeros((32,), np.float32)
    sign[0] = 1.0
    for k in range(count):
        source[1 + k], sign[1 + k] = 1 + count + k, -1.0
        source[1 + count + k], sign[1 + count + k] = 1 + k, -1.0
    table = np.zeros((128, 128), np.float32)
    for group, offset in ((0, 0), (1, 0), (2, 32)):
        for k in range(32):
            table[offset + source[k], 32 * group + k] = sign[k]
    return jnp.asarray(table, BF16)


def tile_kernel(sub, step, table, rows_ref, *refs):
    *columns, out = refs
    width = out.shape[1]
    rows = rows_ref.shape[0]
    u_rows = rows_ref[:, :width]
    fac = rows_ref[:, width:]
    twice = (u_rows.astype(F32) * -2.0).astype(BF16)
    left = jnp.dot(fac, table[...], preferred_element_type=F32).astype(BF16)
    lane = lax.broadcasted_iota(jnp.int32, (128, 128), 0)
    pick = jnp.where((lane >= 96) & (lane < 99), 1.0, 0.0).astype(BF16)
    sq_rows = jnp.dot(fac, pick, preferred_element_type=F32)[:, :1]
    lane = lax.broadcasted_iota(jnp.int32, (8, 128), 1)
    pick_cols = jnp.where((lane >= 96) & (lane < 99), 1.0, 0.0).astype(BF16)
    blocks = [slice(k, k + sub) for k in range(0, rows, sub)]
    acc = [jnp.zeros((sub, width), F32) for _ in blocks]
    total = [jnp.zeros((sub, 128), F32) for _ in blocks]
    work = [
        (ref, start, k)
        for ref in columns
        for start in range(0, ref.shape[0], step)
        for k in range(len(blocks))
    ]

    def products(ref, start, k):
        u_cols = ref[start : start + step, :width]
        right = ref[start : start + step, width:]
        sq_cols = dot_nt(pick_cols, right)[:1]
        return u_cols, sq_cols, dot_nt(twice[blocks[k]], u_cols), dot_nt(left[blocks[k]], right)

    ahead = products(*work[0])
    for index, (_, _, k) in enumerate(work):
        u_cols, sq_cols, cross, pair = ahead
        if index + 1 < len(work):
            ahead = products(*work[index + 1])
        d2 = jnp.maximum((sq_rows[blocks[k]] + sq_cols) + cross, 1e-30)
        dist = d2 * lax.rsqrt(d2)
        coupling = pair * ((dist + 1.0 / ROOT5) * jnp.exp2(dist * (-ROOT5 * LOG2E)))
        for j in range(0, step, 128):
            total[k] = total[k] + coupling[:, j : j + 128]
        acc[k] = acc[k] + jnp.dot(coupling.astype(BF16), u_cols, preferred_element_type=F32)
    for k, block in enumerate(blocks):
        row_total = jnp.sum(total[k], axis=1, keepdims=True)
        out[block, :] = (acc[k] - row_total * u_rows[block].astype(F32)).astype(out.dtype)


def sum_rows_kernel(count, *refs):
    parts, (embeds, partial, own, *others) = refs[:count], refs[count:]
    rows = own.shape[0]
    total = parts[0][...]
    for ref in parts[1:]:
        total = total + ref[...].astype(F32)
    hi = total.astype(BF16)
    lo = (total - hi.astype(F32)).astype(BF16)
    own[...] = total[:rows]
    for k, ref in enumerate(others):
        ref[...] = hi[(k + 1) * rows : (k + 2) * rows]
    partial[...] = (dot_tn(embeds[...], hi) + dot_tn(embeds[...], lo)).astype(BF16)


def finish_rows_kernel(own, b, c, d, grad_rows):
    grad_rows[...] = (own[...] + b[...].astype(F32)) + (c[...].astype(F32) + d[...].astype(F32))


def sum_spread_kernel(parts, out):
    total = parts[0].astype(F32)
    for k in range(1, parts.shape[0]):
        total = total + parts[k].astype(F32)
    low = total.astype(out.dtype)
    for k in range(out.shape[0]):
        out[k] = low


def sum_spread(parts, copies, dtype):
    return pl.pallas_call(
        sum_spread_kernel,
        out_shape=jax.ShapeDtypeStruct((copies,) + parts.shape[1:], dtype),
        in_specs=[VMEM],
        out_specs=VMEM,
        compiler_params=params(16),
        name="sum_spread",
    )(parts)


def ring(array, axis, size, shift):
    return lax.ppermute(array, axis, [(i, (i + shift) % size) for i in range(size)])


def move(array, sizes, where):
    dims = [sizes[a] for a in ALL]
    perm = []
    for source in range(math.prod(dims)):
        place = dict(zip(ALL, (int(i) for i in np.unravel_index(source, dims))))
        for axis, shift in where(place["core"]).items():
            if axis == "z":
                z = (place["zh"] * sizes["zl"] + place["zl"] + shift) % (sizes["zh"] * sizes["zl"])
                place["zh"], place["zl"] = divmod(z, sizes["zl"])
            else:
                place[axis] = (place[axis] + shift) % sizes[axis]
        perm.append((source, int(np.ravel_multi_index([place[a] for a in ALL], dims))))
    return lax.ppermute(array, ALL, perm)


def turn(array, sizes, stage, shift):
    return move(array, sizes, lambda core: {"y" if (core + stage) % 2 == 0 else "x": shift})


def exchange(array, axes):
    return lax.all_to_all(array, axes, split_axis=0, concat_axis=0, tiled=True)


def shards(sizes, embeds, weight, solve, probes, probe_solves):
    rows, width = embeds.shape[0], weight.shape[1]
    n_side, n_z = sizes["x"], sizes["zh"] * sizes["zl"]
    pack, extended = pl.pallas_call(
        pack_kernel,
        out_shape=[
            jax.ShapeDtypeStruct((rows, width + 128), BF16),
            jax.ShapeDtypeStruct((rows, width + 128 + embeds.shape[1]), BF16),
        ],
        in_specs=[pl.BlockSpec(memory_space=pl.ANY)] * 5,
        out_specs=[VMEM] * 2,
        scratch_shapes=[
            pltpu.VMEM(weight.shape, BF16),
            pltpu.VMEM((1, rows), F32),
            pltpu.VMEM(probes.shape[::-1], F32),
            pltpu.VMEM(probes.shape[::-1], F32),
            pltpu.SemaphoreType.DMA((5,)),
        ],
        compiler_params=params(48),
        name="pack",
    )(embeds, weight, solve[None, :], probes.T, probe_solves.T)

    blocks = [extended] + [turn(extended, sizes, 0, -d) for d in range(1, n_side)]
    line, embeds_line = pl.pallas_call(
        functools.partial(split_kernel, n_side),
        out_shape=[
            jax.ShapeDtypeStruct((n_side * rows, width + 128), BF16),
            jax.ShapeDtypeStruct((n_side * rows, embeds.shape[1]), BF16),
        ],
        in_specs=[VMEM] * n_side,
        out_specs=[VMEM] * 2,
        compiler_params=params(8),
        name="split",
    )(*blocks)
    pair = jnp.concatenate([pack, ring(pack, DEPTH, n_z, n_z // 2)], axis=0)
    pair, line = lax.optimization_barrier((pair, line))
    swap = ring(pair, "core", 2, 1)
    far = move(pair, sizes, lambda core: {"z": 2 - 4 * core})
    near = [move(part, sizes, lambda core: {"z": 1 - 2 * core}) for part in (pair, swap)]
    lines = [line] + [turn(line, sizes, 1, -d) for d in range(1, n_side)]
    columns = [pair, swap, far, *near] + [ring(part, "core", 2, 1) for part in (far, *near)]

    table = left_map(probes.shape[1])
    back = {}
    for d in (0, 3, 1, 2):
        if d != 0:
            lines[d], _ = lax.optimization_barrier((lines[d], back[0]))
        part = pl.pallas_call(
            functools.partial(tile_kernel, 256, 256),
            out_shape=jax.ShapeDtypeStruct((n_side * rows, width), F32 if d == 0 else BF16),
            in_specs=[VMEM] * (2 + len(columns)),
            out_specs=VMEM,
            compiler_params=params(16),
            name="tile",
        )(table, lines[d], *columns)
        back[d] = part if d == 0 else turn(part, sizes, 1, d)

    partial, own_rows, *other_rows = pl.pallas_call(
        functools.partial(sum_rows_kernel, n_side),
        out_shape=[
            jax.ShapeDtypeStruct((embeds.shape[1], width), BF16),
            jax.ShapeDtypeStruct((rows, width), F32),
        ]
        + [jax.ShapeDtypeStruct((rows, width), BF16)] * (n_side - 1),
        in_specs=[VMEM] * (n_side + 1),
        out_specs=[VMEM] * (n_side + 1),
        compiler_params=params(16),
        name="sum_rows",
    )(*(back[d] for d in range(n_side)), embeds_line)
    arrived = [turn(block, sizes, 0, d + 1) for d, block in enumerate(other_rows)]
    n_plane = n_side * n_side * 2
    pieces = exchange(partial.reshape(n_plane, -1, width), PLANE)
    pieces, arrived[0] = lax.optimization_barrier((pieces, arrived[0]))
    pieces = exchange(sum_spread(pieces, n_z, F32), DEPTH)
    pieces, arrived[1] = lax.optimization_barrier((pieces, arrived[1]))
    pieces = exchange(sum_spread(pieces, n_plane, BF16), PLANE)
    grad_rows = pl.pallas_call(
        finish_rows_kernel,
        out_shape=jax.ShapeDtypeStruct((rows, width), F32),
        in_specs=[VMEM] * 4,
        out_specs=VMEM,
        compiler_params=params(16),
        name="finish_rows",
    )(own_rows, *arrived)
    pieces, grad_rows = lax.optimization_barrier((pieces, grad_rows))
    total_points = rows * n_plane * n_z
    grad_weight = pieces.reshape(-1, width).astype(F32) * (1.0 / math.sqrt(total_points))
    return grad_rows, grad_weight


def solution(mesh):
    sizes = {"y": 4, "zh": 2, "core": 2, "zl": 4, "x": 4}
    fine = Mesh(mesh.devices.reshape(tuple(sizes[a] for a in ALL)), ALL)
    return jax.shard_map(
        functools.partial(shards, sizes),
        mesh=fine,
        in_specs=(P(ALL, None), P(), P(ALL), P(ALL, None), P(ALL, None)),
        out_specs=(P(ALL, None), P()),
        check_vma=False,
    )
```

```python
import functools
import math

import jax
import jax.numpy as jnp
import numpy as np
from jax import lax
from jax.experimental import pallas as pl
from jax.experimental.pallas import tpu as pltpu
from jax.sharding import Mesh, PartitionSpec as P

LOG2E = math.log2(math.e)
ROOT5 = math.sqrt(5.0)
ALL = ("y", "zh", "core", "zl", "x")
PLANE = ("y", "x")
DEPTH = ("zh", "zl")
F32 = jnp.float32
BF16 = jnp.bfloat16
VMEM = pl.BlockSpec(memory_space=pltpu.VMEM)


def params(mib):
    return pltpu.CompilerParams(vmem_limit_bytes=mib << 20)


def dot_nt(a, b):
    return lax.dot_general(a, b, (((1,), (1,)), ((), ())), preferred_element_type=F32)


def dot_tn(a, b):
    return lax.dot_general(a, b, (((0,), (0,)), ((), ())), preferred_element_type=F32)


def pack_kernel(embeds, weight, solve, probes, probe_solves, packed, extended, weight_in, solve_in, probes_in, probe_solves_in, sems):
    rows, width = embeds.shape[0], weight.shape[1]
    embeds_in = extended.at[:, width + 128 :]
    loads = [
        pltpu.make_async_copy(source, target, sems.at[k])
        for k, (source, target) in enumerate(
            (
                (weight, weight_in),
                (embeds, embeds_in),
                (probes, probes_in),
                (probe_solves, probe_solves_in),
                (solve, solve_in),
            )
        )
    ]
    for load in loads:
        load.start()
    for load in loads:
        load.wait()
    feats = jnp.dot(embeds_in[...], weight_in[...], preferred_element_type=F32).astype(BF16)
    wide = feats.astype(F32)
    sq = jnp.sum(wide * wide, axis=1, keepdims=True)
    sq_hi = sq.astype(BF16).astype(F32)
    sq_mid = (sq - sq_hi).astype(BF16).astype(F32)
    sq_lo = sq - sq_hi - sq_mid
    fold = math.sqrt(5.0 / 3.0 * ROOT5)
    scale = (2.0 * probes.shape[0]) ** (-0.5) * fold
    both = jnp.concatenate(
        [solve_in[...] * fold, probes_in[...] * -scale, probe_solves_in[...] * -scale, jnp.zeros((1, rows), F32)],
        axis=0,
    ).T
    hi = both.astype(BF16).astype(F32)
    lo = both - hi
    lane = lax.broadcasted_iota(jnp.int32, (rows, 32), 1)
    tail = jnp.where(lane == 0, sq_hi, jnp.where(lane == 1, sq_mid, jnp.where(lane == 2, sq_lo, 0.0)))
    tail = jnp.concatenate([hi, lo, hi, tail], axis=1).astype(BF16)
    extended[:, :width] = feats
    extended[:, width : width + 128] = tail
    packed[:, :width] = feats
    packed[:, width:] = tail


def split_kernel(count, *refs):
    line, embeds = refs[count:]
    rows, width = refs[0].shape[0], line.shape[1]
    for k, ref in enumerate(refs[:count]):
        line[k * rows : (k + 1) * rows, :] = ref[:, :width]
        embeds[k * rows : (k + 1) * rows, :] = ref[:, width:]


def left_map(count):
    source = np.zeros((32,), np.int32)
    sign = np.zeros((32,), np.float32)
    sign[0] = 1.0
    for k in range(count):
        source[1 + k], sign[1 + k] = 1 + count + k, -1.0
        source[1 + count + k], sign[1 + count + k] = 1 + k, -1.0
    table = np.zeros((128, 128), np.float32)
    for group, offset in ((0, 0), (1, 0), (2, 32)):
        for k in range(32):
            table[offset + source[k], 32 * group + k] = sign[k]
    return jnp.asarray(table, BF16)


def tile_kernel(sub, step, adds, table, rows_ref, *refs):
    *columns, out = refs
    if adds:
        begin, *columns = columns
    width = out.shape[1]
    rows = rows_ref.shape[0]
    u_rows = rows_ref[:, :width]
    fac = rows_ref[:, width:]
    twice = (u_rows.astype(F32) * -2.0).astype(BF16)
    left = jnp.dot(fac, table[...], preferred_element_type=F32).astype(BF16)
    lane = lax.broadcasted_iota(jnp.int32, (128, 128), 0)
    pick = jnp.where((lane >= 96) & (lane < 99), 1.0, 0.0).astype(BF16)
    sq_rows = jnp.dot(fac, pick, preferred_element_type=F32)[:, :1]
    lane = lax.broadcasted_iota(jnp.int32, (8, 128), 1)
    pick_cols = jnp.where((lane >= 96) & (lane < 99), 1.0, 0.0).astype(BF16)
    blocks = [slice(k, k + sub) for k in range(0, rows, sub)]
    acc = [begin[block, :] if adds else jnp.zeros((sub, width), F32) for block in blocks]
    total = [jnp.zeros((sub, 128), F32) for _ in blocks]
    work = [
        (ref, start, k)
        for ref in columns
        for start in range(0, ref.shape[0], step)
        for k in range(len(blocks))
    ]

    def products(ref, start, k):
        u_cols = ref[start : start + step, :width]
        right = ref[start : start + step, width:]
        sq_cols = dot_nt(pick_cols, right)[:1]
        return u_cols, sq_cols, dot_nt(twice[blocks[k]], u_cols), dot_nt(left[blocks[k]], right)

    ahead = products(*work[0])
    for index, (_, _, k) in enumerate(work):
        u_cols, sq_cols, cross, pair = ahead
        if index + 1 < len(work):
            ahead = products(*work[index + 1])
        d2 = jnp.maximum((sq_rows[blocks[k]] + sq_cols) + cross, 1e-30)
        dist = d2 * lax.rsqrt(d2)
        coupling = pair * ((dist + 1.0 / ROOT5) * jnp.exp2(dist * (-ROOT5 * LOG2E)))
        for j in range(0, step, 128):
            total[k] = total[k] + coupling[:, j : j + 128]
        acc[k] = acc[k] + jnp.dot(coupling.astype(BF16), u_cols, preferred_element_type=F32)
    for k, block in enumerate(blocks):
        row_total = jnp.sum(total[k], axis=1, keepdims=True)
        out[block, :] = (acc[k] - row_total * u_rows[block].astype(F32)).astype(out.dtype)


def sum_rows_kernel(count, *refs):
    parts, (embeds, partial, own, *others) = refs[:count], refs[count:]
    rows = own.shape[0]
    total = parts[0][...]
    for ref in parts[1:]:
        total = total + ref[...].astype(F32)
    hi = total.astype(BF16)
    lo = (total - hi.astype(F32)).astype(BF16)
    own[...] = total[:rows]
    for k, ref in enumerate(others):
        ref[...] = hi[(k + 1) * rows : (k + 2) * rows]
    partial[...] = (dot_tn(embeds[...], hi) + dot_tn(embeds[...], lo)).astype(BF16)


def finish_rows_kernel(own, b, c, d, grad_rows):
    grad_rows[...] = (own[...] + b[...].astype(F32)) + (c[...].astype(F32) + d[...].astype(F32))


def sum_spread_kernel(*refs):
    *parts, out = refs
    total = None
    for ref in parts:
        for k in range(ref.shape[0]):
            term = ref[k].astype(F32)
            total = term if total is None else total + term
    low = total.astype(out.dtype)
    for k in range(out.shape[0]):
        out[k] = low


def sum_spread(parts, copies, dtype):
    return pl.pallas_call(
        sum_spread_kernel,
        out_shape=jax.ShapeDtypeStruct((copies,) + parts[0].shape[1:], dtype),
        in_specs=[VMEM] * len(parts),
        out_specs=VMEM,
        compiler_params=params(16),
        name="sum_spread",
    )(*parts)


def ring(array, axis, size, shift):
    return lax.ppermute(array, axis, [(i, (i + shift) % size) for i in range(size)])


def move(array, sizes, where):
    dims = [sizes[a] for a in ALL]
    perm = []
    for source in range(math.prod(dims)):
        place = dict(zip(ALL, (int(i) for i in np.unravel_index(source, dims))))
        for axis, shift in where(place["core"]).items():
            if axis == "z":
                z = (place["zh"] * sizes["zl"] + place["zl"] + shift) % (sizes["zh"] * sizes["zl"])
                place["zh"], place["zl"] = divmod(z, sizes["zl"])
            else:
                place[axis] = (place[axis] + shift) % sizes[axis]
        perm.append((source, int(np.ravel_multi_index([place[a] for a in ALL], dims))))
    return lax.ppermute(array, ALL, perm)


def turn(array, sizes, stage, shift):
    return move(array, sizes, lambda core: {"y" if (core + stage) % 2 == 0 else "x": shift})


def exchange(array, axes):
    return lax.all_to_all(array, axes, split_axis=0, concat_axis=0, tiled=True)


def shards(sizes, embeds, weight, solve, probes, probe_solves):
    rows, width = embeds.shape[0], weight.shape[1]
    n_side, n_z = sizes["x"], sizes["zh"] * sizes["zl"]
    pack, extended = pl.pallas_call(
        pack_kernel,
        out_shape=[
            jax.ShapeDtypeStruct((rows, width + 128), BF16),
            jax.ShapeDtypeStruct((rows, width + 128 + embeds.shape[1]), BF16),
        ],
        in_specs=[pl.BlockSpec(memory_space=pltpu.HBM)] * 5,
        out_specs=[VMEM] * 2,
        scratch_shapes=[
            pltpu.VMEM(weight.shape, BF16),
            pltpu.VMEM((1, rows), F32),
            pltpu.VMEM(probes.shape[::-1], F32),
            pltpu.VMEM(probes.shape[::-1], F32),
            pltpu.SemaphoreType.DMA((5,)),
        ],
        compiler_params=params(48),
        name="pack",
    )(*(pltpu.with_memory_space_constraint(a, pltpu.HBM) for a in (embeds, weight, solve[None, :], probes.T, probe_solves.T)))

    blocks = [extended] + [turn(extended, sizes, 0, -d) for d in range(1, n_side)]
    line, embeds_line = pl.pallas_call(
        functools.partial(split_kernel, n_side),
        out_shape=[
            jax.ShapeDtypeStruct((n_side * rows, width + 128), BF16),
            jax.ShapeDtypeStruct((n_side * rows, embeds.shape[1]), BF16),
        ],
        in_specs=[VMEM] * n_side,
        out_specs=[VMEM] * 2,
        compiler_params=params(8),
        name="split",
    )(*blocks)
    pair = jnp.concatenate([pack, ring(pack, DEPTH, n_z, n_z // 2)], axis=0)
    pair, line = lax.optimization_barrier((pair, line))
    four = jnp.concatenate([pair, ring(pair, "core", 2, 1)], axis=0)
    near = move(four, sizes, lambda core: {"z": 1 - 2 * core})
    far = move(pair, sizes, lambda core: {"z": 2 - 4 * core})
    lines = [line] + [turn(line, sizes, 1, -d) for d in range(1, n_side)]
    near, far, lines = lax.optimization_barrier((near, far, lines))
    columns = [four, near, far, ring(near, "core", 2, 1), ring(far, "core", 2, 1)]

    table = left_map(probes.shape[1])

    def tile(rows_in, columns, dtype, start=None):
        return pl.pallas_call(
            functools.partial(tile_kernel, 256, 256, start is not None),
            out_shape=jax.ShapeDtypeStruct((rows_in.shape[0], width), dtype),
            in_specs=[VMEM] * (2 + len(columns) + (start is not None)),
            out_specs=VMEM,
            compiler_params=params(16),
            name="tile",
        )(table, rows_in, *([] if start is None else [start]), *columns)

    back = {}
    for d in (0, 3, 1, 2):
        if d == 2:
            part = tile(lines[d], columns[3:], BF16, tile(lines[d], columns[:3], F32))
        else:
            part = tile(lines[d], columns, F32 if d == 0 else BF16)
        back[d] = part if d == 0 else turn(part, sizes, 1, d)

    partial, own_rows, *other_rows = pl.pallas_call(
        functools.partial(sum_rows_kernel, n_side),
        out_shape=[
            jax.ShapeDtypeStruct((embeds.shape[1], width), BF16),
            jax.ShapeDtypeStruct((rows, width), F32),
        ]
        + [jax.ShapeDtypeStruct((rows, width), BF16)] * (n_side - 1),
        in_specs=[VMEM] * (n_side + 1),
        out_specs=[VMEM] * (n_side + 1),
        compiler_params=params(16),
        name="sum_rows",
    )(*(back[d] for d in range(n_side)), embeds_line)
    arrived = [turn(other_rows[0], sizes, 0, 1)]
    n_plane = n_side * n_side
    pieces = exchange(partial.reshape(n_plane, -1, width), PLANE)
    pieces, arrived[0] = lax.optimization_barrier((pieces, arrived[0]))
    piece = sum_spread([pieces], 1, F32)
    spread = sum_spread([piece, ring(piece, "core", 2, 1)], n_z, F32)
    spread, other_rows[1] = lax.optimization_barrier((spread, other_rows[1]))
    pieces = exchange(spread, DEPTH)
    arrived.append(turn(other_rows[1], sizes, 0, 2))
    pieces, arrived[1] = lax.optimization_barrier((pieces, arrived[1]))
    spread = sum_spread([pieces], n_plane, BF16)
    spread, other_rows[2] = lax.optimization_barrier((spread, other_rows[2]))
    pieces = exchange(spread, PLANE)
    arrived.append(turn(other_rows[2], sizes, 0, 3))
    grad_rows = pl.pallas_call(
        finish_rows_kernel,
        out_shape=jax.ShapeDtypeStruct((rows, width), F32),
        in_specs=[VMEM] * 4,
        out_specs=VMEM,
        compiler_params=params(16),
        name="finish_rows",
    )(own_rows, *arrived)
    pieces, grad_rows = lax.optimization_barrier((pieces, grad_rows))
    total_points = rows * n_plane * n_z * 2
    grad_weight = pieces.reshape(-1, width).astype(F32) * (1.0 / math.sqrt(total_points))
    return grad_rows, grad_weight


def solution(mesh):
    sizes = {"y": 4, "zh": 2, "core": 2, "zl": 4, "x": 4}
    fine = Mesh(mesh.devices.reshape(tuple(sizes[a] for a in ALL)), ALL)
    return jax.shard_map(
        functools.partial(shards, sizes),
        mesh=fine,
        in_specs=(P(ALL, None), P(), P(ALL), P(ALL, None), P(ALL, None)),
        out_specs=(P(ALL, None), P()),
        check_vma=False,
    )
```

```python
import functools
import math

import jax
import jax.numpy as jnp
import numpy as np
from jax import lax
from jax.experimental import pallas as pl
from jax.experimental.pallas import tpu as pltpu
from jax.sharding import Mesh, PartitionSpec as P

LOG2E = math.log2(math.e)
ROOT5 = math.sqrt(5.0)
ALL = ("y", "zh", "core", "zl", "x")
PLANE = ("y", "x")
DEPTH = ("zh", "zl")
F32 = jnp.float32
BF16 = jnp.bfloat16
VMEM = pl.BlockSpec(memory_space=pltpu.VMEM)


def params(mib):
    return pltpu.CompilerParams(vmem_limit_bytes=mib << 20)


def dot_nt(a, b):
    return lax.dot_general(a, b, (((1,), (1,)), ((), ())), preferred_element_type=F32)


def dot_tn(a, b):
    return lax.dot_general(a, b, (((0,), (0,)), ((), ())), preferred_element_type=F32)


def pack_kernel(embeds, weight, solve, probes, probe_solves, packed, extended, weight_in, solve_in, probes_in, probe_solves_in, sems):
    rows, width = embeds.shape[0], weight.shape[1]
    embeds_in = extended.at[:, width + 128 :]
    loads = [
        pltpu.make_async_copy(source, target, sems.at[k])
        for k, (source, target) in enumerate(
            (
                (weight, weight_in),
                (embeds, embeds_in),
                (probes, probes_in),
                (probe_solves, probe_solves_in),
                (solve, solve_in),
            )
        )
    ]
    for load in loads:
        load.start()
    for load in loads:
        load.wait()
    feats = jnp.dot(embeds_in[...], weight_in[...], preferred_element_type=F32).astype(BF16)
    wide = feats.astype(F32)
    sq = jnp.sum(wide * wide, axis=1, keepdims=True)
    sq_hi = sq.astype(BF16).astype(F32)
    sq_mid = (sq - sq_hi).astype(BF16).astype(F32)
    sq_lo = sq - sq_hi - sq_mid
    fold = math.sqrt(5.0 / 3.0 * ROOT5)
    scale = (2.0 * probes.shape[0]) ** (-0.5) * fold
    both = jnp.concatenate(
        [solve_in[...] * fold, probes_in[...] * -scale, probe_solves_in[...] * -scale, jnp.zeros((1, rows), F32)],
        axis=0,
    ).T
    hi = both.astype(BF16).astype(F32)
    lo = both - hi
    lane = lax.broadcasted_iota(jnp.int32, (rows, 32), 1)
    tail = jnp.where(lane == 0, sq_hi, jnp.where(lane == 1, sq_mid, jnp.where(lane == 2, sq_lo, 0.0)))
    tail = jnp.concatenate([hi, lo, hi, tail], axis=1).astype(BF16)
    extended[:, :width] = feats
    extended[:, width : width + 128] = tail
    packed[:, :width] = feats
    packed[:, width:] = tail


def split_kernel(count, *refs):
    line, embeds = refs[count:]
    rows, width = refs[0].shape[0], line.shape[1]
    for k, ref in enumerate(refs[:count]):
        line[k * rows : (k + 1) * rows, :] = ref[:, :width]
        embeds[k * rows : (k + 1) * rows, :] = ref[:, width:]


def left_map(count):
    source = np.zeros((32,), np.int32)
    sign = np.zeros((32,), np.float32)
    sign[0] = 1.0
    for k in range(count):
        source[1 + k], sign[1 + k] = 1 + count + k, -1.0
        source[1 + count + k], sign[1 + count + k] = 1 + k, -1.0
    table = np.zeros((128, 128), np.float32)
    for group, offset in ((0, 0), (1, 0), (2, 32)):
        for k in range(32):
            table[offset + source[k], 32 * group + k] = sign[k]
    return jnp.asarray(table, BF16)


def tile_kernel(sub, step, adds, table, rows_ref, *refs):
    *columns, out = refs
    if adds:
        begin, *columns = columns
    width = out.shape[1]
    rows = rows_ref.shape[0]
    u_rows = rows_ref[:, :width]
    fac = rows_ref[:, width:]
    twice = (u_rows.astype(F32) * -2.0).astype(BF16)
    left = jnp.dot(fac, table[...], preferred_element_type=F32).astype(BF16)
    lane = lax.broadcasted_iota(jnp.int32, (128, 128), 0)
    pick = jnp.where((lane >= 96) & (lane < 99), 1.0, 0.0).astype(BF16)
    sq_rows = jnp.dot(fac, pick, preferred_element_type=F32)[:, :1]
    lane = lax.broadcasted_iota(jnp.int32, (8, 128), 1)
    pick_cols = jnp.where((lane >= 96) & (lane < 99), 1.0, 0.0).astype(BF16)
    blocks = [slice(k, k + sub) for k in range(0, rows, sub)]
    acc = [begin[block, :] if adds else jnp.zeros((sub, width), F32) for block in blocks]
    total = [jnp.zeros((sub, 128), F32) for _ in blocks]
    work = [
        (ref, start, k)
        for ref in columns
        for start in range(0, ref.shape[0], step)
        for k in range(len(blocks))
    ]

    def products(ref, start, k):
        u_cols = ref[start : start + step, :width]
        right = ref[start : start + step, width:]
        sq_cols = dot_nt(pick_cols, right)[:1]
        return u_cols, sq_cols, dot_nt(twice[blocks[k]], u_cols), dot_nt(left[blocks[k]], right)

    ahead = products(*work[0])
    for index, (_, _, k) in enumerate(work):
        u_cols, sq_cols, cross, pair = ahead
        if index + 1 < len(work):
            ahead = products(*work[index + 1])
        d2 = jnp.maximum((sq_rows[blocks[k]] + sq_cols) + cross, 1e-30)
        dist = d2 * lax.rsqrt(d2)
        coupling = pair * ((dist + 1.0 / ROOT5) * jnp.exp2(dist * (-ROOT5 * LOG2E)))
        for j in range(0, step, 128):
            total[k] = total[k] + coupling[:, j : j + 128]
        acc[k] = acc[k] + jnp.dot(coupling.astype(BF16), u_cols, preferred_element_type=F32)
    for k, block in enumerate(blocks):
        row_total = jnp.sum(total[k], axis=1, keepdims=True)
        out[block, :] = (acc[k] - row_total * u_rows[block].astype(F32)).astype(out.dtype)


def sum_rows_kernel(count, core, *refs):
    parts, (embeds, keep, send, own, *others, weight) = refs[:count], refs[count:]
    rows, half = own.shape[0], keep.shape[0]
    total = parts[0][...]
    for ref in parts[1:]:
        total = total + ref[...].astype(F32)
    hi = total.astype(BF16)
    lo = (total - hi.astype(F32)).astype(BF16)
    own[...] = total[:rows]
    for k, ref in enumerate(others):
        ref[...] = hi[(k + 1) * rows : (k + 2) * rows]
    weight[...] = dot_tn(embeds[...], hi) + dot_tn(embeds[...], lo)
    keep[...] = weight[pl.ds(pl.multiple_of(core[0] * half, half), half), :]
    send[...] = weight[pl.ds(pl.multiple_of((1 - core[0]) * half, half), half), :]


def add_halves_kernel(a, b, out):
    out[...] = (a[...] + b[...]).astype(out.dtype)


def join_halves_kernel(scale, core, a, b, out):
    half = a.shape[0]
    out[pl.ds(pl.multiple_of(core[0] * half, half), half), :] = a[...].astype(F32) * scale
    out[pl.ds(pl.multiple_of((1 - core[0]) * half, half), half), :] = b[...].astype(F32) * scale


def finish_rows_kernel(own, b, c, d, grad_rows):
    grad_rows[...] = (own[...] + b[...].astype(F32)) + (c[...].astype(F32) + d[...].astype(F32))


def sum_spread_kernel(parts, out):
    total = parts[0].astype(F32)
    for k in range(1, parts.shape[0]):
        total = total + parts[k].astype(F32)
    low = total.astype(out.dtype)
    for k in range(out.shape[0]):
        out[k] = low


def sum_spread(parts, copies, dtype):
    return pl.pallas_call(
        sum_spread_kernel,
        out_shape=jax.ShapeDtypeStruct((copies,) + parts.shape[1:], dtype),
        in_specs=[VMEM],
        out_specs=VMEM,
        compiler_params=params(16),
        name="sum_spread",
    )(parts)


def ring(array, axis, size, shift):
    return lax.ppermute(array, axis, [(i, (i + shift) % size) for i in range(size)])


def move(array, sizes, where):
    dims = [sizes[a] for a in ALL]
    perm = []
    for source in range(math.prod(dims)):
        place = dict(zip(ALL, (int(i) for i in np.unravel_index(source, dims))))
        for axis, shift in where(place["core"]).items():
            if axis == "z":
                z = (place["zh"] * sizes["zl"] + place["zl"] + shift) % (sizes["zh"] * sizes["zl"])
                place["zh"], place["zl"] = divmod(z, sizes["zl"])
            else:
                place[axis] = (place[axis] + shift) % sizes[axis]
        perm.append((source, int(np.ravel_multi_index([place[a] for a in ALL], dims))))
    return lax.ppermute(array, ALL, perm)


def turn(array, sizes, stage, shift):
    return move(array, sizes, lambda core: {"y" if (core + stage) % 2 == 0 else "x": shift})


def exchange(array, axes):
    return lax.all_to_all(array, axes, split_axis=0, concat_axis=0, tiled=True)


def shards(sizes, embeds, weight, solve, probes, probe_solves):
    rows, width = embeds.shape[0], weight.shape[1]
    n_side, n_z = sizes["x"], sizes["zh"] * sizes["zl"]
    pack, extended = pl.pallas_call(
        pack_kernel,
        out_shape=[
            jax.ShapeDtypeStruct((rows, width + 128), BF16),
            jax.ShapeDtypeStruct((rows, width + 128 + embeds.shape[1]), BF16),
        ],
        in_specs=[pl.BlockSpec(memory_space=pltpu.HBM)] * 5,
        out_specs=[VMEM] * 2,
        scratch_shapes=[
            pltpu.VMEM(weight.shape, BF16),
            pltpu.VMEM((1, rows), F32),
            pltpu.VMEM(probes.shape[::-1], F32),
            pltpu.VMEM(probes.shape[::-1], F32),
            pltpu.SemaphoreType.DMA((5,)),
        ],
        compiler_params=params(48),
        name="pack",
    )(*(pltpu.with_memory_space_constraint(a, pltpu.HBM) for a in (embeds, weight, solve[None, :], probes.T, probe_solves.T)))

    blocks = [extended] + [turn(extended, sizes, 0, -d) for d in range(1, n_side)]
    line, embeds_line = pl.pallas_call(
        functools.partial(split_kernel, n_side),
        out_shape=[
            jax.ShapeDtypeStruct((n_side * rows, width + 128), BF16),
            jax.ShapeDtypeStruct((n_side * rows, embeds.shape[1]), BF16),
        ],
        in_specs=[VMEM] * n_side,
        out_specs=[VMEM] * 2,
        compiler_params=params(8),
        name="split",
    )(*blocks)
    pair = jnp.concatenate([pack, ring(pack, DEPTH, n_z, n_z // 2)], axis=0)
    pair, line = lax.optimization_barrier((pair, line))
    four = jnp.concatenate([pair, ring(pair, "core", 2, 1)], axis=0)
    four, line = lax.optimization_barrier((four, line))
    far = move(pair, sizes, lambda core: {"z": 2 - 4 * core})
    lines = [line] + [turn(line, sizes, 1, -d) for d in range(1, n_side)]
    near = move(four, sizes, lambda core: {"z": 1 - 2 * core})
    near, far, lines = lax.optimization_barrier((near, far, lines))
    columns = [four, near, far, ring(near, "core", 2, 1), ring(far, "core", 2, 1)]

    table = left_map(probes.shape[1])

    def tile(rows_in, columns, dtype, start=None):
        return pl.pallas_call(
            functools.partial(tile_kernel, 256, 256, start is not None),
            out_shape=jax.ShapeDtypeStruct((rows_in.shape[0], width), dtype),
            in_specs=[VMEM] * (2 + len(columns) + (start is not None)),
            out_specs=VMEM,
            compiler_params=params(16),
            name="tile",
        )(table, rows_in, *([] if start is None else [start]), *columns)

    back = {}
    for d in (0, 3, 1, 2):
        if d == 2:
            part = tile(lines[d], columns[3:], BF16, tile(lines[d], columns[:3], F32))
        else:
            part = tile(lines[d], columns, F32 if d == 0 else BF16)
        back[d] = part if d == 0 else turn(part, sizes, 1, d)

    core = lax.axis_index("core")[None]
    scalar = pl.BlockSpec(memory_space=pltpu.SMEM)
    half = embeds.shape[1] // 2
    keep, send, own_rows, *other_rows = pl.pallas_call(
        functools.partial(sum_rows_kernel, n_side),
        out_shape=[jax.ShapeDtypeStruct((half, width), F32)] * 2
        + [jax.ShapeDtypeStruct((rows, width), F32)]
        + [jax.ShapeDtypeStruct((rows, width), BF16)] * (n_side - 1),
        in_specs=[scalar] + [VMEM] * (n_side + 1),
        out_specs=[VMEM] * (n_side + 2),
        scratch_shapes=[pltpu.VMEM((2 * half, width), F32)],
        compiler_params=params(16),
        name="sum_rows",
    )(core, *(back[d] for d in range(n_side)), embeds_line)
    partial = pl.pallas_call(
        add_halves_kernel,
        out_shape=jax.ShapeDtypeStruct((half, width), BF16),
        in_specs=[VMEM] * 2,
        out_specs=VMEM,
        compiler_params=params(16),
        name="add_halves",
    )(keep, ring(send, "core", 2, 1))
    partial, other_rows[0] = lax.optimization_barrier((partial, other_rows[0]))

    n_plane = n_side * n_side
    pieces = exchange(partial.reshape(n_plane, -1, width), PLANE)
    arrived = [turn(other_rows[0], sizes, 0, 1)]
    pieces, arrived[0] = lax.optimization_barrier((pieces, arrived[0]))
    spread = sum_spread(pieces, n_z, F32)
    spread, other_rows[1] = lax.optimization_barrier((spread, other_rows[1]))
    pieces = exchange(spread, DEPTH)
    arrived.append(turn(other_rows[1], sizes, 0, 2))
    pieces, arrived[1] = lax.optimization_barrier((pieces, arrived[1]))
    spread = sum_spread(pieces, n_plane, BF16)
    spread, other_rows[2] = lax.optimization_barrier((spread, other_rows[2]))
    pieces = exchange(spread, PLANE)
    arrived.append(turn(other_rows[2], sizes, 0, 3))
    grad_rows = pl.pallas_call(
        finish_rows_kernel,
        out_shape=jax.ShapeDtypeStruct((rows, width), F32),
        in_specs=[VMEM] * 4,
        out_specs=VMEM,
        compiler_params=params(16),
        name="finish_rows",
    )(own_rows, *arrived)
    pieces, grad_rows = lax.optimization_barrier((pieces, grad_rows))
    pieces = pieces.reshape(half, width)
    grad_weight = pl.pallas_call(
        functools.partial(join_halves_kernel, 1.0 / math.sqrt(rows * n_plane * n_z * 2)),
        out_shape=jax.ShapeDtypeStruct((2 * half, width), F32),
        in_specs=[scalar] + [VMEM] * 2,
        out_specs=VMEM,
        compiler_params=params(16),
        name="join_halves",
    )(core, pieces, ring(pieces, "core", 2, 1))
    return grad_rows, grad_weight


def solution(mesh):
    sizes = {"y": 4, "zh": 2, "core": 2, "zl": 4, "x": 4}
    fine = Mesh(mesh.devices.reshape(tuple(sizes[a] for a in ALL)), ALL)
    return jax.shard_map(
        functools.partial(shards, sizes),
        mesh=fine,
        in_specs=(P(ALL, None), P(), P(ALL), P(ALL, None), P(ALL, None)),
        out_specs=(P(ALL, None), P()),
        check_vma=False,
    )
```

```python
import functools
import math

import jax
import jax.numpy as jnp
import numpy as np
from jax import lax
from jax.experimental import pallas as pl
from jax.experimental.pallas import tpu as pltpu
from jax.sharding import Mesh, PartitionSpec as P

LOG2E = math.log2(math.e)
ROOT5 = math.sqrt(5.0)
ALL = ("y", "zh", "core", "zl", "x")
PLANE = ("y", "core", "x")
DEPTH = ("zh", "zl")
F32 = jnp.float32
BF16 = jnp.bfloat16
VMEM = pl.BlockSpec(memory_space=pltpu.VMEM)


def params(mib):
    return pltpu.CompilerParams(vmem_limit_bytes=mib << 20)


def dot_nt(a, b):
    return lax.dot_general(a, b, (((1,), (1,)), ((), ())), preferred_element_type=F32)


def dot_tn(a, b):
    return lax.dot_general(a, b, (((0,), (0,)), ((), ())), preferred_element_type=F32)


def pack_kernel(embeds, weight, solve, probes, probe_solves, packed, extended, weight_in, solve_in, probes_in, probe_solves_in, sems):
    rows, width = embeds.shape[0], weight.shape[1]
    embeds_in = extended.at[:, width + 128 :]
    loads = [
        pltpu.make_async_copy(source, target, sems.at[k])
        for k, (source, target) in enumerate(
            (
                (weight, weight_in),
                (embeds, embeds_in),
                (probes, probes_in),
                (probe_solves, probe_solves_in),
                (solve, solve_in),
            )
        )
    ]
    for load in loads:
        load.start()
    for load in loads:
        load.wait()
    feats = jnp.dot(embeds_in[...], weight_in[...], preferred_element_type=F32).astype(BF16)
    wide = feats.astype(F32)
    sq = jnp.sum(wide * wide, axis=1, keepdims=True)
    sq_hi = sq.astype(BF16).astype(F32)
    sq_mid = (sq - sq_hi).astype(BF16).astype(F32)
    sq_lo = sq - sq_hi - sq_mid
    fold = math.sqrt(5.0 / 3.0 * ROOT5)
    scale = (2.0 * probes.shape[0]) ** (-0.5) * fold
    both = jnp.concatenate(
        [solve_in[...] * fold, probes_in[...] * -scale, probe_solves_in[...] * -scale, jnp.zeros((1, rows), F32)],
        axis=0,
    ).T
    hi = both.astype(BF16).astype(F32)
    lo = both - hi
    lane = lax.broadcasted_iota(jnp.int32, (rows, 32), 1)
    tail = jnp.where(lane == 0, sq_hi, jnp.where(lane == 1, sq_mid, jnp.where(lane == 2, sq_lo, 0.0)))
    tail = jnp.concatenate([hi, lo, hi, tail], axis=1).astype(BF16)
    extended[:, :width] = feats
    extended[:, width : width + 128] = tail
    packed[:, :width] = feats
    packed[:, width:] = tail


def split_kernel(own, other, pair, embeds):
    rows, width = own.shape[0], pair.shape[1]
    for k, ref in enumerate((own, other)):
        pair[k * rows : (k + 1) * rows, :] = ref[:, :width]
        embeds[k * rows : (k + 1) * rows, :] = ref[:, width:]


def left_map(count):
    source = np.zeros((32,), np.int32)
    sign = np.zeros((32,), np.float32)
    sign[0] = 1.0
    for k in range(count):
        source[1 + k], sign[1 + k] = 1 + count + k, -1.0
        source[1 + count + k], sign[1 + count + k] = 1 + k, -1.0
    table = np.zeros((128, 128), np.float32)
    for group, offset in ((0, 0), (1, 0), (2, 32)):
        for k in range(32):
            table[offset + source[k], 32 * group + k] = sign[k]
    return jnp.asarray(table, BF16)


def tile_kernel(sub, step, adds, table, rows_ref, *refs):
    *columns, out = refs
    if adds:
        begin, *columns = columns
    width = out.shape[1]
    rows = rows_ref.shape[0]
    u_rows = rows_ref[:, :width]
    fac = rows_ref[:, width:]
    twice = (u_rows.astype(F32) * -2.0).astype(BF16)
    left = jnp.dot(fac, table[...], preferred_element_type=F32).astype(BF16)
    lane = lax.broadcasted_iota(jnp.int32, (128, 128), 0)
    pick = jnp.where((lane >= 96) & (lane < 99), 1.0, 0.0).astype(BF16)
    sq_rows = jnp.dot(fac, pick, preferred_element_type=F32)[:, :1]
    lane = lax.broadcasted_iota(jnp.int32, (8, 128), 1)
    pick_cols = jnp.where((lane >= 96) & (lane < 99), 1.0, 0.0).astype(BF16)
    blocks = [slice(k, k + sub) for k in range(0, rows, sub)]
    acc = [begin[block, :] if adds else jnp.zeros((sub, width), F32) for block in blocks]
    total = [jnp.zeros((sub, 128), F32) for _ in blocks]
    work = [
        (ref, start, k)
        for ref in columns
        for start in range(0, ref.shape[0], step)
        for k in range(len(blocks))
    ]

    def products(ref, start, k):
        u_cols = ref[start : start + step, :width]
        right = ref[start : start + step, width:]
        sq_cols = dot_nt(pick_cols, right)[:1]
        return u_cols, sq_cols, dot_nt(twice[blocks[k]], u_cols), dot_nt(left[blocks[k]], right)

    ahead = products(*work[0])
    for index, (_, _, k) in enumerate(work):
        u_cols, sq_cols, cross, pair = ahead
        if index + 1 < len(work):
            ahead = products(*work[index + 1])
        d2 = jnp.maximum((sq_rows[blocks[k]] + sq_cols) + cross, 1e-30)
        dist = d2 * lax.rsqrt(d2)
        coupling = pair * ((dist + 1.0 / ROOT5) * jnp.exp2(dist * (-ROOT5 * LOG2E)))
        for j in range(0, step, 128):
            total[k] = total[k] + coupling[:, j : j + 128]
        acc[k] = acc[k] + jnp.dot(coupling.astype(BF16), u_cols, preferred_element_type=F32)
    for k, block in enumerate(blocks):
        row_total = jnp.sum(total[k], axis=1, keepdims=True)
        out[block, :] = (acc[k] - row_total * u_rows[block].astype(F32)).astype(out.dtype)


def sum_rows_kernel(a, b, c, d, embeds, partial, own, other):
    rows = own.shape[0]
    total = (a[...] + b[...].astype(F32)) + (c[...].astype(F32) + d[...].astype(F32))
    hi = total.astype(BF16)
    lo = (total - hi.astype(F32)).astype(BF16)
    own[...] = total[:rows]
    other[...] = hi[rows:]
    partial[...] = (dot_tn(embeds[...], hi) + dot_tn(embeds[...], lo)).astype(BF16)


def finish_rows_kernel(own, arrived, grad_rows):
    grad_rows[...] = own[...] + arrived[...].astype(F32)


def sum_spread_kernel(parts, out):
    total = parts[0].astype(F32)
    for k in range(1, parts.shape[0]):
        total = total + parts[k].astype(F32)
    low = total.astype(out.dtype)
    for k in range(out.shape[0]):
        out[k] = low


def sum_spread(parts, copies, dtype):
    return pl.pallas_call(
        sum_spread_kernel,
        out_shape=jax.ShapeDtypeStruct((copies,) + parts.shape[1:], dtype),
        in_specs=[VMEM],
        out_specs=VMEM,
        compiler_params=params(16),
        name="sum_spread",
    )(parts)


def ring(array, axis, size, shift):
    return lax.ppermute(array, axis, [(i, (i + shift) % size) for i in range(size)])


def move(array, sizes, where):
    dims = [sizes[a] for a in ALL]
    perm = []
    for source in range(math.prod(dims)):
        place = dict(zip(ALL, (int(i) for i in np.unravel_index(source, dims))))
        for axis, shift in where(place["core"]).items():
            if axis == "z":
                z = (place["zh"] * sizes["zl"] + place["zl"] + shift) % (sizes["zh"] * sizes["zl"])
                place["zh"], place["zl"] = divmod(z, sizes["zl"])
            else:
                place[axis] = (place[axis] + shift) % sizes[axis]
        perm.append((source, int(np.ravel_multi_index([place[a] for a in ALL], dims))))
    return lax.ppermute(array, ALL, perm)


def turn(array, sizes, stage, shift):
    return move(array, sizes, lambda core: {"y" if (core + stage) % 2 == 0 else "x": shift})


def exchange(array, axes):
    return lax.all_to_all(array, axes, split_axis=0, concat_axis=0, tiled=True)


def shards(sizes, embeds, weight, solve, probes, probe_solves):
    rows, width = embeds.shape[0], weight.shape[1]
    n_side, n_z = sizes["x"], sizes["zh"] * sizes["zl"]
    pack, extended = pl.pallas_call(
        pack_kernel,
        out_shape=[
            jax.ShapeDtypeStruct((rows, width + 128), BF16),
            jax.ShapeDtypeStruct((rows, width + 128 + embeds.shape[1]), BF16),
        ],
        in_specs=[pl.BlockSpec(memory_space=pltpu.HBM)] * 5,
        out_specs=[VMEM] * 2,
        scratch_shapes=[
            pltpu.VMEM(weight.shape, BF16),
            pltpu.VMEM((1, rows), F32),
            pltpu.VMEM(probes.shape[::-1], F32),
            pltpu.VMEM(probes.shape[::-1], F32),
            pltpu.SemaphoreType.DMA((5,)),
        ],
        compiler_params=params(48),
        name="pack",
    )(*(pltpu.with_memory_space_constraint(a, pltpu.HBM) for a in (embeds, weight, solve[None, :], probes.T, probe_solves.T)))

    line = jnp.concatenate([pack] + [turn(pack, sizes, 0, d) for d in range(1, n_side)], axis=0)
    pair, embeds_pair = pl.pallas_call(
        split_kernel,
        out_shape=[
            jax.ShapeDtypeStruct((2 * rows, width + 128), BF16),
            jax.ShapeDtypeStruct((2 * rows, embeds.shape[1]), BF16),
        ],
        in_specs=[VMEM] * 2,
        out_specs=[VMEM] * 2,
        compiler_params=params(8),
        name="split",
    )(extended, ring(extended, DEPTH, n_z, n_z // 2))
    line, pair = lax.optimization_barrier((line, pair))

    def along(array, step):
        return move(array, sizes, lambda core: {"z": step if abs(step) == 1 else step * (1 - 2 * core)})

    steps = (1, -1, 2)
    columns = [line] + [turn(line, sizes, 1, d) for d in range(1, n_side)]
    lines = [along(pair, step) for step in steps]
    columns, lines = lax.optimization_barrier((columns, lines))
    swapped = [ring(part, "core", 2, 1) for part in columns]

    table = left_map(probes.shape[1])

    def tile(rows_in, columns, dtype, start=None):
        return pl.pallas_call(
            functools.partial(tile_kernel, 256, 256, start is not None),
            out_shape=jax.ShapeDtypeStruct((rows_in.shape[0], width), dtype),
            in_specs=[VMEM] * (2 + len(columns) + (start is not None)),
            out_specs=VMEM,
            compiler_params=params(16),
            name="tile",
        )(table, rows_in, *([] if start is None else [start]), *columns)

    own = tile(pair, columns, F32)
    first = tile(lines[0], columns, F32)
    swapped, own, first = lax.optimization_barrier((swapped, own, first))
    own = tile(pair, swapped, F32, own)
    back = [None] * len(steps)
    for k in (1, 2):
        back[k] = along(tile(lines[k], columns + swapped, BF16), -steps[k])
    back[0] = along(tile(lines[0], swapped, BF16, first), -steps[0])

    partial, own_rows, other_rows = pl.pallas_call(
        sum_rows_kernel,
        out_shape=[
            jax.ShapeDtypeStruct((embeds.shape[1], width), BF16),
            jax.ShapeDtypeStruct((rows, width), F32),
            jax.ShapeDtypeStruct((rows, width), BF16),
        ],
        in_specs=[VMEM] * 5,
        out_specs=[VMEM] * 3,
        compiler_params=params(16),
        name="sum_rows",
    )(own, *back, embeds_pair)

    n_plane = n_side * n_side * 2
    pieces = exchange(partial.reshape(n_plane, -1, width), PLANE)
    arrived = ring(other_rows, DEPTH, n_z, n_z // 2)
    grad_rows = pl.pallas_call(
        finish_rows_kernel,
        out_shape=jax.ShapeDtypeStruct((rows, width), F32),
        in_specs=[VMEM] * 2,
        out_specs=VMEM,
        compiler_params=params(16),
        name="finish_rows",
    )(own_rows, arrived)
    pieces, grad_rows = lax.optimization_barrier((pieces, grad_rows))
    pieces = exchange(sum_spread(pieces, n_z, F32), DEPTH)
    pieces = exchange(sum_spread(pieces, n_plane, BF16), PLANE)
    total_points = rows * n_plane * n_z
    grad_weight = pieces.reshape(-1, width).astype(F32) * (1.0 / math.sqrt(total_points))
    return grad_rows, grad_weight


def solution(mesh):
    sizes = {"y": 4, "zh": 2, "core": 2, "zl": 4, "x": 4}
    fine = Mesh(mesh.devices.reshape(tuple(sizes[a] for a in ALL)), ALL)
    return jax.shard_map(
        functools.partial(shards, sizes),
        mesh=fine,
        in_specs=(P(ALL, None), P(), P(ALL), P(ALL, None), P(ALL, None)),
        out_specs=(P(ALL, None), P()),
        check_vma=False,
    )
```

```python
import functools
import math

import jax
import jax.numpy as jnp
import numpy as np
from jax import lax
from jax.experimental import pallas as pl
from jax.experimental.pallas import tpu as pltpu
from jax.sharding import Mesh, PartitionSpec as P

LOG2E = math.log2(math.e)
ROOT5 = math.sqrt(5.0)
ALL = ("y", "zh", "core", "zl", "x")
PLANE = ("y", "x")
STACK = ("zh", "core", "zl")
DEPTH = ("zh", "zl")
F32 = jnp.float32
BF16 = jnp.bfloat16
VMEM = pl.BlockSpec(memory_space=pltpu.VMEM)


def params(mib):
    return pltpu.CompilerParams(vmem_limit_bytes=mib << 20)


def dot_nt(a, b):
    return lax.dot_general(a, b, (((1,), (1,)), ((), ())), preferred_element_type=F32)


def dot_tn(a, b):
    return lax.dot_general(a, b, (((0,), (0,)), ((), ())), preferred_element_type=F32)


def pack_kernel(embeds, weight, solve, probes, probe_solves, packed, extended, weight_in, solve_in, probes_in, probe_solves_in, sems):
    rows, width = embeds.shape[0], weight.shape[1]
    embeds_in = extended.at[:, 128:]
    loads = [
        pltpu.make_async_copy(source, target, sems.at[k])
        for k, (source, target) in enumerate(
            (
                (weight, weight_in),
                (embeds, embeds_in),
                (probes, probes_in),
                (probe_solves, probe_solves_in),
                (solve, solve_in),
            )
        )
    ]
    for load in loads:
        load.start()
    for load in loads:
        load.wait()
    feats = jnp.dot(embeds_in[...], weight_in[...], preferred_element_type=F32).astype(BF16)
    wide = feats.astype(F32)
    sq = jnp.sum(wide * wide, axis=1, keepdims=True)
    sq_hi = sq.astype(BF16).astype(F32)
    sq_mid = (sq - sq_hi).astype(BF16).astype(F32)
    sq_lo = sq - sq_hi - sq_mid
    fold = math.sqrt(5.0 / 3.0 * ROOT5)
    scale = (2.0 * probes.shape[0]) ** (-0.5) * fold
    both = jnp.concatenate(
        [solve_in[...] * fold, probes_in[...] * -scale, probe_solves_in[...] * -scale, jnp.zeros((1, rows), F32)],
        axis=0,
    ).T
    hi = both.astype(BF16).astype(F32)
    lo = both - hi
    lane = lax.broadcasted_iota(jnp.int32, (rows, 32), 1)
    tail = jnp.where(lane == 0, sq_hi, jnp.where(lane == 1, sq_mid, jnp.where(lane == 2, sq_lo, 0.0)))
    tail = jnp.concatenate([hi, lo, hi, tail], axis=1).astype(BF16)
    extended[:, :128] = tail
    packed[:, :width] = feats
    packed[:, width:] = tail


def split_kernel(count, weight, *refs):
    line, embeds = refs[count:]
    rows, width = refs[0].shape[0], weight.shape[1]
    for k, ref in enumerate(refs[:count]):
        block = slice(k * rows, (k + 1) * rows)
        own = ref[:, 128:]
        line[block, :width] = jnp.dot(own, weight[...], preferred_element_type=F32).astype(BF16)
        line[block, width:] = ref[:, :128]
        embeds[block, :] = own


def left_map(count):
    source = np.zeros((32,), np.int32)
    sign = np.zeros((32,), np.float32)
    sign[0] = 1.0
    for k in range(count):
        source[1 + k], sign[1 + k] = 1 + count + k, -1.0
        source[1 + count + k], sign[1 + count + k] = 1 + k, -1.0
    table = np.zeros((128, 128), np.float32)
    for group, offset in ((0, 0), (1, 0), (2, 32)):
        for k in range(32):
            table[offset + source[k], 32 * group + k] = sign[k]
    return jnp.asarray(table, BF16)


def tile_kernel(sub, step, adds, table, rows_ref, *refs):
    *columns, out = refs
    if adds:
        begin, *columns = columns
    width = out.shape[1]
    rows = rows_ref.shape[0]
    u_rows = rows_ref[:, :width]
    fac = rows_ref[:, width:]
    twice = (u_rows.astype(F32) * -2.0).astype(BF16)
    left = jnp.dot(fac, table[...], preferred_element_type=F32).astype(BF16)
    lane = lax.broadcasted_iota(jnp.int32, (128, 128), 0)
    pick = jnp.where((lane >= 96) & (lane < 99), 1.0, 0.0).astype(BF16)
    sq_rows = jnp.dot(fac, pick, preferred_element_type=F32)[:, :1]
    lane = lax.broadcasted_iota(jnp.int32, (8, 128), 1)
    pick_cols = jnp.where((lane >= 96) & (lane < 99), 1.0, 0.0).astype(BF16)
    blocks = [slice(k, k + sub) for k in range(0, rows, sub)]
    acc = [begin[block, :] if adds else jnp.zeros((sub, width), F32) for block in blocks]
    total = [jnp.zeros((sub, 128), F32) for _ in blocks]
    work = [
        (ref, start, k)
        for ref in columns
        for start in range(0, ref.shape[0], step)
        for k in range(len(blocks))
    ]

    def products(ref, start, k):
        u_cols = ref[start : start + step, :width]
        right = ref[start : start + step, width:]
        sq_cols = dot_nt(pick_cols, right)[:1]
        return u_cols, sq_cols, dot_nt(twice[blocks[k]], u_cols), dot_nt(left[blocks[k]], right)

    ahead = products(*work[0])
    for index, (_, _, k) in enumerate(work):
        u_cols, sq_cols, cross, pair = ahead
        if index + 1 < len(work):
            ahead = products(*work[index + 1])
        d2 = jnp.maximum((sq_rows[blocks[k]] + sq_cols) + cross, 1e-30)
        dist = d2 * lax.rsqrt(d2)
        coupling = pair * ((dist + 1.0 / ROOT5) * jnp.exp2(dist * (-ROOT5 * LOG2E)))
        for j in range(0, step, 128):
            total[k] = total[k] + coupling[:, j : j + 128]
        acc[k] = acc[k] + jnp.dot(coupling.astype(BF16), u_cols, preferred_element_type=F32)
    for k, block in enumerate(blocks):
        row_total = jnp.sum(total[k], axis=1, keepdims=True)
        out[block, :] = (acc[k] - row_total * u_rows[block].astype(F32)).astype(out.dtype)


def sum_rows_kernel(count, *refs):
    parts, (embeds, partial, own, *others) = refs[:count], refs[count:]
    rows = own.shape[0]
    total = parts[0][...]
    for ref in parts[1:]:
        total = total + ref[...].astype(F32)
    hi = total.astype(BF16)
    lo = (total - hi.astype(F32)).astype(BF16)
    own[...] = total[:rows]
    for k, ref in enumerate(others):
        ref[...] = hi[(k + 1) * rows : (k + 2) * rows]
    partial[...] = (dot_tn(embeds[...], hi) + dot_tn(embeds[...], lo)).astype(BF16)


def finish_rows_kernel(own, b, c, d, grad_rows):
    grad_rows[...] = (own[...] + b[...].astype(F32)) + (c[...].astype(F32) + d[...].astype(F32))


def sum_spread_kernel(*refs):
    *parts, out = refs
    total = None
    for ref in parts:
        for k in range(ref.shape[0]):
            term = ref[k].astype(F32)
            total = term if total is None else total + term
    low = total.astype(out.dtype)
    for k in range(out.shape[0]):
        out[k] = low


def sum_spread(parts, copies, dtype):
    return pl.pallas_call(
        sum_spread_kernel,
        out_shape=jax.ShapeDtypeStruct((copies,) + parts[0].shape[1:], dtype),
        in_specs=[VMEM] * len(parts),
        out_specs=VMEM,
        compiler_params=params(16),
        name="sum_spread",
    )(*parts)


def ring(array, axis, size, shift):
    return lax.ppermute(array, axis, [(i, (i + shift) % size) for i in range(size)])


def move(array, sizes, where):
    dims = [sizes[a] for a in ALL]
    perm = []
    for source in range(math.prod(dims)):
        place = dict(zip(ALL, (int(i) for i in np.unravel_index(source, dims))))
        for axis, shift in where(place["core"]).items():
            if axis == "z":
                z = (place["zh"] * sizes["zl"] + place["zl"] + shift) % (sizes["zh"] * sizes["zl"])
                place["zh"], place["zl"] = divmod(z, sizes["zl"])
            else:
                place[axis] = (place[axis] + shift) % sizes[axis]
        perm.append((source, int(np.ravel_multi_index([place[a] for a in ALL], dims))))
    return lax.ppermute(array, ALL, perm)


def turn(array, sizes, stage, shift):
    return move(array, sizes, lambda core: {"y" if (core + stage) % 2 == 0 else "x": shift})


def exchange(array, axes):
    return lax.all_to_all(array, axes, split_axis=0, concat_axis=0, tiled=True)


def shards(sizes, embeds, weight, solve, probes, probe_solves):
    rows, width = embeds.shape[0], weight.shape[1]
    n_side, n_z = sizes["x"], sizes["zh"] * sizes["zl"]
    pack, extended = pl.pallas_call(
        pack_kernel,
        out_shape=[
            jax.ShapeDtypeStruct((rows, width + 128), BF16),
            jax.ShapeDtypeStruct((rows, 128 + embeds.shape[1]), BF16),
        ],
        in_specs=[pl.BlockSpec(memory_space=pltpu.HBM)] * 5,
        out_specs=[VMEM] * 2,
        scratch_shapes=[
            pltpu.VMEM(weight.shape, BF16),
            pltpu.VMEM((1, rows), F32),
            pltpu.VMEM(probes.shape[::-1], F32),
            pltpu.VMEM(probes.shape[::-1], F32),
            pltpu.SemaphoreType.DMA((5,)),
        ],
        compiler_params=params(48),
        name="pack",
    )(*(pltpu.with_memory_space_constraint(a, pltpu.HBM) for a in (embeds, weight, solve[None, :], probes.T, probe_solves.T)))

    blocks = [extended] + [turn(extended, sizes, 0, -d) for d in range(1, n_side)]
    line, embeds_line = pl.pallas_call(
        functools.partial(split_kernel, n_side),
        out_shape=[
            jax.ShapeDtypeStruct((n_side * rows, width + 128), BF16),
            jax.ShapeDtypeStruct((n_side * rows, embeds.shape[1]), BF16),
        ],
        in_specs=[VMEM] * (n_side + 1),
        out_specs=[VMEM] * 2,
        compiler_params=params(8),
        name="split",
    )(weight, *blocks)
    pair = jnp.concatenate([pack, ring(pack, DEPTH, n_z, n_z // 2)], axis=0)
    pair, line = lax.optimization_barrier((pair, line))
    four = jnp.concatenate([pair, ring(pair, "core", 2, 1)], axis=0)
    near = move(four, sizes, lambda core: {"z": 1 - 2 * core})
    far = move(pair, sizes, lambda core: {"z": 2 - 4 * core})
    lines = [line] + [turn(line, sizes, 1, -d) for d in range(1, n_side)]
    table = left_map(probes.shape[1])

    def tile(rows_in, columns, dtype, start=None):
        return pl.pallas_call(
            functools.partial(tile_kernel, 256, 256, start is not None),
            out_shape=jax.ShapeDtypeStruct((rows_in.shape[0], width), dtype),
            in_specs=[VMEM] * (2 + len(columns) + (start is not None)),
            out_specs=VMEM,
            compiler_params=params(16),
            name="tile",
        )(table, rows_in, *([] if start is None else [start]), *columns)

    begin = tile(line, [four], F32)
    near, far, lines, begin = lax.optimization_barrier((near, far, lines, begin))
    columns = [four, near, far, ring(near, "core", 2, 1), ring(far, "core", 2, 1)]

    back = {}
    for d in (0, 3, 1, 2):
        if d == 2:
            part = tile(lines[d], columns[3:], BF16, tile(lines[d], columns[:3], F32))
        elif d == 0:
            part = tile(line, columns[1:], F32, begin)
        else:
            part = tile(lines[d], columns, BF16)
        back[d] = part if d == 0 else turn(part, sizes, 1, d)

    partial, own_rows, *other_rows = pl.pallas_call(
        functools.partial(sum_rows_kernel, n_side),
        out_shape=[
            jax.ShapeDtypeStruct((embeds.shape[1], width), BF16),
            jax.ShapeDtypeStruct((rows, width), F32),
        ]
        + [jax.ShapeDtypeStruct((rows, width), BF16)] * (n_side - 1),
        in_specs=[VMEM] * (n_side + 1),
        out_specs=[VMEM] * (n_side + 1),
        compiler_params=params(16),
        name="sum_rows",
    )(*(back[d] for d in range(n_side)), embeds_line)
    arrived = [turn(other_rows[0], sizes, 0, 1)]
    n_plane = n_side * n_side
    pieces = exchange(partial.reshape(n_plane, -1, width), PLANE)
    pieces, arrived[0] = lax.optimization_barrier((pieces, arrived[0]))
    spread = sum_spread([pieces], n_z * 2, BF16)
    spread, other_rows[1] = lax.optimization_barrier((spread, other_rows[1]))
    pieces = exchange(spread, STACK)
    arrived.append(turn(other_rows[1], sizes, 0, 2))
    pieces, arrived[1] = lax.optimization_barrier((pieces, arrived[1]))
    spread = sum_spread([pieces], n_plane, BF16)
    spread, other_rows[2] = lax.optimization_barrier((spread, other_rows[2]))
    pieces = exchange(spread, PLANE)
    arrived.append(turn(other_rows[2], sizes, 0, 3))
    grad_rows = pl.pallas_call(
        finish_rows_kernel,
        out_shape=jax.ShapeDtypeStruct((rows, width), F32),
        in_specs=[VMEM] * 4,
        out_specs=VMEM,
        compiler_params=params(16),
        name="finish_rows",
    )(own_rows, *arrived)
    pieces, grad_rows = lax.optimization_barrier((pieces, grad_rows))
    total_points = rows * n_plane * n_z * 2
    grad_weight = pieces.reshape(-1, width).astype(F32) * (1.0 / math.sqrt(total_points))
    return grad_rows, grad_weight


def solution(mesh):
    sizes = {"y": 4, "zh": 2, "core": 2, "zl": 4, "x": 4}
    fine = Mesh(mesh.devices.reshape(tuple(sizes[a] for a in ALL)), ALL)
    return jax.shard_map(
        functools.partial(shards, sizes),
        mesh=fine,
        in_specs=(P(ALL, None), P(), P(ALL), P(ALL, None), P(ALL, None)),
        out_specs=(P(ALL, None), P()),
        check_vma=False,
    )
```

```python
import functools
import math

import jax
import jax.numpy as jnp
import numpy as np
from jax import lax
from jax.experimental import pallas as pl
from jax.experimental.pallas import tpu as pltpu
from jax.sharding import Mesh, PartitionSpec as P

LOG2E = math.log2(math.e)
ROOT5 = math.sqrt(5.0)
ALL = ("y", "zh", "core", "zl", "x")
PLANE = ("y", "x")
STACK = ("zh", "core", "zl")
DEPTH = ("zh", "zl")
F32 = jnp.float32
BF16 = jnp.bfloat16
VMEM = pl.BlockSpec(memory_space=pltpu.VMEM)


def params(mib):
    return pltpu.CompilerParams(vmem_limit_bytes=mib << 20)


def dot_nt(a, b):
    return lax.dot_general(a, b, (((1,), (1,)), ((), ())), preferred_element_type=F32)


def dot_tn(a, b):
    return lax.dot_general(a, b, (((0,), (0,)), ((), ())), preferred_element_type=F32)


def pack_kernel(embeds, weight, solve, probes, probe_solves, packed, extended, weight_in, solve_in, probes_in, probe_solves_in, sems):
    rows, width = embeds.shape[0], weight.shape[1]
    embeds_in = extended.at[:, 128:]
    loads = [
        pltpu.make_async_copy(source, target, sems.at[k])
        for k, (source, target) in enumerate(
            (
                (weight, weight_in),
                (embeds, embeds_in),
                (probes, probes_in),
                (probe_solves, probe_solves_in),
                (solve, solve_in),
            )
        )
    ]
    for load in loads:
        load.start()
    for load in loads:
        load.wait()
    feats = jnp.dot(embeds_in[...], weight_in[...], preferred_element_type=F32).astype(BF16)
    wide = feats.astype(F32)
    sq = jnp.sum(wide * wide, axis=1, keepdims=True)
    sq_hi = sq.astype(BF16).astype(F32)
    sq_mid = (sq - sq_hi).astype(BF16).astype(F32)
    sq_lo = sq - sq_hi - sq_mid
    fold = math.sqrt(5.0 / 3.0 * ROOT5)
    scale = (2.0 * probes.shape[0]) ** (-0.5) * fold
    both = jnp.concatenate(
        [solve_in[...] * fold, probes_in[...] * -scale, probe_solves_in[...] * -scale, jnp.zeros((1, rows), F32)],
        axis=0,
    ).T
    hi = both.astype(BF16).astype(F32)
    lo = both - hi
    lane = lax.broadcasted_iota(jnp.int32, (rows, 32), 1)
    tail = jnp.where(lane == 0, sq_hi, jnp.where(lane == 1, sq_mid, jnp.where(lane == 2, sq_lo, 0.0)))
    tail = jnp.concatenate([hi, lo, hi, tail], axis=1).astype(BF16)
    extended[:, :128] = tail
    packed[:, :width] = feats
    packed[:, width:] = tail


def split_kernel(count, weight, *refs):
    line, embeds = refs[count:]
    rows, width = refs[0].shape[0], weight.shape[1]
    for k, ref in enumerate(refs[:count]):
        block = slice(k * rows, (k + 1) * rows)
        own = ref[:, 128:]
        line[block, :] = jnp.dot(own, weight[...], preferred_element_type=F32).astype(BF16)
        embeds[block, :] = own
    for k in range(0, count, 2):
        both = [ref[:, :64].astype(F32) for ref in refs[k : k + 2]]
        line[count * rows :, k * 64 : k * 64 + 128] = jnp.concatenate(both, axis=1).astype(BF16)


def left_map(count):
    source = np.zeros((32,), np.int32)
    sign = np.zeros((32,), np.float32)
    sign[0] = 1.0
    for k in range(count):
        source[1 + k], sign[1 + k] = 1 + count + k, -1.0
        source[1 + count + k], sign[1 + count + k] = 1 + k, -1.0
    table = np.zeros((2, 128, 128), np.float32)
    for half in range(2):
        for group, offset in ((0, 0), (1, 0), (2, 32)):
            for k in range(32):
                table[half, 64 * half + offset + source[k], 32 * group + k] = sign[k]
    return jnp.asarray(table, BF16)


def tile_kernel(sub, step, adds, table, rows_ref, *refs):
    *columns, out = refs
    if adds:
        begin, *columns = columns
    width = out.shape[1]
    block = rows_ref.shape[0] // 5
    rows = 4 * block
    u_rows = rows_ref[:rows, :]
    wide = u_rows.astype(F32)
    twice = (wide * -2.0).astype(BF16)
    left = []
    for k in range(4):
        start = k // 2 * 128
        fac = rows_ref[rows:, start : start + 128]
        left.append(jnp.dot(fac, table[k % 2], preferred_element_type=F32).astype(BF16))
    left = jnp.concatenate(left, axis=0)
    sq_rows = jnp.sum(wide * wide, axis=1, keepdims=True)
    lane = lax.broadcasted_iota(jnp.int32, (8, 128), 1)
    pick_cols = jnp.where((lane >= 96) & (lane < 99), 1.0, 0.0).astype(BF16)
    blocks = [slice(k, k + sub) for k in range(0, rows, sub)]
    acc = [begin[block, :] if adds else jnp.zeros((sub, width), F32) for block in blocks]
    total = [jnp.zeros((sub, 128), F32) for _ in blocks]
    work = [
        (ref, start, k)
        for ref in columns
        for start in range(0, ref.shape[0], step)
        for k in range(len(blocks))
    ]

    def products(ref, start, k):
        u_cols = ref[start : start + step, :width]
        right = ref[start : start + step, width:]
        sq_cols = dot_nt(pick_cols, right)[:1]
        return u_cols, sq_cols, dot_nt(twice[blocks[k]], u_cols), dot_nt(left[blocks[k]], right)

    ahead = products(*work[0])
    for index, (_, _, k) in enumerate(work):
        u_cols, sq_cols, cross, pair = ahead
        if index + 1 < len(work):
            ahead = products(*work[index + 1])
        d2 = jnp.maximum((sq_rows[blocks[k]] + sq_cols) + cross, 1e-30)
        dist = d2 * lax.rsqrt(d2)
        coupling = pair * ((dist + 1.0 / ROOT5) * jnp.exp2(dist * (-ROOT5 * LOG2E)))
        for j in range(0, step, 128):
            total[k] = total[k] + coupling[:, j : j + 128]
        acc[k] = acc[k] + jnp.dot(coupling.astype(BF16), u_cols, preferred_element_type=F32)
    for k, block in enumerate(blocks):
        row_total = jnp.sum(total[k], axis=1, keepdims=True)
        out[block, :] = (acc[k] - row_total * u_rows[block].astype(F32)).astype(out.dtype)


def sum_rows_kernel(count, *refs):
    parts, (embeds, partial, own, *others) = refs[:count], refs[count:]
    rows = own.shape[0]
    total = parts[0][...]
    for ref in parts[1:]:
        total = total + ref[...].astype(F32)
    hi = total.astype(BF16)
    lo = (total - hi.astype(F32)).astype(BF16)
    own[...] = total[:rows]
    for k, ref in enumerate(others):
        ref[...] = hi[(k + 1) * rows : (k + 2) * rows]
    partial[...] = (dot_tn(embeds[...], hi) + dot_tn(embeds[...], lo)).astype(BF16)


def finish_rows_kernel(own, b, c, d, grad_rows):
    grad_rows[...] = (own[...] + b[...].astype(F32)) + (c[...].astype(F32) + d[...].astype(F32))


def sum_spread_kernel(*refs):
    *parts, out = refs
    total = None
    for ref in parts:
        for k in range(ref.shape[0]):
            term = ref[k].astype(F32)
            total = term if total is None else total + term
    low = total.astype(out.dtype)
    for k in range(out.shape[0]):
        out[k] = low


def sum_spread(parts, copies, dtype):
    return pl.pallas_call(
        sum_spread_kernel,
        out_shape=jax.ShapeDtypeStruct((copies,) + parts[0].shape[1:], dtype),
        in_specs=[VMEM] * len(parts),
        out_specs=VMEM,
        compiler_params=params(16),
        name="sum_spread",
    )(*parts)


def ring(array, axis, size, shift):
    return lax.ppermute(array, axis, [(i, (i + shift) % size) for i in range(size)])


def move(array, sizes, where):
    dims = [sizes[a] for a in ALL]
    perm = []
    for source in range(math.prod(dims)):
        place = dict(zip(ALL, (int(i) for i in np.unravel_index(source, dims))))
        for axis, shift in where(place["core"]).items():
            if axis == "z":
                z = (place["zh"] * sizes["zl"] + place["zl"] + shift) % (sizes["zh"] * sizes["zl"])
                place["zh"], place["zl"] = divmod(z, sizes["zl"])
            else:
                place[axis] = (place[axis] + shift) % sizes[axis]
        perm.append((source, int(np.ravel_multi_index([place[a] for a in ALL], dims))))
    return lax.ppermute(array, ALL, perm)


def turn(array, sizes, stage, shift):
    return move(array, sizes, lambda core: {"y" if (core + stage) % 2 == 0 else "x": shift})


def exchange(array, axes):
    return lax.all_to_all(array, axes, split_axis=0, concat_axis=0, tiled=True)


def shards(sizes, embeds, weight, solve, probes, probe_solves):
    rows, width = embeds.shape[0], weight.shape[1]
    n_side, n_z = sizes["x"], sizes["zh"] * sizes["zl"]
    pack, extended = pl.pallas_call(
        pack_kernel,
        out_shape=[
            jax.ShapeDtypeStruct((rows, width + 128), BF16),
            jax.ShapeDtypeStruct((rows, 128 + embeds.shape[1]), BF16),
        ],
        in_specs=[pl.BlockSpec(memory_space=pltpu.HBM)] * 5,
        out_specs=[VMEM] * 2,
        scratch_shapes=[
            pltpu.VMEM(weight.shape, BF16),
            pltpu.VMEM((1, rows), F32),
            pltpu.VMEM(probes.shape[::-1], F32),
            pltpu.VMEM(probes.shape[::-1], F32),
            pltpu.SemaphoreType.DMA((5,)),
        ],
        compiler_params=params(48),
        name="pack",
    )(*(pltpu.with_memory_space_constraint(a, pltpu.HBM) for a in (embeds, weight, solve[None, :], probes.T, probe_solves.T)))

    blocks = [extended] + [turn(extended, sizes, 0, -d) for d in range(1, n_side)]
    line, embeds_line = pl.pallas_call(
        functools.partial(split_kernel, n_side),
        out_shape=[
            jax.ShapeDtypeStruct(((n_side + 1) * rows, width), BF16),
            jax.ShapeDtypeStruct((n_side * rows, embeds.shape[1]), BF16),
        ],
        in_specs=[VMEM] * (n_side + 1),
        out_specs=[VMEM] * 2,
        compiler_params=params(8),
        name="split",
    )(weight, *blocks)
    pair = jnp.concatenate([pack, ring(pack, DEPTH, n_z, n_z // 2)], axis=0)
    pair, line = lax.optimization_barrier((pair, line))
    four = jnp.concatenate([pair, ring(pair, "core", 2, 1)], axis=0)
    near = move(four, sizes, lambda core: {"z": 1 - 2 * core})
    far = move(pair, sizes, lambda core: {"z": 2 - 4 * core})
    lines = [line] + [turn(line, sizes, 1, -d) for d in range(1, n_side)]
    table = left_map(probes.shape[1])

    def tile(rows_in, columns, dtype, start=None):
        return pl.pallas_call(
            functools.partial(tile_kernel, 256, 256, start is not None),
            out_shape=jax.ShapeDtypeStruct((n_side * rows, width), dtype),
            in_specs=[VMEM] * (2 + len(columns) + (start is not None)),
            out_specs=VMEM,
            compiler_params=params(16),
            name="tile",
        )(table, rows_in, *([] if start is None else [start]), *columns)

    begin = tile(line, [four], F32)
    near, far, lines, begin = lax.optimization_barrier((near, far, lines, begin))
    columns = [four, near, far, ring(near, "core", 2, 1), ring(far, "core", 2, 1)]

    back = {}
    for d in (0, 3, 1, 2):
        if d == 2:
            part = tile(lines[d], columns[3:], BF16, tile(lines[d], columns[:3], F32))
        elif d == 0:
            part = tile(line, columns[1:], F32, begin)
        else:
            part = tile(lines[d], columns, BF16)
        back[d] = part if d == 0 else turn(part, sizes, 1, d)

    partial, own_rows, *other_rows = pl.pallas_call(
        functools.partial(sum_rows_kernel, n_side),
        out_shape=[
            jax.ShapeDtypeStruct((embeds.shape[1], width), BF16),
            jax.ShapeDtypeStruct((rows, width), F32),
        ]
        + [jax.ShapeDtypeStruct((rows, width), BF16)] * (n_side - 1),
        in_specs=[VMEM] * (n_side + 1),
        out_specs=[VMEM] * (n_side + 1),
        compiler_params=params(16),
        name="sum_rows",
    )(*(back[d] for d in range(n_side)), embeds_line)
    arrived = [turn(other_rows[0], sizes, 0, 1)]
    n_plane = n_side * n_side
    pieces = exchange(partial.reshape(n_plane, -1, width), PLANE)
    pieces, arrived[0] = lax.optimization_barrier((pieces, arrived[0]))
    spread = sum_spread([pieces], n_z * 2, BF16)
    spread, other_rows[1], other_rows[2] = lax.optimization_barrier((spread, other_rows[1], other_rows[2]))
    pieces = exchange(spread, STACK)
    arrived += [turn(other_rows[d], sizes, 0, d + 1) for d in (1, 2)]
    grad_rows = pl.pallas_call(
        finish_rows_kernel,
        out_shape=jax.ShapeDtypeStruct((rows, width), F32),
        in_specs=[VMEM] * 4,
        out_specs=VMEM,
        compiler_params=params(16),
        name="finish_rows",
    )(own_rows, *arrived)
    pieces, grad_rows = lax.optimization_barrier((pieces, grad_rows))
    pieces = exchange(sum_spread([pieces], n_plane, BF16), PLANE)
    total_points = rows * n_plane * n_z * 2
    grad_weight = pieces.reshape(-1, width).astype(F32) * (1.0 / math.sqrt(total_points))
    return grad_rows, grad_weight


def solution(mesh):
    sizes = {"y": 4, "zh": 2, "core": 2, "zl": 4, "x": 4}
    fine = Mesh(mesh.devices.reshape(tuple(sizes[a] for a in ALL)), ALL)
    return jax.shard_map(
        functools.partial(shards, sizes),
        mesh=fine,
        in_specs=(P(ALL, None), P(), P(ALL), P(ALL, None), P(ALL, None)),
        out_specs=(P(ALL, None), P()),
        check_vma=False,
    )
```

```python
import functools
import math

import jax
import jax.numpy as jnp
import numpy as np
from jax import lax
from jax.experimental import pallas as pl
from jax.experimental.pallas import tpu as pltpu
from jax.sharding import Mesh, PartitionSpec as P

LOG2E = math.log2(math.e)
ROOT5 = math.sqrt(5.0)
ALL = ("y", "zh", "core", "zl", "x")
PLANE = ("y", "x")
STACK = ("zh", "core", "zl")
DEPTH = ("zh", "zl")
F32 = jnp.float32
BF16 = jnp.bfloat16
VMEM = pl.BlockSpec(memory_space=pltpu.VMEM)


def params(mib):
    return pltpu.CompilerParams(vmem_limit_bytes=mib << 20)


def dot_nt(a, b):
    return lax.dot_general(a, b, (((1,), (1,)), ((), ())), preferred_element_type=F32)


def dot_tn(a, b):
    return lax.dot_general(a, b, (((0,), (0,)), ((), ())), preferred_element_type=F32)


def pack_kernel(embeds, weight, solve, probes, probe_solves, packed, extended, weight_in, solve_in, probes_in, probe_solves_in, sems):
    rows, width = embeds.shape[0], weight.shape[1]
    embeds_in = extended.at[:, 128:]
    loads = [
        pltpu.make_async_copy(source, target, sems.at[k])
        for k, (source, target) in enumerate(
            (
                (weight, weight_in),
                (embeds, embeds_in),
                (probes, probes_in),
                (probe_solves, probe_solves_in),
                (solve, solve_in),
            )
        )
    ]
    for load in loads:
        load.start()
    for load in loads:
        load.wait()
    feats = jnp.dot(embeds_in[...], weight_in[...], preferred_element_type=F32).astype(BF16)
    wide = feats.astype(F32)
    sq = jnp.sum(wide * wide, axis=1, keepdims=True)
    sq_hi = sq.astype(BF16).astype(F32)
    sq_mid = (sq - sq_hi).astype(BF16).astype(F32)
    sq_lo = sq - sq_hi - sq_mid
    fold = math.sqrt(5.0 / 3.0 * ROOT5)
    scale = (2.0 * probes.shape[0]) ** (-0.5) * fold
    both = jnp.concatenate(
        [solve_in[...] * fold, probes_in[...] * -scale, probe_solves_in[...] * -scale, jnp.zeros((1, rows), F32)],
        axis=0,
    ).T
    hi = both.astype(BF16).astype(F32)
    lo = both - hi
    lane = lax.broadcasted_iota(jnp.int32, (rows, 32), 1)
    tail = jnp.where(lane == 0, sq_hi, jnp.where(lane == 1, sq_mid, jnp.where(lane == 2, sq_lo, 0.0)))
    tail = jnp.concatenate([hi, lo, hi, tail], axis=1).astype(BF16)
    extended[:, :128] = tail
    packed[:, :width] = feats
    packed[:, width:] = tail


def split_kernel(count, weight, *refs):
    line, embeds = refs[count:]
    rows, width = refs[0].shape[0], weight.shape[1]
    for k, ref in enumerate(refs[:count]):
        block = slice(k * rows, (k + 1) * rows)
        own = ref[:, 128:]
        line[block, :] = jnp.dot(own, weight[...], preferred_element_type=F32).astype(BF16)
        embeds[block, :] = own
    for k in range(0, count, 2):
        both = [ref[:, :64].astype(F32) for ref in refs[k : k + 2]]
        line[count * rows :, k * 64 : k * 64 + 128] = jnp.concatenate(both, axis=1).astype(BF16)


def left_map(count):
    source = np.zeros((32,), np.int32)
    sign = np.zeros((32,), np.float32)
    sign[0] = 1.0
    for k in range(count):
        source[1 + k], sign[1 + k] = 1 + count + k, -1.0
        source[1 + count + k], sign[1 + count + k] = 1 + k, -1.0
    table = np.zeros((2, 128, 128), np.float32)
    for half in range(2):
        for group, offset in ((0, 0), (1, 0), (2, 32)):
            for k in range(32):
                table[half, 64 * half + offset + source[k], 32 * group + k] = sign[k]
    return jnp.asarray(table, BF16)


def tile_kernel(sub, step, adds, table, rows_ref, *refs):
    *columns, out = refs
    if adds:
        begin, *columns = columns
    width = out.shape[1]
    block = rows_ref.shape[0] // 5
    rows = 4 * block
    u_rows = rows_ref[:rows, :]
    wide = u_rows.astype(F32)
    twice = (wide * -2.0).astype(BF16)
    left = []
    for k in range(4):
        start = k // 2 * 128
        fac = rows_ref[rows:, start : start + 128]
        left.append(jnp.dot(fac, table[k % 2], preferred_element_type=F32).astype(BF16))
    left = jnp.concatenate(left, axis=0)
    sq_rows = jnp.sum(wide * wide, axis=1, keepdims=True)
    lane = lax.broadcasted_iota(jnp.int32, (8, 128), 1)
    pick_cols = jnp.where((lane >= 96) & (lane < 99), 1.0, 0.0).astype(BF16)
    blocks = [slice(k, k + sub) for k in range(0, rows, sub)]
    acc = [begin[block, :] if adds else jnp.zeros((sub, width), F32) for block in blocks]
    total = [jnp.zeros((sub, 128), F32) for _ in blocks]
    work = [
        (ref, start, k)
        for ref in columns
        for start in range(0, ref.shape[0], step)
        for k in range(len(blocks))
    ]

    def products(ref, start, k):
        u_cols = ref[start : start + step, :width]
        right = ref[start : start + step, width:]
        sq_cols = dot_nt(pick_cols, right)[:1]
        return u_cols, sq_cols, dot_nt(twice[blocks[k]], u_cols), dot_nt(left[blocks[k]], right)

    ahead = products(*work[0])
    for index, (_, _, k) in enumerate(work):
        u_cols, sq_cols, cross, pair = ahead
        if index + 1 < len(work):
            ahead = products(*work[index + 1])
        d2 = jnp.maximum((sq_rows[blocks[k]] + sq_cols) + cross, 1e-30)
        dist = d2 * lax.rsqrt(d2)
        coupling = pair * ((dist + 1.0 / ROOT5) * jnp.exp2(dist * (-ROOT5 * LOG2E)))
        for j in range(0, step, 128):
            total[k] = total[k] + coupling[:, j : j + 128]
        acc[k] = acc[k] + jnp.dot(coupling.astype(BF16), u_cols, preferred_element_type=F32)
    for k, block in enumerate(blocks):
        row_total = jnp.sum(total[k], axis=1, keepdims=True)
        out[block, :] = (acc[k] - row_total * u_rows[block].astype(F32)).astype(out.dtype)


def sum_rows_kernel(a, b, c, embeds, total, weight):
    rows = a[...] + (b[...].astype(F32) + c[...].astype(F32))
    hi = rows.astype(BF16)
    lo = (rows - hi.astype(F32)).astype(BF16)
    total[...] = rows
    weight[...] = dot_tn(embeds[...], hi) + dot_tn(embeds[...], lo)


def last_rows_kernel(total, weight, last, embeds, partial, own, *others):
    rows = own.shape[0]
    partial[...] = (weight[...] + dot_tn(embeds[...], last[...])).astype(BF16)
    own[...] = total[:rows] + last[:rows].astype(F32)
    for k, ref in enumerate(others):
        block = slice((k + 1) * rows, (k + 2) * rows)
        ref[...] = (total[block] + last[block].astype(F32)).astype(BF16)


def finish_rows_kernel(own, b, c, d, grad_rows):
    grad_rows[...] = (own[...] + b[...].astype(F32)) + (c[...].astype(F32) + d[...].astype(F32))


def sum_spread_kernel(*refs):
    *parts, out = refs
    total = None
    for ref in parts:
        for k in range(ref.shape[0]):
            term = ref[k].astype(F32)
            total = term if total is None else total + term
    low = total.astype(out.dtype)
    for k in range(out.shape[0]):
        out[k] = low


def sum_spread(parts, copies, dtype):
    return pl.pallas_call(
        sum_spread_kernel,
        out_shape=jax.ShapeDtypeStruct((copies,) + parts[0].shape[1:], dtype),
        in_specs=[VMEM] * len(parts),
        out_specs=VMEM,
        compiler_params=params(16),
        name="sum_spread",
    )(*parts)


def ring(array, axis, size, shift):
    return lax.ppermute(array, axis, [(i, (i + shift) % size) for i in range(size)])


def move(array, sizes, where):
    dims = [sizes[a] for a in ALL]
    perm = []
    for source in range(math.prod(dims)):
        place = dict(zip(ALL, (int(i) for i in np.unravel_index(source, dims))))
        for axis, shift in where(place["core"]).items():
            if axis == "z":
                z = (place["zh"] * sizes["zl"] + place["zl"] + shift) % (sizes["zh"] * sizes["zl"])
                place["zh"], place["zl"] = divmod(z, sizes["zl"])
            else:
                place[axis] = (place[axis] + shift) % sizes[axis]
        perm.append((source, int(np.ravel_multi_index([place[a] for a in ALL], dims))))
    return lax.ppermute(array, ALL, perm)


def turn(array, sizes, stage, shift):
    return move(array, sizes, lambda core: {"y" if (core + stage) % 2 == 0 else "x": shift})


def exchange(array, axes):
    return lax.all_to_all(array, axes, split_axis=0, concat_axis=0, tiled=True)


def shards(sizes, embeds, weight, solve, probes, probe_solves):
    rows, width = embeds.shape[0], weight.shape[1]
    n_side, n_z = sizes["x"], sizes["zh"] * sizes["zl"]
    pack, extended = pl.pallas_call(
        pack_kernel,
        out_shape=[
            jax.ShapeDtypeStruct((rows, width + 128), BF16),
            jax.ShapeDtypeStruct((rows, 128 + embeds.shape[1]), BF16),
        ],
        in_specs=[pl.BlockSpec(memory_space=pltpu.HBM)] * 5,
        out_specs=[VMEM] * 2,
        scratch_shapes=[
            pltpu.VMEM(weight.shape, BF16),
            pltpu.VMEM((1, rows), F32),
            pltpu.VMEM(probes.shape[::-1], F32),
            pltpu.VMEM(probes.shape[::-1], F32),
            pltpu.SemaphoreType.DMA((5,)),
        ],
        compiler_params=params(48),
        name="pack",
    )(*(pltpu.with_memory_space_constraint(a, pltpu.HBM) for a in (embeds, weight, solve[None, :], probes.T, probe_solves.T)))

    blocks = [extended] + [turn(extended, sizes, 0, -d) for d in range(1, n_side)]
    line, embeds_line = pl.pallas_call(
        functools.partial(split_kernel, n_side),
        out_shape=[
            jax.ShapeDtypeStruct(((n_side + 1) * rows, width), BF16),
            jax.ShapeDtypeStruct((n_side * rows, embeds.shape[1]), BF16),
        ],
        in_specs=[VMEM] * (n_side + 1),
        out_specs=[VMEM] * 2,
        compiler_params=params(8),
        name="split",
    )(weight, *blocks)
    pair = jnp.concatenate([pack, ring(pack, DEPTH, n_z, n_z // 2)], axis=0)
    pair, line = lax.optimization_barrier((pair, line))
    near = [ring(pair, DEPTH, n_z, d) for d in (1, -1)]
    near.append(move(pair, sizes, lambda core: {"z": 2 - 4 * core}))
    four = [pair, ring(pair, "core", 2, 1)]
    lines = [line] + [turn(line, sizes, 1, -d) for d in range(1, n_side)]
    table = left_map(probes.shape[1])

    def tile(rows_in, columns, dtype, start=None):
        return pl.pallas_call(
            functools.partial(tile_kernel, 256, 256, start is not None),
            out_shape=jax.ShapeDtypeStruct((n_side * rows, width), dtype),
            in_specs=[VMEM] * (2 + len(columns) + (start is not None)),
            out_specs=VMEM,
            compiler_params=params(16),
            name="tile",
        )(table, rows_in, *([] if start is None else [start]), *columns)

    begin = tile(line, four, F32)
    near, lines, begin = lax.optimization_barrier((near, lines, begin))
    columns = four + near
    count = len(columns)
    columns += [ring(part, "core", 2, 1) for part in near]

    back = {}
    for d in (0, 3, 1, 2):
        if d == 2:
            part = tile(lines[d], columns[count:], BF16, tile(lines[d], columns[:count], F32))
        elif d == 0:
            part = tile(line, columns[len(four) :], F32, begin)
        else:
            part = tile(lines[d], columns, BF16)
        back[d] = part if d == 0 else turn(part, sizes, 1, d)

    total, weight_sum = pl.pallas_call(
        sum_rows_kernel,
        out_shape=[
            jax.ShapeDtypeStruct((n_side * rows, width), F32),
            jax.ShapeDtypeStruct((embeds.shape[1], width), F32),
        ],
        in_specs=[VMEM] * 4,
        out_specs=[VMEM] * 2,
        compiler_params=params(16),
        name="sum_rows",
    )(back[0], back[1], back[2], embeds_line)
    partial, own_rows, *other_rows = pl.pallas_call(
        last_rows_kernel,
        out_shape=[
            jax.ShapeDtypeStruct((embeds.shape[1], width), BF16),
            jax.ShapeDtypeStruct((rows, width), F32),
        ]
        + [jax.ShapeDtypeStruct((rows, width), BF16)] * (n_side - 1),
        in_specs=[VMEM] * 4,
        out_specs=[VMEM] * (n_side + 1),
        compiler_params=params(16),
        name="last_rows",
    )(total, weight_sum, back[3], embeds_line)
    arrived = [turn(other_rows[0], sizes, 0, 1)]

    n_plane = n_side * n_side
    pieces = exchange(partial.reshape(n_plane, -1, width), PLANE)
    pieces, arrived[0] = lax.optimization_barrier((pieces, arrived[0]))
    spread = sum_spread([pieces], n_z * 2, BF16)
    spread, other_rows[1], other_rows[2] = lax.optimization_barrier((spread, other_rows[1], other_rows[2]))
    pieces = exchange(spread, STACK)
    arrived += [turn(other_rows[d], sizes, 0, d + 1) for d in (1, 2)]
    grad_rows = pl.pallas_call(
        finish_rows_kernel,
        out_shape=jax.ShapeDtypeStruct((rows, width), F32),
        in_specs=[VMEM] * 4,
        out_specs=VMEM,
        compiler_params=params(16),
        name="finish_rows",
    )(own_rows, *arrived)
    pieces, grad_rows = lax.optimization_barrier((pieces, grad_rows))
    pieces = exchange(sum_spread([pieces], n_plane, BF16), PLANE)
    total_points = rows * n_plane * n_z * 2
    grad_weight = pieces.reshape(-1, width).astype(F32) * (1.0 / math.sqrt(total_points))
    return grad_rows, grad_weight


def solution(mesh):
    sizes = {"y": 4, "zh": 2, "core": 2, "zl": 4, "x": 4}
    fine = Mesh(mesh.devices.reshape(tuple(sizes[a] for a in ALL)), ALL)
    return jax.shard_map(
        functools.partial(shards, sizes),
        mesh=fine,
        in_specs=(P(ALL, None), P(), P(ALL), P(ALL, None), P(ALL, None)),
        out_specs=(P(ALL, None), P()),
        check_vma=False,
    )
```

```python
import functools
import math

import jax
import jax.numpy as jnp
import numpy as np
from jax import lax
from jax.experimental import pallas as pl
from jax.experimental.pallas import tpu as pltpu
from jax.sharding import Mesh, PartitionSpec as P

LOG2E = math.log2(math.e)
ROOT5 = math.sqrt(5.0)
ALL = ("y", "zh", "core", "zl", "x")
PLANE = ("y", "x")
STACK = ("zh", "core", "zl")
DEPTH = ("zh", "zl")
F32 = jnp.float32
BF16 = jnp.bfloat16
VMEM = pl.BlockSpec(memory_space=pltpu.VMEM)


def params(mib):
    return pltpu.CompilerParams(vmem_limit_bytes=mib << 20)


def dot_nt(a, b):
    return lax.dot_general(a, b, (((1,), (1,)), ((), ())), preferred_element_type=F32)


def dot_tn(a, b):
    return lax.dot_general(a, b, (((0,), (0,)), ((), ())), preferred_element_type=F32)


def pack_kernel(embeds, weight, solve, probes, probe_solves, packed, extended, weight_in, solve_in, probes_in, probe_solves_in, sems):
    rows, width = embeds.shape[0], weight.shape[1]
    embeds_in = extended.at[:, 128:]
    loads = [
        pltpu.make_async_copy(source, target, sems.at[k])
        for k, (source, target) in enumerate(
            (
                (weight, weight_in),
                (embeds, embeds_in),
                (probes, probes_in),
                (probe_solves, probe_solves_in),
                (solve, solve_in),
            )
        )
    ]
    for load in loads:
        load.start()
    for load in loads:
        load.wait()
    feats = jnp.dot(embeds_in[...], weight_in[...], preferred_element_type=F32).astype(BF16)
    wide = feats.astype(F32)
    sq = jnp.sum(wide * wide, axis=1, keepdims=True)
    sq_hi = sq.astype(BF16).astype(F32)
    sq_mid = (sq - sq_hi).astype(BF16).astype(F32)
    sq_lo = sq - sq_hi - sq_mid
    fold = math.sqrt(5.0 / 3.0 * ROOT5)
    scale = (2.0 * probes.shape[0]) ** (-0.5) * fold
    both = jnp.concatenate(
        [solve_in[...] * fold, probes_in[...] * -scale, probe_solves_in[...] * -scale, jnp.zeros((1, rows), F32)],
        axis=0,
    ).T
    hi = both.astype(BF16).astype(F32)
    lo = both - hi
    lane = lax.broadcasted_iota(jnp.int32, (rows, 32), 1)
    tail = jnp.where(lane == 0, sq_hi, jnp.where(lane == 1, sq_mid, jnp.where(lane == 2, sq_lo, 0.0)))
    tail = jnp.concatenate([hi, lo, hi, tail], axis=1).astype(BF16)
    extended[:, :128] = tail
    packed[:, :width] = feats
    packed[:, width:] = tail


def split_kernel(count, weight, *refs):
    line, embeds = refs[count:]
    rows, width = refs[0].shape[0], weight.shape[1]
    for k, ref in enumerate(refs[:count]):
        block = slice(k * rows, (k + 1) * rows)
        own = ref[:, 128:]
        line[block, :] = jnp.dot(own, weight[...], preferred_element_type=F32).astype(BF16)
        embeds[block, :] = own
    for k in range(0, count, 2):
        both = [ref[:, :64].astype(F32) for ref in refs[k : k + 2]]
        line[count * rows :, k * 64 : k * 64 + 128] = jnp.concatenate(both, axis=1).astype(BF16)


def left_map(count):
    source = np.zeros((32,), np.int32)
    sign = np.zeros((32,), np.float32)
    sign[0] = 1.0
    for k in range(count):
        source[1 + k], sign[1 + k] = 1 + count + k, -1.0
        source[1 + count + k], sign[1 + count + k] = 1 + k, -1.0
    table = np.zeros((2, 128, 128), np.float32)
    for half in range(2):
        for group, offset in ((0, 0), (1, 0), (2, 32)):
            for k in range(32):
                table[half, 64 * half + offset + source[k], 32 * group + k] = sign[k]
    return jnp.asarray(table, BF16)


def tile_kernel(sub, step, adds, table, rows_ref, *refs):
    *columns, out = refs
    if adds:
        begin, *columns = columns
    width = out.shape[1]
    block = rows_ref.shape[0] // 5
    rows = 4 * block
    u_rows = rows_ref[:rows, :]
    wide = u_rows.astype(F32)
    twice = (wide * -2.0).astype(BF16)
    left = []
    for k in range(4):
        start = k // 2 * 128
        fac = rows_ref[rows:, start : start + 128]
        left.append(jnp.dot(fac, table[k % 2], preferred_element_type=F32).astype(BF16))
    left = jnp.concatenate(left, axis=0)
    sq_rows = jnp.sum(wide * wide, axis=1, keepdims=True)
    lane = lax.broadcasted_iota(jnp.int32, (8, 128), 1)
    pick_cols = jnp.where((lane >= 96) & (lane < 99), 1.0, 0.0).astype(BF16)
    blocks = [slice(k, k + sub) for k in range(0, rows, sub)]
    acc = [begin[block, :] if adds else jnp.zeros((sub, width), F32) for block in blocks]
    total = [jnp.zeros((sub, 128), F32) for _ in blocks]
    work = [
        (ref, start, k)
        for ref in columns
        for start in range(0, ref.shape[0], step)
        for k in range(len(blocks))
    ]

    def products(ref, start, k):
        u_cols = ref[start : start + step, :width]
        right = ref[start : start + step, width:]
        sq_cols = dot_nt(pick_cols, right)[:1]
        return u_cols, sq_cols, dot_nt(twice[blocks[k]], u_cols), dot_nt(left[blocks[k]], right)

    ahead = products(*work[0])
    for index, (_, _, k) in enumerate(work):
        u_cols, sq_cols, cross, pair = ahead
        if index + 1 < len(work):
            ahead = products(*work[index + 1])
        d2 = jnp.maximum((sq_rows[blocks[k]] + sq_cols) + cross, 1e-30)
        dist = d2 * lax.rsqrt(d2)
        coupling = pair * ((dist + 1.0 / ROOT5) * jnp.exp2(dist * (-ROOT5 * LOG2E)))
        for j in range(0, step, 128):
            total[k] = total[k] + coupling[:, j : j + 128]
        acc[k] = acc[k] + jnp.dot(coupling.astype(BF16), u_cols, preferred_element_type=F32)
    for k, block in enumerate(blocks):
        row_total = jnp.sum(total[k], axis=1, keepdims=True)
        out[block, :] = (acc[k] - row_total * u_rows[block].astype(F32)).astype(out.dtype)


def sum_rows_kernel(a, b, c, embeds, total, weight):
    rows = a[...] + (b[...].astype(F32) + c[...].astype(F32))
    hi = rows.astype(BF16)
    lo = (rows - hi.astype(F32)).astype(BF16)
    total[...] = rows
    weight[...] = dot_tn(embeds[...], hi) + dot_tn(embeds[...], lo)


def last_rows_kernel(total, weight, last, embeds, partial, own, *others):
    rows = own.shape[0]
    partial[...] = (weight[...] + dot_tn(embeds[...], last[...])).astype(BF16)
    own[...] = total[:rows] + last[:rows].astype(F32)
    for k, ref in enumerate(others):
        block = slice((k + 1) * rows, (k + 2) * rows)
        ref[...] = (total[block] + last[block].astype(F32)).astype(BF16)


def finish_rows_kernel(own, b, c, d, grad_rows):
    grad_rows[...] = (own[...] + b[...].astype(F32)) + (c[...].astype(F32) + d[...].astype(F32))


def sum_spread_kernel(*refs):
    *parts, out = refs
    total = None
    for ref in parts:
        for k in range(ref.shape[0]):
            term = ref[k].astype(F32)
            total = term if total is None else total + term
    low = total.astype(out.dtype)
    for k in range(out.shape[0]):
        out[k] = low


def sum_spread(parts, copies, dtype):
    return pl.pallas_call(
        sum_spread_kernel,
        out_shape=jax.ShapeDtypeStruct((copies,) + parts[0].shape[1:], dtype),
        in_specs=[VMEM] * len(parts),
        out_specs=VMEM,
        compiler_params=params(16),
        name="sum_spread",
    )(*parts)


def ring(array, axis, size, shift):
    return lax.ppermute(array, axis, [(i, (i + shift) % size) for i in range(size)])


def move(array, sizes, where):
    dims = [sizes[a] for a in ALL]
    perm = []
    for source in range(math.prod(dims)):
        place = dict(zip(ALL, (int(i) for i in np.unravel_index(source, dims))))
        for axis, shift in where(place["core"]).items():
            if axis == "z":
                z = (place["zh"] * sizes["zl"] + place["zl"] + shift) % (sizes["zh"] * sizes["zl"])
                place["zh"], place["zl"] = divmod(z, sizes["zl"])
            else:
                place[axis] = (place[axis] + shift) % sizes[axis]
        perm.append((source, int(np.ravel_multi_index([place[a] for a in ALL], dims))))
    return lax.ppermute(array, ALL, perm)


def turn(array, sizes, stage, shift):
    return move(array, sizes, lambda core: {"y" if (core + stage) % 2 == 0 else "x": shift})


def exchange(array, axes):
    return lax.all_to_all(array, axes, split_axis=0, concat_axis=0, tiled=True)


def shards(sizes, embeds, weight, solve, probes, probe_solves):
    rows, width = embeds.shape[0], weight.shape[1]
    n_side, n_z = sizes["x"], sizes["zh"] * sizes["zl"]
    pack, extended = pl.pallas_call(
        pack_kernel,
        out_shape=[
            jax.ShapeDtypeStruct((rows, width + 128), BF16),
            jax.ShapeDtypeStruct((rows, 128 + embeds.shape[1]), BF16),
        ],
        in_specs=[pl.BlockSpec(memory_space=pltpu.HBM)] * 5,
        out_specs=[VMEM] * 2,
        scratch_shapes=[
            pltpu.VMEM(weight.shape, BF16),
            pltpu.VMEM((1, rows), F32),
            pltpu.VMEM(probes.shape[::-1], F32),
            pltpu.VMEM(probes.shape[::-1], F32),
            pltpu.SemaphoreType.DMA((5,)),
        ],
        compiler_params=params(48),
        name="pack",
    )(*(pltpu.with_memory_space_constraint(a, pltpu.HBM) for a in (embeds, weight, solve[None, :], probes.T, probe_solves.T)))

    blocks = [extended] + [turn(extended, sizes, 0, -d) for d in range(1, n_side)]
    line, embeds_line = pl.pallas_call(
        functools.partial(split_kernel, n_side),
        out_shape=[
            jax.ShapeDtypeStruct(((n_side + 1) * rows, width), BF16),
            jax.ShapeDtypeStruct((n_side * rows, embeds.shape[1]), BF16),
        ],
        in_specs=[VMEM] * (n_side + 1),
        out_specs=[VMEM] * 2,
        compiler_params=params(8),
        name="split",
    )(weight, *blocks)
    pair = [pack, ring(pack, DEPTH, n_z, n_z // 2)]
    four = jnp.concatenate(pair + [ring(part, "core", 2, 1) for part in pair], axis=0)
    pair = jnp.concatenate(pair, axis=0)
    pair, four, line = lax.optimization_barrier((pair, four, line))
    far = move(pair, sizes, lambda core: {"z": 2 - 4 * core})
    lines = [line] + [turn(line, sizes, 1, -d) for d in range(1, n_side)]
    near = move(four, sizes, lambda core: {"z": 1 - 2 * core})
    table = left_map(probes.shape[1])

    def tile(rows_in, columns, dtype, start=None):
        return pl.pallas_call(
            functools.partial(tile_kernel, 256, 256, start is not None),
            out_shape=jax.ShapeDtypeStruct((n_side * rows, width), dtype),
            in_specs=[VMEM] * (2 + len(columns) + (start is not None)),
            out_specs=VMEM,
            compiler_params=params(16),
            name="tile",
        )(table, rows_in, *([] if start is None else [start]), *columns)

    begin = tile(line, [four], F32)
    near, far, lines, begin = lax.optimization_barrier((near, far, lines, begin))
    columns = [four, near, far, ring(near, "core", 2, 1), ring(far, "core", 2, 1)]

    back = {}
    for d in (0, 3, 1, 2):
        if d == 2:
            part = tile(lines[d], columns[3:], BF16, tile(lines[d], columns[:3], F32))
        elif d == 0:
            part = tile(line, columns[1:], F32, begin)
        else:
            part = tile(lines[d], columns, BF16)
        back[d] = part if d == 0 else turn(part, sizes, 1, d)

    total, weight_sum = pl.pallas_call(
        sum_rows_kernel,
        out_shape=[
            jax.ShapeDtypeStruct((n_side * rows, width), F32),
            jax.ShapeDtypeStruct((embeds.shape[1], width), F32),
        ],
        in_specs=[VMEM] * 4,
        out_specs=[VMEM] * 2,
        compiler_params=params(16),
        name="sum_rows",
    )(back[0], back[1], back[2], embeds_line)
    partial, own_rows, *other_rows = pl.pallas_call(
        last_rows_kernel,
        out_shape=[
            jax.ShapeDtypeStruct((embeds.shape[1], width), BF16),
            jax.ShapeDtypeStruct((rows, width), F32),
        ]
        + [jax.ShapeDtypeStruct((rows, width), BF16)] * (n_side - 1),
        in_specs=[VMEM] * 4,
        out_specs=[VMEM] * (n_side + 1),
        compiler_params=params(16),
        name="last_rows",
    )(total, weight_sum, back[3], embeds_line)
    arrived = [turn(other_rows[0], sizes, 0, 1)]

    n_plane = n_side * n_side
    pieces = exchange(partial.reshape(n_plane, -1, width), PLANE)
    pieces, arrived[0] = lax.optimization_barrier((pieces, arrived[0]))
    spread = sum_spread([pieces], n_z * 2, BF16)
    spread, other_rows[1], other_rows[2] = lax.optimization_barrier((spread, other_rows[1], other_rows[2]))
    pieces = exchange(spread, STACK)
    arrived += [turn(other_rows[d], sizes, 0, d + 1) for d in (1, 2)]
    grad_rows = pl.pallas_call(
        finish_rows_kernel,
        out_shape=jax.ShapeDtypeStruct((rows, width), F32),
        in_specs=[VMEM] * 4,
        out_specs=VMEM,
        compiler_params=params(16),
        name="finish_rows",
    )(own_rows, *arrived)
    pieces, grad_rows = lax.optimization_barrier((pieces, grad_rows))
    pieces = exchange(sum_spread([pieces], n_plane, BF16), PLANE)
    total_points = rows * n_plane * n_z * 2
    grad_weight = pieces.reshape(-1, width).astype(F32) * (1.0 / math.sqrt(total_points))
    return grad_rows, grad_weight


def solution(mesh):
    sizes = {"y": 4, "zh": 2, "core": 2, "zl": 4, "x": 4}
    fine = Mesh(mesh.devices.reshape(tuple(sizes[a] for a in ALL)), ALL)
    return jax.shard_map(
        functools.partial(shards, sizes),
        mesh=fine,
        in_specs=(P(ALL, None), P(), P(ALL), P(ALL, None), P(ALL, None)),
        out_specs=(P(ALL, None), P()),
        check_vma=False,
    )
```

```python
import functools
import math

import jax
import jax.numpy as jnp
import numpy as np
from jax import lax
from jax.experimental import pallas as pl
from jax.experimental.pallas import tpu as pltpu
from jax.sharding import Mesh, PartitionSpec as P

LOG2E = math.log2(math.e)
ROOT5 = math.sqrt(5.0)
ALL = ("y", "zh", "core", "zl", "x")
PLANE = ("y", "x")
STACK = ("zh", "core", "zl")
DEPTH = ("zh", "zl")
F32 = jnp.float32
BF16 = jnp.bfloat16
VMEM = pl.BlockSpec(memory_space=pltpu.VMEM)


def params(mib):
    return pltpu.CompilerParams(vmem_limit_bytes=mib << 20)


def dot_nt(a, b):
    return lax.dot_general(a, b, (((1,), (1,)), ((), ())), preferred_element_type=F32)


def dot_tn(a, b):
    return lax.dot_general(a, b, (((0,), (0,)), ((), ())), preferred_element_type=F32)


def pack_kernel(embeds, weight, solve, probes, probe_solves, packed, extended, weight_in, solve_in, probes_in, probe_solves_in, sems):
    rows, width = embeds.shape[0], weight.shape[1]
    embeds_in = extended.at[:, 128:]
    loads = [
        pltpu.make_async_copy(source, target, sems.at[k])
        for k, (source, target) in enumerate(
            (
                (weight, weight_in),
                (embeds, embeds_in),
                (probes, probes_in),
                (probe_solves, probe_solves_in),
                (solve, solve_in),
            )
        )
    ]
    for load in loads:
        load.start()
    for load in loads:
        load.wait()
    feats = jnp.dot(embeds_in[...], weight_in[...], preferred_element_type=F32).astype(BF16)
    wide = feats.astype(F32)
    sq = jnp.sum(wide * wide, axis=1, keepdims=True)
    sq_hi = sq.astype(BF16).astype(F32)
    sq_mid = (sq - sq_hi).astype(BF16).astype(F32)
    sq_lo = sq - sq_hi - sq_mid
    fold = math.sqrt(5.0 / 3.0 * ROOT5)
    scale = (2.0 * probes.shape[0]) ** (-0.5) * fold
    both = jnp.concatenate(
        [solve_in[...] * fold, probes_in[...] * -scale, probe_solves_in[...] * -scale, jnp.zeros((1, rows), F32)],
        axis=0,
    ).T
    hi = both.astype(BF16).astype(F32)
    lo = both - hi
    lane = lax.broadcasted_iota(jnp.int32, (rows, 32), 1)
    tail = jnp.where(lane == 0, sq_hi, jnp.where(lane == 1, sq_mid, jnp.where(lane == 2, sq_lo, 0.0)))
    tail = jnp.concatenate([hi, lo, hi, tail], axis=1).astype(BF16)
    extended[:, :128] = tail
    packed[:, :width] = feats
    packed[:, width:] = tail


def split_kernel(count, weight, *refs):
    line, embeds = refs[count:]
    rows, width = refs[0].shape[0], weight.shape[1]
    for k, ref in enumerate(refs[:count]):
        block = slice(k * rows, (k + 1) * rows)
        own = ref[:, 128:]
        line[block, :] = jnp.dot(own, weight[...], preferred_element_type=F32).astype(BF16)
        embeds[block, :] = own
    for k in range(0, count, 2):
        both = [ref[:, :64].astype(F32) for ref in refs[k : k + 2]]
        line[count * rows :, k * 64 : k * 64 + 128] = jnp.concatenate(both, axis=1).astype(BF16)


def left_map(count):
    source = np.zeros((32,), np.int32)
    sign = np.zeros((32,), np.float32)
    sign[0] = 1.0
    for k in range(count):
        source[1 + k], sign[1 + k] = 1 + count + k, -1.0
        source[1 + count + k], sign[1 + count + k] = 1 + k, -1.0
    table = np.zeros((2, 128, 128), np.float32)
    for half in range(2):
        for group, offset in ((0, 0), (1, 0), (2, 32)):
            for k in range(32):
                table[half, 64 * half + offset + source[k], 32 * group + k] = sign[k]
    return jnp.asarray(table, BF16)


def tile_kernel(sub, step, adds, table, rows_ref, *refs):
    *columns, out = refs
    if adds:
        begin, *columns = columns
    width = out.shape[1]
    block = rows_ref.shape[0] // 5
    rows = 4 * block
    u_rows = rows_ref[:rows, :]
    wide = u_rows.astype(F32)
    twice = (wide * -2.0).astype(BF16)
    left = []
    for k in range(4):
        start = k // 2 * 128
        fac = rows_ref[rows:, start : start + 128]
        left.append(jnp.dot(fac, table[k % 2], preferred_element_type=F32).astype(BF16))
    left = jnp.concatenate(left, axis=0)
    sq_rows = jnp.sum(wide * wide, axis=1, keepdims=True)
    lane = lax.broadcasted_iota(jnp.int32, (8, 128), 1)
    pick_cols = jnp.where((lane >= 96) & (lane < 99), 1.0, 0.0).astype(BF16)
    blocks = [slice(k, k + sub) for k in range(0, rows, sub)]
    acc = [begin[block, :] if adds else jnp.zeros((sub, width), F32) for block in blocks]
    total = [jnp.zeros((sub, 128), F32) for _ in blocks]
    work = [
        (ref, start, k)
        for ref in columns
        for start in range(0, ref.shape[0], step)
        for k in range(len(blocks))
    ]

    def products(ref, start, k):
        u_cols = ref[start : start + step, :width]
        right = ref[start : start + step, width:]
        sq_cols = dot_nt(pick_cols, right)[:1]
        return u_cols, sq_cols, dot_nt(twice[blocks[k]], u_cols), dot_nt(left[blocks[k]], right)

    ahead = products(*work[0])
    for index, (_, _, k) in enumerate(work):
        u_cols, sq_cols, cross, pair = ahead
        if index + 1 < len(work):
            ahead = products(*work[index + 1])
        d2 = jnp.maximum((sq_rows[blocks[k]] + sq_cols) + cross, 1e-30)
        dist = d2 * lax.rsqrt(d2)
        coupling = pair * ((dist + 1.0 / ROOT5) * jnp.exp2(dist * (-ROOT5 * LOG2E)))
        for j in range(0, step, 128):
            total[k] = total[k] + coupling[:, j : j + 128]
        acc[k] = acc[k] + jnp.dot(coupling.astype(BF16), u_cols, preferred_element_type=F32)
    for k, block in enumerate(blocks):
        row_total = jnp.sum(total[k], axis=1, keepdims=True)
        out[block, :] = (acc[k] - row_total * u_rows[block].astype(F32)).astype(out.dtype)


def sum_rows_kernel(a, b, c, embeds, total, weight):
    rows = a[...] + (b[...].astype(F32) + c[...].astype(F32))
    hi = rows.astype(BF16)
    lo = (rows - hi.astype(F32)).astype(BF16)
    total[...] = rows
    weight[...] = dot_tn(embeds[...], hi) + dot_tn(embeds[...], lo)


def last_rows_kernel(total, weight, last, embeds, partial, own, *others):
    rows = own.shape[0]
    partial[...] = (weight[...] + dot_tn(embeds[...], last[...])).astype(BF16)
    own[...] = total[:rows] + last[:rows].astype(F32)
    for k, ref in enumerate(others):
        block = slice((k + 1) * rows, (k + 2) * rows)
        ref[...] = (total[block] + last[block].astype(F32)).astype(BF16)


def finish_rows_kernel(own, b, c, d, grad_rows):
    grad_rows[...] = (own[...] + b[...].astype(F32)) + (c[...].astype(F32) + d[...].astype(F32))


def sum_spread_kernel(*refs):
    *parts, out = refs
    total = None
    for ref in parts:
        for k in range(ref.shape[0]):
            term = ref[k].astype(F32)
            total = term if total is None else total + term
    low = total.astype(out.dtype)
    for k in range(out.shape[0]):
        out[k] = low


def sum_spread(parts, copies, dtype):
    return pl.pallas_call(
        sum_spread_kernel,
        out_shape=jax.ShapeDtypeStruct((copies,) + parts[0].shape[1:], dtype),
        in_specs=[VMEM] * len(parts),
        out_specs=VMEM,
        compiler_params=params(16),
        name="sum_spread",
    )(*parts)


def ring(array, axis, size, shift):
    return lax.ppermute(array, axis, [(i, (i + shift) % size) for i in range(size)])


def move(array, sizes, where):
    dims = [sizes[a] for a in ALL]
    perm = []
    for source in range(math.prod(dims)):
        place = dict(zip(ALL, (int(i) for i in np.unravel_index(source, dims))))
        for axis, shift in where(place["core"]).items():
            if axis == "z":
                z = (place["zh"] * sizes["zl"] + place["zl"] + shift) % (sizes["zh"] * sizes["zl"])
                place["zh"], place["zl"] = divmod(z, sizes["zl"])
            else:
                place[axis] = (place[axis] + shift) % sizes[axis]
        perm.append((source, int(np.ravel_multi_index([place[a] for a in ALL], dims))))
    return lax.ppermute(array, ALL, perm)


def turn(array, sizes, stage, shift):
    return move(array, sizes, lambda core: {"y" if (core + stage) % 2 == 0 else "x": shift})


def exchange(array, axes):
    return lax.all_to_all(array, axes, split_axis=0, concat_axis=0, tiled=True)


def shards(sizes, embeds, weight, solve, probes, probe_solves):
    rows, width = embeds.shape[0], weight.shape[1]
    n_side, n_z = sizes["x"], sizes["zh"] * sizes["zl"]
    pack, extended = pl.pallas_call(
        pack_kernel,
        out_shape=[
            jax.ShapeDtypeStruct((rows, width + 128), BF16),
            jax.ShapeDtypeStruct((rows, 128 + embeds.shape[1]), BF16),
        ],
        in_specs=[pl.BlockSpec(memory_space=pltpu.HBM)] * 5,
        out_specs=[VMEM] * 2,
        scratch_shapes=[
            pltpu.VMEM(weight.shape, BF16),
            pltpu.VMEM((1, rows), F32),
            pltpu.VMEM(probes.shape[::-1], F32),
            pltpu.VMEM(probes.shape[::-1], F32),
            pltpu.SemaphoreType.DMA((5,)),
        ],
        compiler_params=params(48),
        name="pack",
    )(*(pltpu.with_memory_space_constraint(a, pltpu.HBM) for a in (embeds, weight, solve[None, :], probes.T, probe_solves.T)))

    blocks = [extended] + [turn(extended, sizes, 0, -d) for d in range(1, n_side)]
    line, embeds_line = pl.pallas_call(
        functools.partial(split_kernel, n_side),
        out_shape=[
            jax.ShapeDtypeStruct(((n_side + 1) * rows, width), BF16),
            jax.ShapeDtypeStruct((n_side * rows, embeds.shape[1]), BF16),
        ],
        in_specs=[VMEM] * (n_side + 1),
        out_specs=[VMEM] * 2,
        compiler_params=params(8),
        name="split",
    )(weight, *blocks)
    pair = [pack, ring(pack, DEPTH, n_z, n_z // 2)]
    four = jnp.concatenate(pair + [ring(part, "core", 2, 1) for part in pair], axis=0)
    pair = jnp.concatenate(pair, axis=0)
    pair, four, line = lax.optimization_barrier((pair, four, line))
    far = move(pair, sizes, lambda core: {"z": 2 - 4 * core})
    lines = [line] + [turn(line, sizes, 1, -d) for d in range(1, n_side)]
    near = move(four, sizes, lambda core: {"z": 1 - 2 * core})
    table = left_map(probes.shape[1])

    def tile(rows_in, columns, dtype, start=None):
        return pl.pallas_call(
            functools.partial(tile_kernel, 256, 256, start is not None),
            out_shape=jax.ShapeDtypeStruct((n_side * rows, width), dtype),
            in_specs=[VMEM] * (2 + len(columns) + (start is not None)),
            out_specs=VMEM,
            compiler_params=params(16),
            name="tile",
        )(table, rows_in, *([] if start is None else [start]), *columns)

    begin = tile(line, [four], F32)
    halves = [near[: 2 * rows], near[2 * rows :]]
    columns = [four, near, ring(halves[0], "core", 2, 1), far]
    columns, lines, begin, halves = lax.optimization_barrier((columns, lines, begin, halves))
    early = len(columns)
    columns += [ring(part, "core", 2, 1) for part in (halves[1], far)]

    back = {}
    for d in (0, 3, 1, 2):
        if d == 2:
            part = tile(lines[d], columns[early:], BF16, tile(lines[d], columns[:early], F32))
        elif d == 0:
            part = tile(line, columns[1:], F32, begin)
        else:
            part = tile(lines[d], columns, BF16)
        back[d] = part if d == 0 else turn(part, sizes, 1, d)

    total, weight_sum = pl.pallas_call(
        sum_rows_kernel,
        out_shape=[
            jax.ShapeDtypeStruct((n_side * rows, width), F32),
            jax.ShapeDtypeStruct((embeds.shape[1], width), F32),
        ],
        in_specs=[VMEM] * 4,
        out_specs=[VMEM] * 2,
        compiler_params=params(16),
        name="sum_rows",
    )(back[0], back[1], back[2], embeds_line)
    partial, own_rows, *other_rows = pl.pallas_call(
        last_rows_kernel,
        out_shape=[
            jax.ShapeDtypeStruct((embeds.shape[1], width), BF16),
            jax.ShapeDtypeStruct((rows, width), F32),
        ]
        + [jax.ShapeDtypeStruct((rows, width), BF16)] * (n_side - 1),
        in_specs=[VMEM] * 4,
        out_specs=[VMEM] * (n_side + 1),
        compiler_params=params(16),
        name="last_rows",
    )(total, weight_sum, back[3], embeds_line)
    n_plane = n_side * n_side
    pieces = exchange(partial.reshape(n_plane, -1, width), PLANE)
    spread = sum_spread([pieces], n_z * 2, BF16)
    spread, other_rows = lax.optimization_barrier((spread, other_rows))
    pieces = exchange(spread, STACK)
    arrived = [turn(block, sizes, 0, d + 1) for d, block in enumerate(other_rows)]
    grad_rows = pl.pallas_call(
        finish_rows_kernel,
        out_shape=jax.ShapeDtypeStruct((rows, width), F32),
        in_specs=[VMEM] * 4,
        out_specs=VMEM,
        compiler_params=params(16),
        name="finish_rows",
    )(own_rows, *arrived)
    pieces, grad_rows = lax.optimization_barrier((pieces, grad_rows))
    pieces = exchange(sum_spread([pieces], n_plane, BF16), PLANE)
    total_points = rows * n_plane * n_z * 2
    grad_weight = pieces.reshape(-1, width).astype(F32) * (1.0 / math.sqrt(total_points))
    return grad_rows, grad_weight


def solution(mesh):
    sizes = {"y": 4, "zh": 2, "core": 2, "zl": 4, "x": 4}
    fine = Mesh(mesh.devices.reshape(tuple(sizes[a] for a in ALL)), ALL)
    return jax.shard_map(
        functools.partial(shards, sizes),
        mesh=fine,
        in_specs=(P(ALL, None), P(), P(ALL), P(ALL, None), P(ALL, None)),
        out_specs=(P(ALL, None), P()),
        check_vma=False,
    )
```

```python
import functools
import math

import jax
import jax.numpy as jnp
import numpy as np
from jax import lax
from jax.experimental import pallas as pl
from jax.experimental.pallas import tpu as pltpu
from jax.sharding import Mesh, PartitionSpec as P

LOG2E = math.log2(math.e)
ROOT5 = math.sqrt(5.0)
ALL = ("y", "zh", "core", "zl", "x")
PLANE = ("y", "x")
STACK = ("zh", "core", "zl")
DEPTH = ("zh", "zl")
F32 = jnp.float32
BF16 = jnp.bfloat16
VMEM = pl.BlockSpec(memory_space=pltpu.VMEM)


def params(mib):
    return pltpu.CompilerParams(vmem_limit_bytes=mib << 20)


def dot_nt(a, b):
    return lax.dot_general(a, b, (((1,), (1,)), ((), ())), preferred_element_type=F32)


def dot_tn(a, b):
    return lax.dot_general(a, b, (((0,), (0,)), ((), ())), preferred_element_type=F32)


def pack_kernel(embeds, weight, solve, probes, probe_solves, packed, extended, weight_in, solve_in, probes_in, probe_solves_in, sems):
    rows, width = embeds.shape[0], weight.shape[1]
    embeds_in = extended.at[:, 128:]
    loads = [
        pltpu.make_async_copy(source, target, sems.at[k])
        for k, (source, target) in enumerate(
            (
                (weight, weight_in),
                (embeds, embeds_in),
                (probes, probes_in),
                (probe_solves, probe_solves_in),
                (solve, solve_in),
            )
        )
    ]
    for load in loads:
        load.start()
    for load in loads:
        load.wait()
    feats = jnp.dot(embeds_in[...], weight_in[...], preferred_element_type=F32).astype(BF16)
    wide = feats.astype(F32)
    sq = jnp.sum(wide * wide, axis=1, keepdims=True)
    sq_hi = sq.astype(BF16).astype(F32)
    sq_mid = (sq - sq_hi).astype(BF16).astype(F32)
    sq_lo = sq - sq_hi - sq_mid
    fold = math.sqrt(5.0 / 3.0 * ROOT5)
    scale = (2.0 * probes.shape[0]) ** (-0.5) * fold
    both = jnp.concatenate(
        [solve_in[...] * fold, probes_in[...] * -scale, probe_solves_in[...] * -scale, jnp.zeros((1, rows), F32)],
        axis=0,
    ).T
    hi = both.astype(BF16).astype(F32)
    lo = both - hi
    lane = lax.broadcasted_iota(jnp.int32, (rows, 32), 1)
    tail = jnp.where(lane == 0, sq_hi, jnp.where(lane == 1, sq_mid, jnp.where(lane == 2, sq_lo, 0.0)))
    tail = jnp.concatenate([hi, lo, hi, tail], axis=1).astype(BF16)
    extended[:, :128] = tail
    packed[:, :width] = feats
    packed[:, width:] = tail


def split_kernel(count, weight, *refs):
    line, embeds = refs[count:]
    rows, width = refs[0].shape[0], weight.shape[1]
    for k, ref in enumerate(refs[:count]):
        block = slice(k * rows, (k + 1) * rows)
        own = ref[:, 128:]
        line[block, :] = jnp.dot(own, weight[...], preferred_element_type=F32).astype(BF16)
        embeds[block, :] = own
    for k in range(0, count, 2):
        both = [ref[:, :64].astype(F32) for ref in refs[k : k + 2]]
        line[count * rows :, k * 64 : k * 64 + 128] = jnp.concatenate(both, axis=1).astype(BF16)


def left_map(count):
    source = np.zeros((32,), np.int32)
    sign = np.zeros((32,), np.float32)
    sign[0] = 1.0
    for k in range(count):
        source[1 + k], sign[1 + k] = 1 + count + k, -1.0
        source[1 + count + k], sign[1 + count + k] = 1 + k, -1.0
    table = np.zeros((2, 128, 128), np.float32)
    for half in range(2):
        for group, offset in ((0, 0), (1, 0), (2, 32)):
            for k in range(32):
                table[half, 64 * half + offset + source[k], 32 * group + k] = sign[k]
    return jnp.asarray(table, BF16)


def tile_kernel(sub, step, adds, table, rows_ref, *refs):
    *columns, out = refs
    if adds:
        begin, *columns = columns
    width = out.shape[1]
    block = rows_ref.shape[0] // 5
    rows = 4 * block
    u_rows = rows_ref[:rows, :]
    wide = u_rows.astype(F32)
    twice = (wide * -2.0).astype(BF16)
    left = []
    for k in range(4):
        start = k // 2 * 128
        fac = rows_ref[rows:, start : start + 128]
        left.append(jnp.dot(fac, table[k % 2], preferred_element_type=F32).astype(BF16))
    left = jnp.concatenate(left, axis=0)
    sq_rows = jnp.sum(wide * wide, axis=1, keepdims=True)
    lane = lax.broadcasted_iota(jnp.int32, (8, 128), 1)
    pick_cols = jnp.where((lane >= 96) & (lane < 99), 1.0, 0.0).astype(BF16)
    blocks = [slice(k, k + sub) for k in range(0, rows, sub)]
    acc = [begin[block, :] if adds else jnp.zeros((sub, width), F32) for block in blocks]
    total = [jnp.zeros((sub, 128), F32) for _ in blocks]
    work = [
        (ref, start, k)
        for ref in columns
        for start in range(0, ref.shape[0], step)
        for k in range(len(blocks))
    ]

    def products(ref, start, k):
        u_cols = ref[start : start + step, :width]
        right = ref[start : start + step, width:]
        sq_cols = dot_nt(pick_cols, right)[:1]
        return u_cols, sq_cols, dot_nt(twice[blocks[k]], u_cols), dot_nt(left[blocks[k]], right)

    ahead = products(*work[0])
    for index, (_, _, k) in enumerate(work):
        u_cols, sq_cols, cross, pair = ahead
        if index + 1 < len(work):
            ahead = products(*work[index + 1])
        d2 = jnp.maximum((sq_rows[blocks[k]] + sq_cols) + cross, 1e-30)
        dist = d2 * lax.rsqrt(d2)
        coupling = pair * ((dist + 1.0 / ROOT5) * jnp.exp2(dist * (-ROOT5 * LOG2E)))
        for j in range(0, step, 128):
            total[k] = total[k] + coupling[:, j : j + 128]
        acc[k] = acc[k] + jnp.dot(coupling.astype(BF16), u_cols, preferred_element_type=F32)
    for k, block in enumerate(blocks):
        row_total = jnp.sum(total[k], axis=1, keepdims=True)
        out[block, :] = (acc[k] - row_total * u_rows[block].astype(F32)).astype(out.dtype)


def sum_rows_kernel(a, b, c, embeds, total, weight):
    rows = a[...] + (b[...].astype(F32) + c[...].astype(F32))
    hi = rows.astype(BF16)
    lo = (rows - hi.astype(F32)).astype(BF16)
    total[...] = rows
    weight[...] = dot_tn(embeds[...], hi) + dot_tn(embeds[...], lo)


def last_rows_kernel(total, weight, last, embeds, partial, own, *others):
    rows = own.shape[0]
    partial[...] = (weight[...] + dot_tn(embeds[...], last[...])).astype(BF16)
    own[...] = total[:rows] + last[:rows].astype(F32)
    for k, ref in enumerate(others):
        block = slice((k + 1) * rows, (k + 2) * rows)
        ref[...] = (total[block] + last[block].astype(F32)).astype(BF16)


def finish_rows_kernel(own, b, c, d, grad_rows):
    grad_rows[...] = (own[...] + b[...].astype(F32)) + (c[...].astype(F32) + d[...].astype(F32))


def sum_spread_kernel(*refs):
    *parts, out = refs
    total = None
    for ref in parts:
        for k in range(ref.shape[0]):
            term = ref[k].astype(F32)
            total = term if total is None else total + term
    low = total.astype(out.dtype)
    for k in range(out.shape[0]):
        out[k] = low


def sum_spread(parts, copies, dtype):
    return pl.pallas_call(
        sum_spread_kernel,
        out_shape=jax.ShapeDtypeStruct((copies,) + parts[0].shape[1:], dtype),
        in_specs=[VMEM] * len(parts),
        out_specs=VMEM,
        compiler_params=params(16),
        name="sum_spread",
    )(*parts)


def ring(array, axis, size, shift):
    return lax.ppermute(array, axis, [(i, (i + shift) % size) for i in range(size)])


def move(array, sizes, where):
    dims = [sizes[a] for a in ALL]
    perm = []
    for source in range(math.prod(dims)):
        place = dict(zip(ALL, (int(i) for i in np.unravel_index(source, dims))))
        for axis, shift in where(place["core"]).items():
            if axis == "z":
                z = (place["zh"] * sizes["zl"] + place["zl"] + shift) % (sizes["zh"] * sizes["zl"])
                place["zh"], place["zl"] = divmod(z, sizes["zl"])
            else:
                place[axis] = (place[axis] + shift) % sizes[axis]
        perm.append((source, int(np.ravel_multi_index([place[a] for a in ALL], dims))))
    return lax.ppermute(array, ALL, perm)


def turn(array, sizes, stage, shift):
    return move(array, sizes, lambda core: {"y" if (core + stage) % 2 == 0 else "x": shift})


def exchange(array, axes):
    return lax.all_to_all(array, axes, split_axis=0, concat_axis=0, tiled=True)


def shards(sizes, embeds, weight, solve, probes, probe_solves):
    rows, width = embeds.shape[0], weight.shape[1]
    n_side, n_z = sizes["x"], sizes["zh"] * sizes["zl"]
    pack, extended = pl.pallas_call(
        pack_kernel,
        out_shape=[
            jax.ShapeDtypeStruct((rows, width + 128), BF16),
            jax.ShapeDtypeStruct((rows, 128 + embeds.shape[1]), BF16),
        ],
        in_specs=[pl.BlockSpec(memory_space=pltpu.HBM)] * 5,
        out_specs=[VMEM] * 2,
        scratch_shapes=[
            pltpu.VMEM(weight.shape, BF16),
            pltpu.VMEM((1, rows), F32),
            pltpu.VMEM(probes.shape[::-1], F32),
            pltpu.VMEM(probes.shape[::-1], F32),
            pltpu.SemaphoreType.DMA((5,)),
        ],
        compiler_params=params(48),
        name="pack",
    )(*(pltpu.with_memory_space_constraint(a, pltpu.HBM) for a in (embeds, weight, solve[None, :], probes.T, probe_solves.T)))

    blocks = [extended] + [turn(extended, sizes, 0, -d) for d in range(1, n_side)]
    line, embeds_line = pl.pallas_call(
        functools.partial(split_kernel, n_side),
        out_shape=[
            jax.ShapeDtypeStruct(((n_side + 1) * rows, width), BF16),
            jax.ShapeDtypeStruct((n_side * rows, embeds.shape[1]), BF16),
        ],
        in_specs=[VMEM] * (n_side + 1),
        out_specs=[VMEM] * 2,
        compiler_params=params(8),
        name="split",
    )(weight, *blocks)
    pair = [pack, ring(pack, DEPTH, n_z, n_z // 2)]
    four = jnp.concatenate(pair + [ring(part, "core", 2, 1) for part in pair], axis=0)
    pair = jnp.concatenate(pair, axis=0)
    pair, four, line = lax.optimization_barrier((pair, four, line))
    far = move(pair, sizes, lambda core: {"z": 2 - 4 * core})
    lines = [line] + [turn(line, sizes, 1, -d) for d in range(1, n_side)]
    near = move(four, sizes, lambda core: {"z": 1 - 2 * core})
    table = left_map(probes.shape[1])

    def tile(rows_in, columns, dtype, start=None):
        return pl.pallas_call(
            functools.partial(tile_kernel, 256, 256, start is not None),
            out_shape=jax.ShapeDtypeStruct((n_side * rows, width), dtype),
            in_specs=[VMEM] * (2 + len(columns) + (start is not None)),
            out_specs=VMEM,
            compiler_params=params(16),
            name="tile",
        )(table, rows_in, *([] if start is None else [start]), *columns)

    first = n_side - 1
    begin = tile(lines[first], [four, near], F32)
    halves = [near[: 2 * rows], near[2 * rows :]]
    columns = [four, near, ring(halves[0], "core", 2, 1), far]
    columns, lines, begin, halves = lax.optimization_barrier((columns, lines, begin, halves))
    early = len(columns)
    columns += [ring(part, "core", 2, 1) for part in (halves[1], columns[-1])]

    back = {}
    for d in range(n_side):
        if d == first:
            part = tile(lines[d], columns[early:], BF16, tile(lines[d], columns[2:early], F32, begin))
        else:
            part = tile(lines[d], columns, BF16 if d else F32)
        back[d] = turn(part, sizes, 1, d) if d else part

    total, weight_sum = pl.pallas_call(
        sum_rows_kernel,
        out_shape=[
            jax.ShapeDtypeStruct((n_side * rows, width), F32),
            jax.ShapeDtypeStruct((embeds.shape[1], width), F32),
        ],
        in_specs=[VMEM] * 4,
        out_specs=[VMEM] * 2,
        compiler_params=params(16),
        name="sum_rows",
    )(back[0], back[2], back[3], embeds_line)
    partial, own_rows, *other_rows = pl.pallas_call(
        last_rows_kernel,
        out_shape=[
            jax.ShapeDtypeStruct((embeds.shape[1], width), BF16),
            jax.ShapeDtypeStruct((rows, width), F32),
        ]
        + [jax.ShapeDtypeStruct((rows, width), BF16)] * (n_side - 1),
        in_specs=[VMEM] * 4,
        out_specs=[VMEM] * (n_side + 1),
        compiler_params=params(16),
        name="last_rows",
    )(total, weight_sum, back[1], embeds_line)
    n_plane = n_side * n_side
    pieces = exchange(partial.reshape(n_plane, -1, width), PLANE)
    spread = sum_spread([pieces], n_z * 2, BF16)
    spread, other_rows = lax.optimization_barrier((spread, other_rows))
    pieces = exchange(spread, STACK)
    arrived = [turn(block, sizes, 0, d + 1) for d, block in enumerate(other_rows)]
    grad_rows = pl.pallas_call(
        finish_rows_kernel,
        out_shape=jax.ShapeDtypeStruct((rows, width), F32),
        in_specs=[VMEM] * 4,
        out_specs=VMEM,
        compiler_params=params(16),
        name="finish_rows",
    )(own_rows, *arrived)
    pieces, grad_rows = lax.optimization_barrier((pieces, grad_rows))
    pieces = exchange(sum_spread([pieces], n_plane, BF16), PLANE)
    total_points = rows * n_plane * n_z * 2
    grad_weight = pieces.reshape(-1, width).astype(F32) * (1.0 / math.sqrt(total_points))
    return grad_rows, grad_weight


def solution(mesh):
    sizes = {"y": 4, "zh": 2, "core": 2, "zl": 4, "x": 4}
    fine = Mesh(mesh.devices.reshape(tuple(sizes[a] for a in ALL)), ALL)
    return jax.shard_map(
        functools.partial(shards, sizes),
        mesh=fine,
        in_specs=(P(ALL, None), P(), P(ALL), P(ALL, None), P(ALL, None)),
        out_specs=(P(ALL, None), P()),
        check_vma=False,
    )
```

```python
import functools
import math

import jax
import jax.numpy as jnp
import numpy as np
from jax import lax
from jax.experimental import pallas as pl
from jax.experimental.pallas import tpu as pltpu
from jax.sharding import Mesh, PartitionSpec as P

LOG2E = math.log2(math.e)
ROOT5 = math.sqrt(5.0)
ALL = ("y", "zh", "core", "zl", "x")
PLANE = ("y", "x")
STACK = ("zh", "core", "zl")
DEPTH = ("zh", "zl")
F32 = jnp.float32
BF16 = jnp.bfloat16
VMEM = pl.BlockSpec(memory_space=pltpu.VMEM)


def params(mib):
    return pltpu.CompilerParams(vmem_limit_bytes=mib << 20)


def dot_nt(a, b):
    return lax.dot_general(a, b, (((1,), (1,)), ((), ())), preferred_element_type=F32)


def dot_tn(a, b):
    return lax.dot_general(a, b, (((0,), (0,)), ((), ())), preferred_element_type=F32)


def pack_kernel(embeds, weight, solve, probes, probe_solves, packed, extended, weight_in, solve_in, probes_in, probe_solves_in, sems):
    rows, width = embeds.shape[0], weight.shape[1]
    embeds_in = extended.at[:, 128:]
    loads = [
        pltpu.make_async_copy(source, target, sems.at[k])
        for k, (source, target) in enumerate(
            (
                (weight, weight_in),
                (embeds, embeds_in),
                (probes, probes_in),
                (probe_solves, probe_solves_in),
                (solve, solve_in),
            )
        )
    ]
    for load in loads:
        load.start()
    for load in loads:
        load.wait()
    feats = jnp.dot(embeds_in[...], weight_in[...], preferred_element_type=F32).astype(BF16)
    wide = feats.astype(F32)
    sq = jnp.sum(wide * wide, axis=1, keepdims=True)
    sq_hi = sq.astype(BF16).astype(F32)
    sq_mid = (sq - sq_hi).astype(BF16).astype(F32)
    sq_lo = sq - sq_hi - sq_mid
    fold = math.sqrt(5.0 / 3.0 * ROOT5)
    scale = (2.0 * probes.shape[0]) ** (-0.5) * fold
    both = jnp.concatenate(
        [solve_in[...] * fold, probes_in[...] * -scale, probe_solves_in[...] * -scale, jnp.zeros((1, rows), F32)],
        axis=0,
    ).T
    hi = both.astype(BF16).astype(F32)
    lo = both - hi
    lane = lax.broadcasted_iota(jnp.int32, (rows, 32), 1)
    tail = jnp.where(lane == 0, sq_hi, jnp.where(lane == 1, sq_mid, jnp.where(lane == 2, sq_lo, 0.0)))
    tail = jnp.concatenate([hi, lo, hi, tail], axis=1).astype(BF16)
    extended[:, :128] = tail
    packed[:, :width] = feats
    packed[:, width:] = tail


def split_kernel(count, weight, *refs):
    line, embeds = refs[count:]
    rows, width = refs[0].shape[0], weight.shape[1]
    for k, ref in enumerate(refs[:count]):
        block = slice(k * rows, (k + 1) * rows)
        own = ref[:, 128:]
        line[block, :] = jnp.dot(own, weight[...], preferred_element_type=F32).astype(BF16)
        embeds[block, :] = own
    for k in range(0, count, 2):
        both = [ref[:, :64].astype(F32) for ref in refs[k : k + 2]]
        line[count * rows :, k * 64 : k * 64 + 128] = jnp.concatenate(both, axis=1).astype(BF16)


def left_map(count):
    source = np.zeros((32,), np.int32)
    sign = np.zeros((32,), np.float32)
    sign[0] = 1.0
    for k in range(count):
        source[1 + k], sign[1 + k] = 1 + count + k, -1.0
        source[1 + count + k], sign[1 + count + k] = 1 + k, -1.0
    table = np.zeros((2, 128, 128), np.float32)
    for half in range(2):
        for group, offset in ((0, 0), (1, 0), (2, 32)):
            for k in range(32):
                table[half, 64 * half + offset + source[k], 32 * group + k] = sign[k]
    return jnp.asarray(table, BF16)


def tile_kernel(sub, step, adds, table, rows_ref, *refs):
    *columns, out = refs
    if adds:
        begin, *columns = columns
    width = out.shape[1]
    block = rows_ref.shape[0] // 5
    rows = 4 * block
    u_rows = rows_ref[:rows, :]
    wide = u_rows.astype(F32)
    twice = (wide * -2.0).astype(BF16)
    left = []
    for k in range(4):
        start = k // 2 * 128
        fac = rows_ref[rows:, start : start + 128]
        left.append(jnp.dot(fac, table[k % 2], preferred_element_type=F32).astype(BF16))
    left = jnp.concatenate(left, axis=0)
    sq_rows = jnp.sum(wide * wide, axis=1, keepdims=True)
    lane = lax.broadcasted_iota(jnp.int32, (8, 128), 1)
    pick_cols = jnp.where((lane >= 96) & (lane < 99), 1.0, 0.0).astype(BF16)
    blocks = [slice(k, k + sub) for k in range(0, rows, sub)]
    acc = [begin[block, :] if adds else jnp.zeros((sub, width), F32) for block in blocks]
    total = [jnp.zeros((sub, 128), F32) for _ in blocks]
    work = [
        (ref, start, k)
        for ref in columns
        for start in range(0, ref.shape[0], step)
        for k in range(len(blocks))
    ]

    def products(ref, start, k):
        u_cols = ref[start : start + step, :width]
        right = ref[start : start + step, width:]
        sq_cols = dot_nt(pick_cols, right)[:1]
        return u_cols, sq_cols, dot_nt(twice[blocks[k]], u_cols), dot_nt(left[blocks[k]], right)

    ahead = products(*work[0])
    for index, (_, _, k) in enumerate(work):
        u_cols, sq_cols, cross, pair = ahead
        if index + 1 < len(work):
            ahead = products(*work[index + 1])
        d2 = jnp.maximum((sq_rows[blocks[k]] + sq_cols) + cross, 1e-30)
        dist = d2 * lax.rsqrt(d2)
        coupling = pair * ((dist + 1.0 / ROOT5) * jnp.exp2(dist * (-ROOT5 * LOG2E)))
        for j in range(0, step, 128):
            total[k] = total[k] + coupling[:, j : j + 128]
        acc[k] = acc[k] + jnp.dot(coupling.astype(BF16), u_cols, preferred_element_type=F32)
    for k, block in enumerate(blocks):
        row_total = jnp.sum(total[k], axis=1, keepdims=True)
        out[block, :] = (acc[k] - row_total * u_rows[block].astype(F32)).astype(out.dtype)


def sum_rows_kernel(a, b, c, embeds, total, weight):
    rows = a[...] + (b[...].astype(F32) + c[...].astype(F32))
    hi = rows.astype(BF16)
    lo = (rows - hi.astype(F32)).astype(BF16)
    total[...] = rows
    weight[...] = dot_tn(embeds[...], hi) + dot_tn(embeds[...], lo)


def last_rows_kernel(total, weight, last, embeds, partial, own, *others):
    rows = own.shape[0]
    partial[...] = (weight[...] + dot_tn(embeds[...], last[...])).astype(BF16)
    own[...] = total[:rows] + last[:rows].astype(F32)
    for k, ref in enumerate(others):
        block = slice((k + 1) * rows, (k + 2) * rows)
        ref[...] = (total[block] + last[block].astype(F32)).astype(BF16)


def finish_rows_kernel(own, b, c, d, grad_rows):
    grad_rows[...] = (own[...] + b[...].astype(F32)) + (c[...].astype(F32) + d[...].astype(F32))


def sum_spread_kernel(*refs):
    *parts, out = refs
    total = None
    for ref in parts:
        for k in range(ref.shape[0]):
            term = ref[k].astype(F32)
            total = term if total is None else total + term
    low = total.astype(out.dtype)
    for k in range(out.shape[0]):
        out[k] = low


def sum_spread(parts, copies, dtype):
    return pl.pallas_call(
        sum_spread_kernel,
        out_shape=jax.ShapeDtypeStruct((copies,) + parts[0].shape[1:], dtype),
        in_specs=[VMEM] * len(parts),
        out_specs=VMEM,
        compiler_params=params(16),
        name="sum_spread",
    )(*parts)


def ring(array, axis, size, shift):
    return lax.ppermute(array, axis, [(i, (i + shift) % size) for i in range(size)])


def move(array, sizes, where):
    dims = [sizes[a] for a in ALL]
    perm = []
    for source in range(math.prod(dims)):
        place = dict(zip(ALL, (int(i) for i in np.unravel_index(source, dims))))
        for axis, shift in where(place["core"]).items():
            if axis == "z":
                z = (place["zh"] * sizes["zl"] + place["zl"] + shift) % (sizes["zh"] * sizes["zl"])
                place["zh"], place["zl"] = divmod(z, sizes["zl"])
            else:
                place[axis] = (place[axis] + shift) % sizes[axis]
        perm.append((source, int(np.ravel_multi_index([place[a] for a in ALL], dims))))
    return lax.ppermute(array, ALL, perm)


def turn(array, sizes, stage, shift):
    return move(array, sizes, lambda core: {"y" if (core + stage) % 2 == 0 else "x": shift})


def exchange(array, axes):
    return lax.all_to_all(array, axes, split_axis=0, concat_axis=0, tiled=True)


def shards(sizes, embeds, weight, solve, probes, probe_solves):
    rows, width = embeds.shape[0], weight.shape[1]
    n_side, n_z = sizes["x"], sizes["zh"] * sizes["zl"]
    pack, extended = pl.pallas_call(
        pack_kernel,
        out_shape=[
            jax.ShapeDtypeStruct((rows, width + 128), BF16),
            jax.ShapeDtypeStruct((rows, 128 + embeds.shape[1]), BF16),
        ],
        in_specs=[pl.BlockSpec(memory_space=pltpu.HBM)] * 5,
        out_specs=[VMEM] * 2,
        scratch_shapes=[
            pltpu.VMEM(weight.shape, BF16),
            pltpu.VMEM((1, rows), F32),
            pltpu.VMEM(probes.shape[::-1], F32),
            pltpu.VMEM(probes.shape[::-1], F32),
            pltpu.SemaphoreType.DMA((5,)),
        ],
        compiler_params=params(48),
        name="pack",
    )(*(pltpu.with_memory_space_constraint(a, pltpu.HBM) for a in (embeds, weight, solve[None, :], probes.T, probe_solves.T)))

    blocks = [extended] + [turn(extended, sizes, 0, -d) for d in range(1, n_side)]
    line, embeds_line = pl.pallas_call(
        functools.partial(split_kernel, n_side),
        out_shape=[
            jax.ShapeDtypeStruct(((n_side + 1) * rows, width), BF16),
            jax.ShapeDtypeStruct((n_side * rows, embeds.shape[1]), BF16),
        ],
        in_specs=[VMEM] * (n_side + 1),
        out_specs=[VMEM] * 2,
        compiler_params=params(8),
        name="split",
    )(weight, *blocks)
    pair = [pack, ring(pack, DEPTH, n_z, n_z // 2)]
    four = jnp.concatenate(pair + [ring(part, "core", 2, 1) for part in pair], axis=0)
    pair = jnp.concatenate(pair, axis=0)
    pair, four, line = lax.optimization_barrier((pair, four, line))
    far = move(pair, sizes, lambda core: {"z": 2 - 4 * core})
    lines = [line] + [turn(line, sizes, 1, -d) for d in range(1, n_side)]
    near = move(four, sizes, lambda core: {"z": 1 - 2 * core})
    table = left_map(probes.shape[1])

    def tile(rows_in, columns, dtype, start=None):
        return pl.pallas_call(
            functools.partial(tile_kernel, 256, 256, start is not None),
            out_shape=jax.ShapeDtypeStruct((n_side * rows, width), dtype),
            in_specs=[VMEM] * (2 + len(columns) + (start is not None)),
            out_specs=VMEM,
            compiler_params=params(16),
            name="tile",
        )(table, rows_in, *([] if start is None else [start]), *columns)

    first = n_side - 1
    begin = {d: tile(lines[d], [four, near], F32) for d in (first, first - 1)}
    halves = [near[: 2 * rows], near[2 * rows :]]
    columns = [four, near, ring(halves[0], "core", 2, 1), far]
    columns, lines, begin, halves = lax.optimization_barrier((columns, lines, begin, halves))
    early = len(columns)
    columns += [ring(part, "core", 2, 1) for part in (halves[1], columns[-1])]

    back = {}
    for d in range(n_side):
        if d == first:
            part = tile(lines[d], columns[early:], BF16, tile(lines[d], columns[2:early], F32, begin[d]))
        elif d in begin:
            part = tile(lines[d], columns[2:], BF16, begin[d])
        else:
            part = tile(lines[d], columns, BF16 if d else F32)
        back[d] = turn(part, sizes, 1, d) if d else part

    total, weight_sum = pl.pallas_call(
        sum_rows_kernel,
        out_shape=[
            jax.ShapeDtypeStruct((n_side * rows, width), F32),
            jax.ShapeDtypeStruct((embeds.shape[1], width), F32),
        ],
        in_specs=[VMEM] * 4,
        out_specs=[VMEM] * 2,
        compiler_params=params(16),
        name="sum_rows",
    )(back[0], back[2], back[3], embeds_line)
    partial, own_rows, *other_rows = pl.pallas_call(
        last_rows_kernel,
        out_shape=[
            jax.ShapeDtypeStruct((embeds.shape[1], width), BF16),
            jax.ShapeDtypeStruct((rows, width), F32),
        ]
        + [jax.ShapeDtypeStruct((rows, width), BF16)] * (n_side - 1),
        in_specs=[VMEM] * 4,
        out_specs=[VMEM] * (n_side + 1),
        compiler_params=params(16),
        name="last_rows",
    )(total, weight_sum, back[1], embeds_line)
    n_plane = n_side * n_side
    pieces = exchange(partial.reshape(n_plane, -1, width), PLANE)
    spread = sum_spread([pieces], n_z * 2, BF16)
    spread, other_rows = lax.optimization_barrier((spread, other_rows))
    pieces = exchange(spread, STACK)
    arrived = [turn(block, sizes, 0, d + 1) for d, block in enumerate(other_rows)]
    grad_rows = pl.pallas_call(
        finish_rows_kernel,
        out_shape=jax.ShapeDtypeStruct((rows, width), F32),
        in_specs=[VMEM] * 4,
        out_specs=VMEM,
        compiler_params=params(16),
        name="finish_rows",
    )(own_rows, *arrived)
    pieces, grad_rows = lax.optimization_barrier((pieces, grad_rows))
    pieces = exchange(sum_spread([pieces], n_plane, BF16), PLANE)
    total_points = rows * n_plane * n_z * 2
    grad_weight = pieces.reshape(-1, width).astype(F32) * (1.0 / math.sqrt(total_points))
    return grad_rows, grad_weight


def solution(mesh):
    sizes = {"y": 4, "zh": 2, "core": 2, "zl": 4, "x": 4}
    fine = Mesh(mesh.devices.reshape(tuple(sizes[a] for a in ALL)), ALL)
    return jax.shard_map(
        functools.partial(shards, sizes),
        mesh=fine,
        in_specs=(P(ALL, None), P(), P(ALL), P(ALL, None), P(ALL, None)),
        out_specs=(P(ALL, None), P()),
        check_vma=False,
    )
```

```python
import functools
import math

import jax
import jax.numpy as jnp
import numpy as np
from jax import lax
from jax.experimental import pallas as pl
from jax.experimental.pallas import tpu as pltpu
from jax.sharding import Mesh, PartitionSpec as P

LOG2E = math.log2(math.e)
ROOT5 = math.sqrt(5.0)
ALL = ("y", "zh", "core", "zl", "x")
PLANE = ("y", "x")
STACK = ("zh", "core", "zl")
DEPTH = ("zh", "zl")
F32 = jnp.float32
BF16 = jnp.bfloat16
VMEM = pl.BlockSpec(memory_space=pltpu.VMEM)


def params(mib):
    return pltpu.CompilerParams(vmem_limit_bytes=mib << 20)


def dot_nt(a, b):
    return lax.dot_general(a, b, (((1,), (1,)), ((), ())), preferred_element_type=F32)


def dot_tn(a, b):
    return lax.dot_general(a, b, (((0,), (0,)), ((), ())), preferred_element_type=F32)


def pack_kernel(embeds, weight, solve, probes, probe_solves, packed, extended, weight_in, solve_in, probes_in, probe_solves_in, sems):
    rows, width = embeds.shape[0], weight.shape[1]
    embeds_in = extended.at[:, 128:]
    loads = [
        pltpu.make_async_copy(source, target, sems.at[k])
        for k, (source, target) in enumerate(
            (
                (weight, weight_in),
                (embeds, embeds_in),
                (probes, probes_in),
                (probe_solves, probe_solves_in),
                (solve, solve_in),
            )
        )
    ]
    for load in loads:
        load.start()
    for load in loads:
        load.wait()
    feats = jnp.dot(embeds_in[...], weight_in[...], preferred_element_type=F32).astype(BF16)
    wide = feats.astype(F32)
    sq = jnp.sum(wide * wide, axis=1, keepdims=True)
    sq_hi = sq.astype(BF16).astype(F32)
    sq_mid = (sq - sq_hi).astype(BF16).astype(F32)
    sq_lo = sq - sq_hi - sq_mid
    fold = math.sqrt(5.0 / 3.0 * ROOT5)
    scale = (2.0 * probes.shape[0]) ** (-0.5) * fold
    both = jnp.concatenate(
        [solve_in[...] * fold, probes_in[...] * -scale, probe_solves_in[...] * -scale, jnp.zeros((1, rows), F32)],
        axis=0,
    ).T
    hi = both.astype(BF16).astype(F32)
    lo = both - hi
    lane = lax.broadcasted_iota(jnp.int32, (rows, 32), 1)
    tail = jnp.where(lane == 0, sq_hi, jnp.where(lane == 1, sq_mid, jnp.where(lane == 2, sq_lo, 0.0)))
    tail = jnp.concatenate([hi, lo, hi, tail], axis=1).astype(BF16)
    extended[:, :128] = tail
    packed[:, :width] = feats
    packed[:, width:] = tail


def split_kernel(count, weight, *refs):
    line, embeds = refs[count:]
    rows, width = refs[0].shape[0], weight.shape[1]
    for k, ref in enumerate(refs[:count]):
        block = slice(k * rows, (k + 1) * rows)
        own = ref[:, 128:]
        line[block, :] = jnp.dot(own, weight[...], preferred_element_type=F32).astype(BF16)
        embeds[block, :] = own
    for k in range(0, count, 2):
        both = [ref[:, :64].astype(F32) for ref in refs[k : k + 2]]
        line[count * rows :, k * 64 : k * 64 + 128] = jnp.concatenate(both, axis=1).astype(BF16)


def left_map(count):
    source = np.zeros((32,), np.int32)
    sign = np.zeros((32,), np.float32)
    sign[0] = 1.0
    for k in range(count):
        source[1 + k], sign[1 + k] = 1 + count + k, -1.0
        source[1 + count + k], sign[1 + count + k] = 1 + k, -1.0
    table = np.zeros((2, 128, 128), np.float32)
    for half in range(2):
        for group, offset in ((0, 0), (1, 0), (2, 32)):
            for k in range(32):
                table[half, 64 * half + offset + source[k], 32 * group + k] = sign[k]
    return jnp.asarray(table, BF16)


def tile_kernel(sub, step, adds, table, rows_ref, *refs):
    *columns, out = refs
    if adds:
        begin, *columns = columns
    width = out.shape[1]
    block = rows_ref.shape[0] // 5
    rows = 4 * block
    u_rows = rows_ref[:rows, :]
    wide = u_rows.astype(F32)
    twice = (wide * -2.0).astype(BF16)
    left = []
    for k in range(4):
        start = k // 2 * 128
        fac = rows_ref[rows:, start : start + 128]
        left.append(jnp.dot(fac, table[k % 2], preferred_element_type=F32).astype(BF16))
    left = jnp.concatenate(left, axis=0)
    sq_rows = jnp.sum(wide * wide, axis=1, keepdims=True)
    lane = lax.broadcasted_iota(jnp.int32, (8, 128), 1)
    pick_cols = jnp.where((lane >= 96) & (lane < 99), 1.0, 0.0).astype(BF16)
    blocks = [slice(k, k + sub) for k in range(0, rows, sub)]
    acc = [begin[block, :] if adds else jnp.zeros((sub, width), F32) for block in blocks]
    total = [jnp.zeros((sub, 128), F32) for _ in blocks]
    work = [
        (ref, start, k)
        for ref in columns
        for start in range(0, ref.shape[0], step)
        for k in range(len(blocks))
    ]

    def products(ref, start, k):
        u_cols = ref[start : start + step, :width]
        right = ref[start : start + step, width:]
        sq_cols = dot_nt(pick_cols, right)[:1]
        return u_cols, sq_cols, dot_nt(twice[blocks[k]], u_cols), dot_nt(left[blocks[k]], right)

    ahead = products(*work[0])
    for index, (_, _, k) in enumerate(work):
        u_cols, sq_cols, cross, pair = ahead
        if index + 1 < len(work):
            ahead = products(*work[index + 1])
        d2 = jnp.maximum((sq_rows[blocks[k]] + sq_cols) + cross, 1e-30)
        dist = d2 * lax.rsqrt(d2)
        coupling = pair * ((dist + 1.0 / ROOT5) * jnp.exp2(dist * (-ROOT5 * LOG2E)))
        for j in range(0, step, 128):
            total[k] = total[k] + coupling[:, j : j + 128]
        acc[k] = acc[k] + jnp.dot(coupling.astype(BF16), u_cols, preferred_element_type=F32)
    for k, block in enumerate(blocks):
        row_total = jnp.sum(total[k], axis=1, keepdims=True)
        out[block, :] = (acc[k] - row_total * u_rows[block].astype(F32)).astype(out.dtype)


def sum_rows_kernel(a, b, c, embeds, total, weight):
    rows = a[...] + (b[...].astype(F32) + c[...].astype(F32))
    hi = rows.astype(BF16)
    lo = (rows - hi.astype(F32)).astype(BF16)
    total[...] = rows
    weight[...] = dot_tn(embeds[...], hi) + dot_tn(embeds[...], lo)


def last_rows_kernel(total, weight, last, embeds, partial, own, *others):
    rows = own.shape[0]
    partial[...] = (weight[...] + dot_tn(embeds[...], last[...])).astype(BF16)
    own[...] = total[:rows] + last[:rows].astype(F32)
    for k, ref in enumerate(others):
        block = slice((k + 1) * rows, (k + 2) * rows)
        ref[...] = (total[block] + last[block].astype(F32)).astype(BF16)


def finish_rows_kernel(own, b, c, d, grad_rows):
    grad_rows[...] = (own[...] + b[...].astype(F32)) + (c[...].astype(F32) + d[...].astype(F32))


def sum_spread_kernel(*refs):
    *parts, out = refs
    total = None
    for ref in parts:
        for k in range(ref.shape[0]):
            term = ref[k].astype(F32)
            total = term if total is None else total + term
    low = total.astype(out.dtype)
    for k in range(out.shape[0]):
        out[k] = low


def sum_spread(parts, copies, dtype):
    return pl.pallas_call(
        sum_spread_kernel,
        out_shape=jax.ShapeDtypeStruct((copies,) + parts[0].shape[1:], dtype),
        in_specs=[VMEM] * len(parts),
        out_specs=VMEM,
        compiler_params=params(16),
        name="sum_spread",
    )(*parts)


def ring(array, axis, size, shift):
    return lax.ppermute(array, axis, [(i, (i + shift) % size) for i in range(size)])


def move(array, sizes, where):
    dims = [sizes[a] for a in ALL]
    perm = []
    for source in range(math.prod(dims)):
        place = dict(zip(ALL, (int(i) for i in np.unravel_index(source, dims))))
        for axis, shift in where(place["core"]).items():
            if axis == "z":
                z = (place["zh"] * sizes["zl"] + place["zl"] + shift) % (sizes["zh"] * sizes["zl"])
                place["zh"], place["zl"] = divmod(z, sizes["zl"])
            else:
                place[axis] = (place[axis] + shift) % sizes[axis]
        perm.append((source, int(np.ravel_multi_index([place[a] for a in ALL], dims))))
    return lax.ppermute(array, ALL, perm)


def turn(array, sizes, stage, shift):
    return move(array, sizes, lambda core: {"y" if (core + stage) % 2 == 0 else "x": shift})


def exchange(array, axes):
    return lax.all_to_all(array, axes, split_axis=0, concat_axis=0, tiled=True)


def shards(sizes, embeds, weight, solve, probes, probe_solves):
    rows, width = embeds.shape[0], weight.shape[1]
    n_side, n_z = sizes["x"], sizes["zh"] * sizes["zl"]
    pack, extended = pl.pallas_call(
        pack_kernel,
        out_shape=[
            jax.ShapeDtypeStruct((rows, width + 128), BF16),
            jax.ShapeDtypeStruct((rows, 128 + embeds.shape[1]), BF16),
        ],
        in_specs=[pl.BlockSpec(memory_space=pltpu.HBM)] * 5,
        out_specs=[VMEM] * 2,
        scratch_shapes=[
            pltpu.VMEM(weight.shape, BF16),
            pltpu.VMEM((1, rows), F32),
            pltpu.VMEM(probes.shape[::-1], F32),
            pltpu.VMEM(probes.shape[::-1], F32),
            pltpu.SemaphoreType.DMA((5,)),
        ],
        compiler_params=params(48),
        name="pack",
    )(*(pltpu.with_memory_space_constraint(a, pltpu.HBM) for a in (embeds, weight, solve[None, :], probes.T, probe_solves.T)))

    blocks = [extended] + [turn(extended, sizes, 0, -d) for d in range(1, n_side)]
    line, embeds_line = pl.pallas_call(
        functools.partial(split_kernel, n_side),
        out_shape=[
            jax.ShapeDtypeStruct(((n_side + 1) * rows, width), BF16),
            jax.ShapeDtypeStruct((n_side * rows, embeds.shape[1]), BF16),
        ],
        in_specs=[VMEM] * (n_side + 1),
        out_specs=[VMEM] * 2,
        compiler_params=params(8),
        name="split",
    )(weight, *blocks)
    pair = [pack, ring(pack, DEPTH, n_z, n_z // 2)]
    four = jnp.concatenate(pair + [ring(part, "core", 2, 1) for part in pair], axis=0)
    pair = jnp.concatenate(pair, axis=0)
    pair, four, line = lax.optimization_barrier((pair, four, line))
    far = move(pair, sizes, lambda core: {"z": 2 - 4 * core})
    lines = [line] + [turn(line, sizes, 1, -d) for d in range(1, n_side)]
    near = move(four, sizes, lambda core: {"z": 1 - 2 * core})
    table = left_map(probes.shape[1])

    def tile(rows_in, columns, dtype, start=None):
        return pl.pallas_call(
            functools.partial(tile_kernel, 256, 256, start is not None),
            out_shape=jax.ShapeDtypeStruct((n_side * rows, width), dtype),
            in_specs=[VMEM] * (2 + len(columns) + (start is not None)),
            out_specs=VMEM,
            compiler_params=params(16),
            name="tile",
        )(table, rows_in, *([] if start is None else [start]), *columns)

    first = n_side - 1
    begin = {d: tile(lines[d], [four, near], F32) for d in (first, first - 1)}
    halves = [near[: 2 * rows], near[2 * rows :]]
    columns = [four, near] + [ring(part, "core", 2, 1) for part in halves] + [far]
    columns, lines, begin = lax.optimization_barrier((columns, lines, begin))
    early = len(columns)
    columns.append(ring(columns[-1], "core", 2, 1))

    back = {}
    for d in range(n_side):
        if d == first:
            part = tile(lines[d], columns[early:], BF16, tile(lines[d], columns[2:early], F32, begin[d]))
        elif d in begin:
            part = tile(lines[d], columns[2:], BF16, begin[d])
        else:
            part = tile(lines[d], columns, BF16 if d else F32)
        back[d] = turn(part, sizes, 1, d) if d else part

    total, weight_sum = pl.pallas_call(
        sum_rows_kernel,
        out_shape=[
            jax.ShapeDtypeStruct((n_side * rows, width), F32),
            jax.ShapeDtypeStruct((embeds.shape[1], width), F32),
        ],
        in_specs=[VMEM] * 4,
        out_specs=[VMEM] * 2,
        compiler_params=params(16),
        name="sum_rows",
    )(back[0], back[2], back[3], embeds_line)
    partial, own_rows, *other_rows = pl.pallas_call(
        last_rows_kernel,
        out_shape=[
            jax.ShapeDtypeStruct((embeds.shape[1], width), BF16),
            jax.ShapeDtypeStruct((rows, width), F32),
        ]
        + [jax.ShapeDtypeStruct((rows, width), BF16)] * (n_side - 1),
        in_specs=[VMEM] * 4,
        out_specs=[VMEM] * (n_side + 1),
        compiler_params=params(16),
        name="last_rows",
    )(total, weight_sum, back[1], embeds_line)
    n_plane = n_side * n_side
    pieces = exchange(partial.reshape(n_plane, -1, width), PLANE)
    spread = sum_spread([pieces], n_z * 2, BF16)
    spread, other_rows = lax.optimization_barrier((spread, other_rows))
    pieces = exchange(spread, STACK)
    arrived = [turn(block, sizes, 0, d + 1) for d, block in enumerate(other_rows)]
    grad_rows = pl.pallas_call(
        finish_rows_kernel,
        out_shape=jax.ShapeDtypeStruct((rows, width), F32),
        in_specs=[VMEM] * 4,
        out_specs=VMEM,
        compiler_params=params(16),
        name="finish_rows",
    )(own_rows, *arrived)
    pieces, grad_rows = lax.optimization_barrier((pieces, grad_rows))
    pieces = exchange(sum_spread([pieces], n_plane, BF16), PLANE)
    total_points = rows * n_plane * n_z * 2
    grad_weight = pieces.reshape(-1, width).astype(F32) * (1.0 / math.sqrt(total_points))
    return grad_rows, grad_weight


def solution(mesh):
    sizes = {"y": 4, "zh": 2, "core": 2, "zl": 4, "x": 4}
    fine = Mesh(mesh.devices.reshape(tuple(sizes[a] for a in ALL)), ALL)
    return jax.shard_map(
        functools.partial(shards, sizes),
        mesh=fine,
        in_specs=(P(ALL, None), P(), P(ALL), P(ALL, None), P(ALL, None)),
        out_specs=(P(ALL, None), P()),
        check_vma=False,
    )
```

```python
import functools
import math

import jax
import jax.numpy as jnp
import numpy as np
from jax import lax
from jax.experimental import pallas as pl
from jax.experimental.pallas import tpu as pltpu
from jax.sharding import Mesh, PartitionSpec as P

LOG2E = math.log2(math.e)
ROOT5 = math.sqrt(5.0)
ALL = ("y", "zh", "core", "zl", "x")
PLANE = ("y", "x")
STACK = ("zh", "core", "zl")
DEPTH = ("zh", "zl")
F32 = jnp.float32
BF16 = jnp.bfloat16
VMEM = pl.BlockSpec(memory_space=pltpu.VMEM)


def params(mib):
    return pltpu.CompilerParams(vmem_limit_bytes=mib << 20)


def dot_nt(a, b):
    return lax.dot_general(a, b, (((1,), (1,)), ((), ())), preferred_element_type=F32)


def dot_tn(a, b):
    return lax.dot_general(a, b, (((0,), (0,)), ((), ())), preferred_element_type=F32)


def pack_kernel(embeds, weight, solve, probes, probe_solves, packed, extended, weight_in, solve_in, probes_in, probe_solves_in, sems):
    rows, width = embeds.shape[0], weight.shape[1]
    embeds_in = extended.at[:rows, :]
    loads = [
        pltpu.make_async_copy(source, target, sems.at[k])
        for k, (source, target) in enumerate(
            (
                (weight, weight_in),
                (embeds, embeds_in),
                (probes, probes_in),
                (probe_solves, probe_solves_in),
                (solve, solve_in),
            )
        )
    ]
    for load in loads:
        load.start()
    for load in loads[2:]:
        load.wait()
    fold = math.sqrt(5.0 / 3.0 * ROOT5)
    scale = (2.0 * probes.shape[0]) ** (-0.5) * fold
    both = jnp.concatenate(
        [solve_in[...] * fold, probes_in[...] * -scale, probe_solves_in[...] * -scale, jnp.zeros((1, rows), F32)],
        axis=0,
    ).T
    hi = both.astype(BF16).astype(F32)
    lo = both - hi
    pair = jnp.concatenate([hi, lo], axis=1)
    part = rows // 8
    extended[rows:, :] = jnp.concatenate(
        [pair[k * part : (k + 1) * part] for k in range(8)], axis=1
    ).astype(BF16)
    for load in loads[:2]:
        load.wait()
    feats = jnp.dot(embeds_in[...], weight_in[...], preferred_element_type=F32).astype(BF16)
    wide = feats.astype(F32)
    sq = jnp.sum(wide * wide, axis=1, keepdims=True)
    sq_hi = sq.astype(BF16).astype(F32)
    sq_mid = (sq - sq_hi).astype(BF16).astype(F32)
    sq_lo = sq - sq_hi - sq_mid
    lane = lax.broadcasted_iota(jnp.int32, (rows, 32), 1)
    tail = jnp.where(lane == 0, sq_hi, jnp.where(lane == 1, sq_mid, jnp.where(lane == 2, sq_lo, 0.0)))
    packed[:, :width] = feats
    packed[:, width:] = jnp.concatenate([pair, hi, tail], axis=1).astype(BF16)


def split_kernel(count, weight, *refs):
    line, embeds = refs[count:]
    rows = embeds.shape[0] // count
    for k, ref in enumerate(refs[:count]):
        block = slice(k * rows, (k + 1) * rows)
        own = ref[:rows, :]
        line[block, :] = jnp.dot(own, weight[...], preferred_element_type=F32).astype(BF16)
        embeds[block, :] = own
    for k in range(0, count, 2):
        both = []
        for ref in refs[k : k + 2]:
            folded = ref[rows:, :].astype(F32)
            both.append(jnp.concatenate([folded[:, 64 * p : 64 * p + 64] for p in range(8)], axis=0))
        line[count * rows :, k * 64 : k * 64 + 128] = jnp.concatenate(both, axis=1).astype(BF16)


def left_map(count):
    source = np.zeros((32,), np.int32)
    sign = np.zeros((32,), np.float32)
    sign[0] = 1.0
    for k in range(count):
        source[1 + k], sign[1 + k] = 1 + count + k, -1.0
        source[1 + count + k], sign[1 + count + k] = 1 + k, -1.0
    table = np.zeros((2, 128, 128), np.float32)
    for half in range(2):
        for group, offset in ((0, 0), (1, 0), (2, 32)):
            for k in range(32):
                table[half, 64 * half + offset + source[k], 32 * group + k] = sign[k]
    return jnp.asarray(table, BF16)


def tile_kernel(sub, step, adds, table, rows_ref, *refs):
    *columns, out = refs
    if adds:
        begin, *columns = columns
    width = out.shape[1]
    block = rows_ref.shape[0] // 5
    rows = 4 * block
    u_rows = rows_ref[:rows, :]
    wide = u_rows.astype(F32)
    twice = (wide * -2.0).astype(BF16)
    left = []
    for k in range(4):
        start = k // 2 * 128
        fac = rows_ref[rows:, start : start + 128]
        left.append(jnp.dot(fac, table[k % 2], preferred_element_type=F32).astype(BF16))
    left = jnp.concatenate(left, axis=0)
    sq_rows = jnp.sum(wide * wide, axis=1, keepdims=True)
    lane = lax.broadcasted_iota(jnp.int32, (8, 128), 1)
    pick_cols = jnp.where((lane >= 96) & (lane < 99), 1.0, 0.0).astype(BF16)
    blocks = [slice(k, k + sub) for k in range(0, rows, sub)]
    acc = [begin[block, :] if adds else jnp.zeros((sub, width), F32) for block in blocks]
    total = [jnp.zeros((sub, 128), F32) for _ in blocks]
    work = [
        (ref, start, k)
        for ref in columns
        for start in range(0, ref.shape[0], step)
        for k in range(len(blocks))
    ]

    def products(ref, start, k):
        u_cols = ref[start : start + step, :width]
        right = ref[start : start + step, width:]
        sq_cols = dot_nt(pick_cols, right)[:1]
        return u_cols, sq_cols, dot_nt(twice[blocks[k]], u_cols), dot_nt(left[blocks[k]], right)

    ahead = products(*work[0])
    for index, (_, _, k) in enumerate(work):
        u_cols, sq_cols, cross, pair = ahead
        if index + 1 < len(work):
            ahead = products(*work[index + 1])
        d2 = jnp.maximum((sq_rows[blocks[k]] + sq_cols) + cross, 1e-30)
        dist = d2 * lax.rsqrt(d2)
        coupling = pair * ((dist + 1.0 / ROOT5) * jnp.exp2(dist * (-ROOT5 * LOG2E)))
        for j in range(0, step, 128):
            total[k] = total[k] + coupling[:, j : j + 128]
        acc[k] = acc[k] + jnp.dot(coupling.astype(BF16), u_cols, preferred_element_type=F32)
    for k, block in enumerate(blocks):
        row_total = jnp.sum(total[k], axis=1, keepdims=True)
        out[block, :] = (acc[k] - row_total * u_rows[block].astype(F32)).astype(out.dtype)


def sum_rows_kernel(a, b, c, embeds, total, weight):
    rows = a[...] + (b[...].astype(F32) + c[...].astype(F32))
    hi = rows.astype(BF16)
    lo = (rows - hi.astype(F32)).astype(BF16)
    total[...] = rows
    weight[...] = dot_tn(embeds[...], hi) + dot_tn(embeds[...], lo)


def last_rows_kernel(total, weight, last, embeds, partial, own, *others):
    rows = own.shape[0]
    partial[...] = (weight[...] + dot_tn(embeds[...], last[...])).astype(BF16)
    own[...] = total[:rows] + last[:rows].astype(F32)
    for k, ref in enumerate(others):
        block = slice((k + 1) * rows, (k + 2) * rows)
        ref[...] = (total[block] + last[block].astype(F32)).astype(BF16)


def finish_rows_kernel(own, b, c, d, grad_rows):
    grad_rows[...] = (own[...] + b[...].astype(F32)) + (c[...].astype(F32) + d[...].astype(F32))


def sum_spread_kernel(*refs):
    *parts, out = refs
    total = None
    for ref in parts:
        for k in range(ref.shape[0]):
            term = ref[k].astype(F32)
            total = term if total is None else total + term
    low = total.astype(out.dtype)
    for k in range(out.shape[0]):
        out[k] = low


def sum_spread(parts, copies, dtype):
    return pl.pallas_call(
        sum_spread_kernel,
        out_shape=jax.ShapeDtypeStruct((copies,) + parts[0].shape[1:], dtype),
        in_specs=[VMEM] * len(parts),
        out_specs=VMEM,
        compiler_params=params(16),
        name="sum_spread",
    )(*parts)


def ring(array, axis, size, shift):
    return lax.ppermute(array, axis, [(i, (i + shift) % size) for i in range(size)])


def move(array, sizes, where):
    dims = [sizes[a] for a in ALL]
    perm = []
    for source in range(math.prod(dims)):
        place = dict(zip(ALL, (int(i) for i in np.unravel_index(source, dims))))
        for axis, shift in where(place["core"]).items():
            if axis == "z":
                z = (place["zh"] * sizes["zl"] + place["zl"] + shift) % (sizes["zh"] * sizes["zl"])
                place["zh"], place["zl"] = divmod(z, sizes["zl"])
            else:
                place[axis] = (place[axis] + shift) % sizes[axis]
        perm.append((source, int(np.ravel_multi_index([place[a] for a in ALL], dims))))
    return lax.ppermute(array, ALL, perm)


def turn(array, sizes, stage, shift):
    return move(array, sizes, lambda core: {"y" if (core + stage) % 2 == 0 else "x": shift})


def exchange(array, axes):
    return lax.all_to_all(array, axes, split_axis=0, concat_axis=0, tiled=True)


def shards(sizes, embeds, weight, solve, probes, probe_solves):
    rows, width = embeds.shape[0], weight.shape[1]
    n_side, n_z = sizes["x"], sizes["zh"] * sizes["zl"]
    pack, extended = pl.pallas_call(
        pack_kernel,
        out_shape=[
            jax.ShapeDtypeStruct((rows, width + 128), BF16),
            jax.ShapeDtypeStruct((rows + rows // 8, embeds.shape[1]), BF16),
        ],
        in_specs=[pl.BlockSpec(memory_space=pltpu.HBM)] * 5,
        out_specs=[VMEM] * 2,
        scratch_shapes=[
            pltpu.VMEM(weight.shape, BF16),
            pltpu.VMEM((1, rows), F32),
            pltpu.VMEM(probes.shape[::-1], F32),
            pltpu.VMEM(probes.shape[::-1], F32),
            pltpu.SemaphoreType.DMA((5,)),
        ],
        compiler_params=params(48),
        name="pack",
    )(*(pltpu.with_memory_space_constraint(a, pltpu.HBM) for a in (embeds, weight, solve[None, :], probes.T, probe_solves.T)))

    blocks = [extended] + [turn(extended, sizes, 0, -d) for d in range(1, n_side)]
    line, embeds_line = pl.pallas_call(
        functools.partial(split_kernel, n_side),
        out_shape=[
            jax.ShapeDtypeStruct(((n_side + 1) * rows, width), BF16),
            jax.ShapeDtypeStruct((n_side * rows, embeds.shape[1]), BF16),
        ],
        in_specs=[VMEM] * (n_side + 1),
        out_specs=[VMEM] * 2,
        compiler_params=params(8),
        name="split",
    )(weight, *blocks)
    pair = [pack, ring(pack, DEPTH, n_z, n_z // 2)]
    four = jnp.concatenate(pair + [ring(part, "core", 2, 1) for part in pair], axis=0)
    pair = jnp.concatenate(pair, axis=0)
    pair, four, line = lax.optimization_barrier((pair, four, line))
    far = move(pair, sizes, lambda core: {"z": 2 - 4 * core})
    lines = [line] + [turn(line, sizes, 1, -d) for d in range(1, n_side)]
    near = move(four, sizes, lambda core: {"z": 1 - 2 * core})
    table = left_map(probes.shape[1])

    def tile(rows_in, columns, dtype, start=None):
        return pl.pallas_call(
            functools.partial(tile_kernel, 256, 256, start is not None),
            out_shape=jax.ShapeDtypeStruct((n_side * rows, width), dtype),
            in_specs=[VMEM] * (2 + len(columns) + (start is not None)),
            out_specs=VMEM,
            compiler_params=params(16),
            name="tile",
        )(table, rows_in, *([] if start is None else [start]), *columns)

    first = n_side - 1
    begin = {d: tile(lines[d], [four, near], F32) for d in (first, first - 1)}
    halves = [near[: 2 * rows], near[2 * rows :]]
    columns = [four, near] + [ring(part, "core", 2, 1) for part in halves] + [far]
    columns, lines, begin = lax.optimization_barrier((columns, lines, begin))
    early = len(columns)
    columns.append(ring(columns[-1], "core", 2, 1))

    back = {}
    for d in range(n_side):
        if d == first:
            part = tile(lines[d], columns[early:], BF16, tile(lines[d], columns[2:early], F32, begin[d]))
        elif d in begin:
            part = tile(lines[d], columns[2:], BF16, begin[d])
        else:
            part = tile(lines[d], columns, BF16 if d else F32)
        back[d] = turn(part, sizes, 1, d) if d else part

    total, weight_sum = pl.pallas_call(
        sum_rows_kernel,
        out_shape=[
            jax.ShapeDtypeStruct((n_side * rows, width), F32),
            jax.ShapeDtypeStruct((embeds.shape[1], width), F32),
        ],
        in_specs=[VMEM] * 4,
        out_specs=[VMEM] * 2,
        compiler_params=params(16),
        name="sum_rows",
    )(back[0], back[2], back[3], embeds_line)
    partial, own_rows, *other_rows = pl.pallas_call(
        last_rows_kernel,
        out_shape=[
            jax.ShapeDtypeStruct((embeds.shape[1], width), BF16),
            jax.ShapeDtypeStruct((rows, width), F32),
        ]
        + [jax.ShapeDtypeStruct((rows, width), BF16)] * (n_side - 1),
        in_specs=[VMEM] * 4,
        out_specs=[VMEM] * (n_side + 1),
        compiler_params=params(16),
        name="last_rows",
    )(total, weight_sum, back[1], embeds_line)
    n_plane = n_side * n_side
    pieces = exchange(partial.reshape(n_plane, -1, width), PLANE)
    spread = sum_spread([pieces], n_z * 2, BF16)
    spread, other_rows = lax.optimization_barrier((spread, other_rows))
    pieces = exchange(spread, STACK)
    arrived = [turn(block, sizes, 0, d + 1) for d, block in enumerate(other_rows)]
    grad_rows = pl.pallas_call(
        finish_rows_kernel,
        out_shape=jax.ShapeDtypeStruct((rows, width), F32),
        in_specs=[VMEM] * 4,
        out_specs=VMEM,
        compiler_params=params(16),
        name="finish_rows",
    )(own_rows, *arrived)
    pieces, grad_rows = lax.optimization_barrier((pieces, grad_rows))
    pieces = exchange(sum_spread([pieces], n_plane, BF16), PLANE)
    total_points = rows * n_plane * n_z * 2
    grad_weight = pieces.reshape(-1, width).astype(F32) * (1.0 / math.sqrt(total_points))
    return grad_rows, grad_weight


def solution(mesh):
    sizes = {"y": 4, "zh": 2, "core": 2, "zl": 4, "x": 4}
    fine = Mesh(mesh.devices.reshape(tuple(sizes[a] for a in ALL)), ALL)
    return jax.shard_map(
        functools.partial(shards, sizes),
        mesh=fine,
        in_specs=(P(ALL, None), P(), P(ALL), P(ALL, None), P(ALL, None)),
        out_specs=(P(ALL, None), P()),
        check_vma=False,
    )
```
